256 devices in a mesh: paper: 64 (over z, y, core), author: 4 (over x).
Axes of the slice: x: 4, y: 4, z: 8, core: 2. Of those that a mesh axis runs over, the one named last changes fastest.
Arguments:
- paper_feat: bfloat16 [16384, 1024], P('paper', 'author'), may hold values from -6 to 6
- author_feat: bfloat16 [16384, 1024], P('paper', 'author'), may hold values from -6 to 6
- cite_owner: int32 [3072, 1], P('paper'), may hold values from 0 to 63; in each aligned block of 48 rows (0 to 47, 48 to 95, ...) no two rows name the same one
- cite_source: int32 [3072], P('paper'), may hold values from 0 to 1
- cite_target: int32 [3072], P('paper'), may hold values from 0 to 1
- cite_edges: int32 [3072], P('paper'), may hold values from 8 to 64
- cite_count: int32 [64], P('paper'), may hold values from 36 to 48, as said below
- citation_weight_tiles: bfloat16 [3072, 128, 128], P('paper'), may hold values from 0 to 1
- write_owner: int32 [2048, 1], P('paper'), may hold values from 0 to 63; in each aligned block of 32 rows (0 to 31, 32 to 63, ...) no two rows name the same one
- write_paper: int32 [2048], P('paper'), may hold values from 0 to 1
- write_author: int32 [2048], P('paper'), may hold values from 0 to 1
- write_edges: int32 [2048], P('paper'), may hold values from 8 to 64
- authorship_weight_tiles: bfloat16 [2048, 128, 128], P('paper'), may hold values from 0 to 1
- w_self: bfloat16 [1024, 1024], replicated, may hold values from -0.1875 to 0.1875
- w_cite: bfloat16 [1024, 1024], replicated, may hold values from -0.1875 to 0.1875
- w_write: bfloat16 [1024, 1024], replicated, may hold values from -0.1875 to 0.1875
- cotangent: bfloat16 [16384, 1024], P('paper', 'author'), may hold values from -6 to 6
Outputs:
- paper_out: bfloat16 [16384, 1024], P('paper', 'author')
- paper_grad: bfloat16 [16384, 1024], P('paper', 'author')
- author_grad: bfloat16 [16384, 1024], P('paper', 'author')
The draws below stay inside these ranges and needn't reach their ends.
Inputs may be any that keep to these rules, and one draw needn't show every extreme that they name: `cite_owner`: among the 48 tiles of one paper index (live or not), at most 1 have their source on any one paper index. The live tiles of a paper index are the first cite_count of its list; some paper index has all 48 live. `write_owner`: among the 32 tiles of one paper index, at most 1 take their author block from any one paper index.
All inputs are finite; a program needn't handle non-finite values.
Results may differ from the reference program's by a relative error of at most 0.007.
Values may be sent and summed in bfloat16 or wider, within the bound.
A program may use at most 128 MiB of HBM per device.

```python
import math
import jax
import jax.numpy as jnp
import numpy as np
from jax import lax

D = 1024
BLOCK = 128
P_BLOCKS = 2
A_BLOCKS = 2
CITE_TILES = 48
WRITE_TILES = 32
SLOTS = 1
WSLOTS = 1
PAPERS = 16384
AUTHORS = 16384
N_PAPER = 64


def draw_cite_count(key, part):
    key = jax.random.fold_in(key, 11)
    first_key, second_key = jax.random.split(key)
    missing = jax.random.randint(first_key, (N_PAPER,), 0, CITE_TILES // 4 + 1)
    counts = CITE_TILES - missing
    chosen = jax.random.randint(second_key, (), 0, N_PAPER)
    return jnp.where(jnp.arange(N_PAPER) == chosen, CITE_TILES, counts).astype(jnp.int32)


def place_ends(result, key, smallest, largest):
    index_at = [jax.random.randint(jax.random.fold_in(key, axis), (), 0, length) for axis, length in enumerate(result.shape)]
    main_axis = result.shape.index(max(result.shape))
    next_to = index_at[:main_axis] + [(index_at[main_axis] + 1) % result.shape[main_axis]] + index_at[main_axis + 1:]
    return result.at[tuple(index_at)].set(smallest).at[tuple(next_to)].set(largest)


def steps_of(rng, extent, pieces, smallest, largest):
    loudness = 1.0
    for dim, parts in pieces:
        steps = jax.random.uniform(jax.random.fold_in(jax.random.fold_in(rng, 6), dim), (parts,), jnp.float32, smallest / len(pieces), largest / len(pieces))
        loudness = loudness * jnp.repeat(jnp.exp(steps), extent[dim] // parts).reshape((-1,) + (1,) * (len(extent) - 1 - dim))
    return loudness


def routed_block(own_key, own, number, rows, count, top, limit, slope):
    ranking = jax.random.permutation(own_key, count)
    packed, usual = shares(count, rows * top, limit, slope, True), shares(count, rows * top, limit, slope, False)
    places = jnp.arange(count)

    def named(tallies, turn):
        used = int((tallies > 0).sum())
        fixed = max(1, used // 4)
        passed = fixed + (places - fixed + turn * (used - fixed)) % max(1, count - fixed)
        return jnp.zeros((count,), jnp.int32).at[ranking[jnp.where(places < fixed, places, passed)]].set(jnp.asarray(tallies, jnp.int32))

    tallies = jnp.where(number % 4 == 0, named(packed, number // 4), named(usual, number - number // 4 - 1))
    mixed = jax.random.permutation(jax.random.fold_in(own, 3), count)
    source_of, sink = mixed[0:count // 2 * 2:2], mixed[1:count // 2 * 2:2]
    slack = jnp.minimum(tallies[source_of] - 1, limit - tallies[sink]) // 2
    slack = jnp.where((source_of == ranking[0]) | (sink == ranking[0]) | (tallies[sink] == 0), 0, jnp.maximum(slack, 0))
    passed = jax.random.randint(jax.random.fold_in(own, 4), (count // 2,), 0, 1 << 20) % (slack + 1)
    tallies = tallies.at[source_of].add(-passed).at[sink].add(passed)
    labels = jnp.searchsorted(jnp.cumsum(tallies), jnp.arange(rows * top), side="right").astype(jnp.int32)
    listing = labels.reshape(top, rows).T
    listing = listing[jax.random.permutation(jax.random.fold_in(own, 1), rows)]
    turn = jax.random.randint(jax.random.fold_in(own, 2), (rows, 1), 0, top)
    return jnp.take_along_axis(listing, (jnp.arange(top)[None, :] + turn) % top, axis=1)


def shares(amount, total, most, lean, full):
    loads = [(1 << 20) // math.isqrt(grade ** lean) + 1 for grade in range(1, amount + 1)]
    largest = most if full else min(most, max(-(-total // amount), total * loads[0] // sum(loads)))
    least = 1 if total - largest >= amount - 1 else 0
    given, rest = [largest] + [least] * (amount - 1), total - largest - least * (amount - 1)
    while rest > 0:
        candidates = [i for i in range(1, amount) if given[i] < largest] or [i for i in range(1, amount) if given[i] < most]
        mass, budget = sum([loads[i] for i in candidates]), rest
        for i in candidates:
            addition = min(most - given[i], max(1, budget * loads[i] // mass), rest)
            given[i] = given[i] + addition
            rest = rest - addition
    return np.array(given)


def centred(key, shape, scale, most, cuts=(), held_as=jnp.bfloat16):
    drawn = scale * jax.random.normal(key, shape, jnp.float32)
    if cuts:
        drawn = drawn * steps_of(key, shape, cuts, -0.22, 0.18)
    return jnp.clip(drawn, -most, most).astype(held_as)


def setup_inputs(seed: int = 0) -> dict:
    key_of = jax.random.split(jax.random.key(seed), 18)
    paper_feat = centred(key_of[0], (PAPERS, D), 1.0, 6.0, ((0, 64), (1, 4)))
    author_feat = centred(key_of[1], (AUTHORS, D), 1.0, 6.0, ((0, 64), (1, 4)))
    cite_owner_keys = jax.random.split(jax.random.fold_in(key_of[2], 1), (N_PAPER * CITE_TILES) // CITE_TILES)
    cite_owner_turns = jax.random.permutation(jax.random.fold_in(key_of[2], 3), (N_PAPER * CITE_TILES) // CITE_TILES)
    cite_owner = jax.vmap(lambda own, number: routed_block(jax.random.fold_in(key_of[2], 2), own, number, CITE_TILES, N_PAPER, 1, SLOTS, 2))(cite_owner_keys, cite_owner_turns).reshape((N_PAPER * CITE_TILES, 1))
    cite_source = place_ends(jax.random.randint(key_of[3], (N_PAPER * CITE_TILES,), 0, P_BLOCKS), jax.random.fold_in(key_of[3], 1), 0, P_BLOCKS - 1).astype(jnp.int32)
    cite_target = place_ends(jax.random.randint(key_of[4], (N_PAPER * CITE_TILES,), 0, P_BLOCKS), jax.random.fold_in(key_of[4], 1), 0, P_BLOCKS - 1).astype(jnp.int32)
    cite_edges = place_ends(jax.random.randint(key_of[5], (N_PAPER * CITE_TILES,), 8, 65), jax.random.fold_in(key_of[5], 1), 8, 64).astype(jnp.int32)
    cite_count = draw_cite_count(jax.random.fold_in(key_of[17], 71), 0)
    citation_weight_tiles = jnp.clip(1.0 * jax.random.uniform(key_of[7], (N_PAPER * CITE_TILES, BLOCK, BLOCK), jnp.float32) ** steps_of(key_of[7], (N_PAPER * CITE_TILES, BLOCK, BLOCK), ((0, 64),), -0.2, 0.2), 0.0, 1.0).astype(jnp.bfloat16)
    write_owner_keys = jax.random.split(jax.random.fold_in(key_of[8], 1), (N_PAPER * WRITE_TILES) // WRITE_TILES)
    write_owner_turns = jax.random.permutation(jax.random.fold_in(key_of[8], 3), (N_PAPER * WRITE_TILES) // WRITE_TILES)
    write_owner = jax.vmap(lambda own, number: routed_block(jax.random.fold_in(key_of[8], 2), own, number, WRITE_TILES, N_PAPER, 1, WSLOTS, 2))(write_owner_keys, write_owner_turns).reshape((N_PAPER * WRITE_TILES, 1))
    write_paper = place_ends(jax.random.randint(key_of[9], (N_PAPER * WRITE_TILES,), 0, P_BLOCKS), jax.random.fold_in(key_of[9], 1), 0, P_BLOCKS - 1).astype(jnp.int32)
    write_author = place_ends(jax.random.randint(key_of[10], (N_PAPER * WRITE_TILES,), 0, A_BLOCKS), jax.random.fold_in(key_of[10], 1), 0, A_BLOCKS - 1).astype(jnp.int32)
    write_edges = place_ends(jax.random.randint(key_of[11], (N_PAPER * WRITE_TILES,), 8, 65), jax.random.fold_in(key_of[11], 1), 8, 64).astype(jnp.int32)
    authorship_weight_tiles = jnp.clip(1.0 * jax.random.uniform(key_of[12], (N_PAPER * WRITE_TILES, BLOCK, BLOCK), jnp.float32) ** steps_of(key_of[12], (N_PAPER * WRITE_TILES, BLOCK, BLOCK), ((0, 64),), -0.2, 0.2), 0.0, 1.0).astype(jnp.bfloat16)
    w_self = centred(key_of[13], (D, D), D ** -0.5, 0.1875)
    w_cite = centred(key_of[14], (D, D), D ** -0.5, 0.1875)
    w_write = centred(key_of[15], (D, D), D ** -0.5, 0.1875)
    cotangent = centred(key_of[16], (PAPERS, D), 1.0, 6.0, ((0, 64), (1, 4)))
    return {"paper_feat": paper_feat, "author_feat": author_feat, "cite_owner": cite_owner, "cite_source": cite_source, "cite_target": cite_target, "cite_edges": cite_edges, "cite_count": cite_count, "citation_weight_tiles": citation_weight_tiles, "write_owner": write_owner, "write_paper": write_paper, "write_author": write_author, "write_edges": write_edges, "authorship_weight_tiles": authorship_weight_tiles, "w_self": w_self, "w_cite": w_cite, "w_write": w_write, "cotangent": cotangent}


TOP_PRECISION = lax.Precision.HIGHEST


def silu_slope(values):
    sigma = jax.nn.sigmoid(values)
    return sigma * (1.0 + values * (1.0 - sigma))


def matmul(left, right):
    return jnp.dot(left, right, preferred_element_type=jnp.float32)


def reference(paper_feat, author_feat, cite_owner, cite_source, cite_target, cite_edges, cite_count, citation_weight_tiles, write_owner, write_paper, write_author, write_edges, authorship_weight_tiles, w_self, w_cite, w_write, cotangent):
    paper_stack = paper_feat.reshape(N_PAPER * P_BLOCKS, BLOCK, D)
    author_stack = author_feat.reshape(N_PAPER * A_BLOCKS, BLOCK, D)
    tile_order = jnp.arange(CITE_TILES, dtype=jnp.int32)
    block_ids = jnp.arange(P_BLOCKS, dtype=jnp.int32)
    live_tile = tile_order[None, :] < cite_count[:, None]
    cite_scale = jnp.where(live_tile, 1.0 / cite_edges.reshape(N_PAPER, CITE_TILES).astype(jnp.float32), jnp.float32(0.0))
    glob_source = (cite_owner[:, 0] * P_BLOCKS + cite_source).astype(jnp.int32).reshape(N_PAPER, CITE_TILES)
    target_group = cite_target.reshape(N_PAPER, CITE_TILES)
    tiles_group = citation_weight_tiles.reshape(N_PAPER, CITE_TILES, BLOCK, BLOCK)

    def cite_group(inputs):
        sources, target_indices, scales, weight_tiles = inputs
        collected_rows = jnp.take(paper_stack, sources, axis=0).astype(jnp.float32)
        block_products = jnp.einsum("eih,ehp->eip", weight_tiles.astype(jnp.float32), collected_rows, precision=TOP_PRECISION)
        edge_weights = jnp.where(target_indices[:, None] == block_ids[None, :], scales[:, None], jnp.float32(0.0))
        return jnp.einsum("nr,nmh->rmh", edge_weights, block_products, precision=TOP_PRECISION)

    cite_sum = lax.map(cite_group, (glob_source, target_group, cite_scale, tiles_group))
    cite_sum = cite_sum.reshape(PAPERS, D).astype(jnp.bfloat16)

    write_glob = (write_owner[:, 0] * A_BLOCKS + write_author).astype(jnp.int32).reshape(N_PAPER, WRITE_TILES)
    write_scale = (1.0 / write_edges.astype(jnp.float32)).reshape(N_PAPER, WRITE_TILES)
    write_target = write_paper.reshape(N_PAPER, WRITE_TILES)
    write_group_tiles = authorship_weight_tiles.reshape(N_PAPER, WRITE_TILES, BLOCK, BLOCK)

    def write_group(inputs):
        sources, target_indices, scales, weight_tiles = inputs
        collected_rows = jnp.take(author_stack, sources, axis=0).astype(jnp.float32)
        block_products = jnp.einsum("eih,ehp->eip", weight_tiles.astype(jnp.float32), collected_rows, precision=TOP_PRECISION)
        edge_weights = jnp.where(target_indices[:, None] == block_ids[None, :], scales[:, None], jnp.float32(0.0))
        return jnp.einsum("nr,nmh->rmh", edge_weights, block_products, precision=TOP_PRECISION)

    authorship_sum = lax.map(write_group, (write_glob, write_target, write_scale, write_group_tiles))
    authorship_sum = authorship_sum.reshape(PAPERS, D).astype(jnp.bfloat16)

    preact = matmul(paper_feat, w_self) + matmul(cite_sum, w_cite) + matmul(authorship_sum, w_write)
    paper_out = (paper_feat.astype(jnp.float32) + jax.nn.silu(preact)).astype(jnp.bfloat16)
    grad_pre = (cotangent.astype(jnp.float32) * silu_slope(preact)).astype(jnp.bfloat16)
    self_back = matmul(grad_pre, w_self.T)
    cite_grad = matmul(grad_pre, w_cite.T).astype(jnp.bfloat16)
    write_grad = matmul(grad_pre, w_write.T).astype(jnp.bfloat16)

    cite_grad_stack = cite_grad.reshape(N_PAPER, P_BLOCKS, BLOCK, D)

    def cite_back_step(total, inputs):
        sources, grads, target_indices, scales, weight_tiles = inputs
        selected_rows = jnp.take(grads, target_indices, axis=0).astype(jnp.float32)
        backward_pass = jnp.einsum("pdg,pdw->pgw", weight_tiles.astype(jnp.float32), selected_rows, precision=TOP_PRECISION)
        backward_pass = (backward_pass * scales[:, None, None]).astype(jnp.bfloat16)
        return total.at[sources].add(backward_pass.astype(jnp.float32)), None

    returned, _ = lax.scan(cite_back_step, jnp.zeros((N_PAPER * P_BLOCKS, BLOCK, D), jnp.float32), (glob_source, cite_grad_stack, target_group, cite_scale, tiles_group))
    paper_grad = (cotangent.astype(jnp.float32) + self_back + returned.reshape(PAPERS, D)).astype(jnp.bfloat16)

    write_grad_stack = write_grad.reshape(N_PAPER, P_BLOCKS, BLOCK, D)

    def author_back_step(total, inputs):
        sources, grads, target_indices, scales, weight_tiles = inputs
        selected_rows = jnp.take(grads, target_indices, axis=0).astype(jnp.float32)
        backward_pass = jnp.einsum("pdg,pdw->pgw", weight_tiles.astype(jnp.float32), selected_rows, precision=TOP_PRECISION)
        backward_pass = (backward_pass * scales[:, None, None]).astype(jnp.bfloat16)
        return total.at[sources].add(backward_pass.astype(jnp.float32)), None

    author_total, _ = lax.scan(author_back_step, jnp.zeros((N_PAPER * A_BLOCKS, BLOCK, D), jnp.float32), (write_glob, write_grad_stack, write_target, write_scale, write_group_tiles))
    author_grad = author_total.reshape(AUTHORS, D).astype(jnp.bfloat16)
    return paper_out, paper_grad, author_grad
```

```python
import functools

import jax
import jax.numpy as jnp
from jax import lax
from jax.experimental import pallas as pl
from jax.experimental.pallas import tpu as pltpu
from jax.sharding import PartitionSpec as P

MESH = pl.DeviceIdType.MESH
F32 = jnp.float32
BF16 = jnp.bfloat16
CORES = 2


def dot(left, right):
    return jnp.dot(left, right, preferred_element_type=F32)


def dot_left_flipped(left, right):
    return lax.dot_general(left, right, (((0,), (0,)), ((), ())), preferred_element_type=F32)


def dot_right_flipped(left, right):
    return lax.dot_general(left, right, (((1,), (1,)), ((), ())), preferred_element_type=F32)


def kernel(
    nx,
    nyc,
    nz,
    slot_tile,
    paper,
    author,
    cot,
    meta_f,
    meta_i,
    cite_tiles,
    write_tiles,
    w_self,
    w_cite,
    w_write,
    paper_out,
    paper_grad,
    author_grad,
    win,
    rows,
    feats,
    proj,
    slots,
    tiles,
    meta_fv,
    meta_iv,
    meta_fs,
    meta_is,
    acc,
    part_send,
    part_recv,
    pre,
    grads,
    grads_x,
    back_send,
    back_recv,
    sums,
    local_sem,
    feats_sem,
    meta_sem,
    tile_sem,
    share_sem,
    proj_sem,
    part_sem,
    grads_sem,
    grads_x_sem,
    back_sem,
    sums_sem,
):
    p = lax.axis_index("paper")
    x = lax.axis_index("author")
    z = p // nyc
    yc = p % nyc
    block = cite_tiles.shape[1]
    quarter = paper.shape[1]
    sent = []

    def send(src, dst, sems, index, device):
        copy = pltpu.make_async_remote_copy(
            src_ref=src,
            dst_ref=dst,
            send_sem=sems.at[(0,) + index],
            recv_sem=sems.at[(1,) + index],
            device_id=device,
            device_id_type=MESH,
        )
        copy.start()
        sent.append(copy)
        return copy

    def at_x(k):
        return (p, lax.rem(x + k + nx, nx))

    def at_yc(k):
        return (z * nyc + lax.rem(yc + k + nyc, nyc), x)

    def at_z(k):
        return (lax.rem(z + k + nz, nz) * nyc + yc, x)

    columns = pl.ds(pl.multiple_of(x * quarter, quarter), quarter)
    loads = []
    for i, w in enumerate((w_cite, w_write, w_self)):
        loads.append(pltpu.make_async_copy(w.at[:, columns], win.at[i], local_sem.at[i]))
        loads.append(pltpu.make_async_copy(w.at[columns, :], rows.at[i], local_sem.at[3 + i]))
    for load in loads:
        load.start()

    barrier = pltpu.get_barrier_semaphore()
    peers = [at_x(k) for k in range(1, nx)] + [at_yc(k) for k in range(1, nyc)] + [at_z(k) for k in range(1, nz)]
    for device in peers:
        pl.semaphore_signal(barrier, inc=1, device_id=device, device_id_type=MESH)
    pl.semaphore_wait(barrier, len(peers))

    feats_in = {}
    for m, own in enumerate((paper, author)):
        for k in range(1, nx):
            feats_in[m, k] = send(own, feats.at[m, x], feats_sem, (m, k), at_x(k))

    meta_in = []
    for k in range(1, nyc):
        to = lax.rem(yc + k, nyc)
        meta_in.append(send(meta_f.at[to], meta_fv.at[yc], meta_sem, (0, k), at_yc(k)))
        meta_in.append(send(meta_i.at[to], meta_iv.at[yc], meta_sem, (1, k), at_yc(k)))
    meta_fv[yc] = meta_f[yc]
    meta_iv[yc] = meta_i[yc]

    tiles_in = {}
    for m, source in enumerate((cite_tiles, write_tiles)):

        def place(i, carry):
            for j in range(nz):
                slots[m, i, j // 2, j % 2] = source[slot_tile[m, i * nz + j]]
            return carry

        lax.fori_loop(0, nyc, place, 0)
        for k in range(1, nyc):
            to = lax.rem(yc + k, nyc)
            for half in range(2):
                q = lax.rem(x + half, nx)
                tiles_in[m, k, half] = send(
                    slots.at[m, to, q], tiles.at[m, yc, q], tile_sem, (m, half, k), at_yc(k)
                )

    for load in loads:
        load.wait()
    turns = ((nz // 2, nz - 1 - nz // 2), (nz - 1 - nz // 2, nz // 2))
    ring = {}

    def pass_on(m, way, k):
        sign = 1 if way == 0 else -1
        origin = lax.rem(z - sign * (k - 1) + nz, nz)
        ring[m, way, k] = send(
            proj.at[m, origin], proj.at[m, origin], proj_sem, (m, way, k), at_z(sign)
        )

    for m, own in enumerate((paper, author)):
        feats[m, x] = own[...]
        for k in range(1, nx):
            feats_in[m, k].wait_recv()
        total = dot(feats[m, 0], win[m, 0:quarter, :])
        for i in range(1, nx):
            total += dot(feats[m, i], win[m, i * quarter : (i + 1) * quarter, :])
        total = total.astype(BF16)
        proj[m, z, 0] = total[0:block]
        proj[m, z, 1] = total[block:]
        for way in range(2):
            pass_on(m, way, 1)
    total = dot(feats[0, 0], win[2, 0:quarter, :])
    for i in range(1, nx):
        total += dot(feats[0, i], win[2, i * quarter : (i + 1) * quarter, :])
    pre[...] = total

    shared_in = {}
    for m in range(2):
        for k in range(1, nyc):
            origin = lax.rem(yc - k + nyc, nyc)
            for half in range(2):
                tiles_in[m, k, half].wait_recv()
                q = lax.rem(x + half, nx)
                place_at = tiles.at[m, origin, q]
                shared_in[m, k, half] = send(
                    place_at, place_at, share_sem, (m, half, k), at_x(1 if half == 0 else -1)
                )
        for k in range(2, nz // 2 + 1):
            if k - 1 <= nz // 2 and m == 0:
                for n in range(2):
                    for way in range(2):
                        if k <= turns[n][way]:
                            ring[n, way, k - 1].wait_recv()
                            pass_on(n, way, k)
    for m in range(2):
        for i in range(nx):
            tiles[m, yc, i] = slots[m, yc, i]
    for copy in meta_in:
        copy.wait_recv()
    small = [
        pltpu.make_async_copy(meta_fv, meta_fs, local_sem.at[6]),
        pltpu.make_async_copy(meta_iv, meta_is, local_sem.at[7]),
    ]
    for copy in small:
        copy.start()
    for copy in small:
        copy.wait()
    for n in range(2):
        for way in range(2):
            ring[n, way, turns[n][way]].wait_recv()

    def share_of(target):
        acc[...] = jnp.zeros_like(acc)

        def step(i, carry):
            m = i // nz
            s = i % nz
            source = meta_is[target, 0, i]
            product = dot(
                tiles[m, target, s // 2, s % 2],
                proj[m, s, source],
            )
            acc[0:block, :] += meta_fs[target, 0, i] * product
            acc[block:, :] += meta_fs[target, 1, i] * product
            return carry

        lax.fori_loop(0, 2 * nz, step, 0)

    share_of(yc)
    pre[...] += acc[...]
    part_in = []
    for k in range(1, nyc):
        for m in range(2):
            for half in range(2):
                shared_in[m, nyc - k, half].wait_recv()
        share_of(lax.rem(yc + k, nyc))
        part_send[k] = acc[...].astype(BF16)
        part_in.append(send(part_send.at[k], part_recv.at[k], part_sem, (k,), at_yc(k)))
    for k in range(1, nyc):
        part_in[k - 1].wait_recv()
        pre[...] += part_recv[k].astype(F32)

    preact = pre[...]
    sigma = jax.nn.sigmoid(preact)
    paper_out[...] = (paper[...].astype(F32) + preact * sigma).astype(BF16)
    slope = sigma * (1.0 + preact * (1.0 - sigma))
    own = (cot[...].astype(F32) * slope).astype(BF16)
    grads[yc, 0] = own[0:block]
    grads[yc, 1] = own[block:]
    grads_x[x] = own
    grads_in = [send(grads.at[yc], grads.at[yc], grads_sem, (k,), at_yc(k)) for k in range(1, nyc)]
    grads_x_in = [send(grads_x.at[x], grads_x.at[x], grads_x_sem, (k,), at_x(k)) for k in range(1, nx)]

    def back_of(m, place_z):
        acc[...] = jnp.zeros_like(acc)

        def step(i, carry):
            column = m * nz + place_z
            target = meta_is[i, 1, column]
            product = dot_left_flipped(
                tiles[m, i, place_z // 2, place_z % 2],
                grads[i, target],
            )
            acc[0:block, :] += meta_fs[i, 2, column] * product
            acc[block:, :] += meta_fs[i, 3, column] * product
            return carry

        lax.fori_loop(0, nyc, step, 0)

    for copy in grads_in:
        copy.wait_recv()
    back = {}
    for k in range(1, nz // 2 + 1):
        for m in range(2):
            for way in range(2):
                if k <= turns[m][way]:
                    sign = 1 if way == 0 else -1
                    distance = turns[m][way] - k + 1
                    back_of(m, lax.rem(z + sign * distance + nz, nz))
                    total = acc[...]
                    if k > 1:
                        back[m, way, k - 1].wait_recv()
                        total += back_recv[m, way, k - 1].astype(F32)
                    back_send[m, way, k] = total.astype(BF16)
                    back[m, way, k] = send(
                        back_send.at[m, way, k],
                        back_recv.at[m, way, k],
                        back_sem,
                        (m, way, k),
                        at_z(sign),
                    )

    for copy in grads_x_in:
        copy.wait_recv()
    total = cot[...].astype(F32)
    for i in range(nx):
        total += dot_right_flipped(grads_x[i], rows[2, :, i * quarter : (i + 1) * quarter])
    pre[...] = total
    sums_in = {}
    for m in range(2):
        back_of(m, z)
        total = acc[...]
        for way in range(2):
            back[m, way, turns[m][way]].wait_recv()
            total += back_recv[m, way, turns[m][way]].astype(F32)
        sums[m, x] = total.astype(BF16)
        for k in range(1, nx):
            sums_in[m, k] = send(sums.at[m, x], sums.at[m, x], sums_sem, (m, k), at_x(k))
    for m, out in enumerate((paper_grad, author_grad)):
        for k in range(1, nx):
            sums_in[m, k].wait_recv()
        total = dot_right_flipped(sums[m, 0], rows[m, :, 0:quarter])
        for i in range(1, nx):
            total += dot_right_flipped(sums[m, i], rows[m, :, i * quarter : (i + 1) * quarter])
        if m == 0:
            total += pre[...]
        out[...] = total.astype(BF16)
    for copy in sent:
        copy.wait_send()


def listing(owner, values, nyc, nz):
    places = jnp.arange(nz, dtype=jnp.int32)[None, :] * nyc + jnp.arange(nyc, dtype=jnp.int32)[:, None]
    named = owner[:, 0][:, None, None] == places[None]
    return jnp.sum(jnp.where(named[None], values[:, :, None, None], 0), axis=1)


def body(
    nx,
    paper_feat,
    author_feat,
    cite_owner,
    cite_source,
    cite_target,
    cite_edges,
    cite_count,
    citation_weight_tiles,
    write_owner,
    write_paper,
    write_author,
    write_edges,
    authorship_weight_tiles,
    w_self,
    w_cite,
    w_write,
    cotangent,
):
    nyc = 4 * CORES
    nz = lax.axis_size("paper") // nyc
    n_rows, quarter = paper_feat.shape
    block = citation_weight_tiles.shape[1]
    width = w_self.shape[0]

    live = jnp.arange(cite_edges.shape[0], dtype=jnp.int32) < cite_count[0]
    cite_scale = jnp.where(live, 1.0 / cite_edges.astype(F32), 0.0)
    write_scale = 1.0 / write_edges.astype(F32)
    floats, ints, order = [], [], []
    for owner, scale, target, source in (
        (cite_owner, cite_scale, cite_target, cite_source),
        (write_owner, write_scale, write_paper, write_author),
    ):
        floats.append(
            listing(
                owner,
                jnp.stack([
                    jnp.where(target == 0, scale, 0.0),
                    jnp.where(target == 1, scale, 0.0),
                    jnp.where(source == 0, scale, 0.0),
                    jnp.where(source == 1, scale, 0.0),
                ]),
                nyc,
                nz,
            )
        )
        number = jnp.arange(owner.shape[0], dtype=jnp.int32)
        found = listing(owner, jnp.stack([source, target, number]), nyc, nz)
        ints.append(found[:2])
        order.append(found[2].reshape(-1))

    def spread(parts):
        joined = jnp.stack(parts, axis=2)
        joined = joined.transpose(1, 0, 2, 3).reshape(nyc, -1, 2 * nz)
        return jnp.pad(joined, ((0, 0), (0, 8 - joined.shape[1]), (0, 128 - 2 * nz)))

    meta_f, meta_i, slot_tile = spread(floats), spread(ints), jnp.stack(order)
    steps = nz // 2 + 1
    vmem = pl.BlockSpec(memory_space=pltpu.VMEM)
    hbm = pl.BlockSpec(memory_space=pl.ANY)
    unit = jax.ShapeDtypeStruct((n_rows, quarter), BF16)

    def sems(*shape):
        return pltpu.SemaphoreType.DMA((2,) + shape)

    return pl.pallas_call(
        functools.partial(kernel, nx, nyc, nz),
        out_shape=(unit, unit, unit),
        in_specs=[pl.BlockSpec(memory_space=pltpu.SMEM)] + [vmem] * 7 + [hbm] * 3,
        out_specs=(vmem, vmem, vmem),
        scratch_shapes=[
            pltpu.VMEM((3, width, quarter), BF16),
            pltpu.VMEM((3, quarter, width), BF16),
            pltpu.VMEM((2, nx, n_rows, quarter), BF16),
            pltpu.VMEM((2, nz, 2, block, quarter), BF16),
            pltpu.VMEM((2, nyc, nz // 2, 2, block, block), BF16),
            pltpu.VMEM((2, nyc, nz // 2, 2, block, block), BF16),
            pltpu.VMEM((nyc, 8, 128), F32),
            pltpu.VMEM((nyc, 8, 128), jnp.int32),
            pltpu.SMEM((nyc, 8, 128), F32),
            pltpu.SMEM((nyc, 8, 128), jnp.int32),
            pltpu.VMEM((n_rows, quarter), F32),
            pltpu.VMEM((nyc, n_rows, quarter), BF16),
            pltpu.VMEM((nyc, n_rows, quarter), BF16),
            pltpu.VMEM((n_rows, quarter), F32),
            pltpu.VMEM((nyc, 2, block, quarter), BF16),
            pltpu.VMEM((nx, n_rows, quarter), BF16),
            pltpu.VMEM((2, 2, steps, n_rows, quarter), BF16),
            pltpu.VMEM((2, 2, steps, n_rows, quarter), BF16),
            pltpu.VMEM((2, nx, n_rows, quarter), BF16),
            pltpu.SemaphoreType.DMA((8,)),
            sems(2, nx),
            sems(2, nyc),
            sems(2, 2, nyc),
            sems(2, 2, nyc),
            sems(2, 2, steps),
            sems(nyc),
            sems(nyc),
            sems(nx),
            sems(2, 2, steps),
            sems(2, nx),
        ],
        compiler_params=pltpu.CompilerParams(
            collective_id=0, has_side_effects=True, vmem_limit_bytes=56 * 1024 * 1024
        ),
    )(
        slot_tile,
        paper_feat,
        author_feat,
        cotangent,
        meta_f,
        meta_i,
        citation_weight_tiles,
        authorship_weight_tiles,
        w_self,
        w_cite,
        w_write,
    )


def solution(mesh):
    in_specs = (
        P("paper", "author"),
        P("paper", "author"),
        P("paper", None),
        P("paper"),
        P("paper"),
        P("paper"),
        P("paper"),
        P("paper", None, None),
        P("paper", None),
        P("paper"),
        P("paper"),
        P("paper"),
        P("paper", None, None),
        P(),
        P(),
        P(),
        P("paper", "author"),
    )
    out_specs = (P("paper", "author"), P("paper", "author"), P("paper", "author"))
    return jax.shard_map(
        functools.partial(body, mesh.shape["author"]),
        mesh=mesh,
        in_specs=in_specs,
        out_specs=out_specs,
        check_vma=False,
    )
```

```python
import functools

import jax
import jax.numpy as jnp
from jax import lax
from jax.experimental import pallas as pl
from jax.experimental.pallas import tpu as pltpu
from jax.sharding import PartitionSpec as P

MESH = pl.DeviceIdType.MESH
F32 = jnp.float32
BF16 = jnp.bfloat16
CORES = 2


def dot(left, right):
    return jnp.dot(left, right, preferred_element_type=F32)


def dot_left_flipped(left, right):
    return lax.dot_general(left, right, (((0,), (0,)), ((), ())), preferred_element_type=F32)


def dot_right_flipped(left, right):
    return lax.dot_general(left, right, (((1,), (1,)), ((), ())), preferred_element_type=F32)


def kernel(
    nx,
    nyc,
    nz,
    cite_count,
    cite_owner,
    cite_source,
    cite_target,
    cite_edges,
    write_owner,
    write_author,
    write_paper,
    write_edges,
    paper,
    author,
    cot,
    cite_tiles_hbm,
    write_tiles_hbm,
    w_self,
    w_cite,
    w_write,
    paper_out,
    paper_grad,
    author_grad,
    cite_tiles,
    write_tiles,
    win,
    rows,
    feats,
    proj,
    meta_f,
    meta_i,
    slot_tab,
    slots,
    tiles,
    meta_fv,
    meta_iv,
    meta_fs,
    meta_is,
    acc,
    part_send,
    part_recv,
    pre,
    grads,
    grads_x,
    back_send,
    back_recv,
    sums,
    local_sem,
    feats_sem,
    meta_sem,
    tile_sem,
    share_sem,
    proj_sem,
    part_sem,
    grads_sem,
    grads_x_sem,
    back_sem,
    sums_sem,
):
    p = lax.axis_index("paper")
    x = lax.axis_index("author")
    z = p // nyc
    yc = p % nyc
    block = cite_tiles.shape[1]
    quarter = paper.shape[1]
    sent = []

    def send(src, dst, sems, index, device):
        copy = pltpu.make_async_remote_copy(
            src_ref=src,
            dst_ref=dst,
            send_sem=sems.at[(0,) + index],
            recv_sem=sems.at[(1,) + index],
            device_id=device,
            device_id_type=MESH,
        )
        copy.start()
        sent.append(copy)
        return copy

    def at_x(k):
        return (p, lax.rem(x + k + nx, nx))

    ny = nyc // CORES
    offsets = [(0, 1), (1, 0), (ny - 1, 0), (1, 1), (ny - 1, 1), (2, 0), (2, 1)]
    n_off = len(offsets)

    def there(k):
        dy, dc = offsets[k]
        return lax.rem(yc // CORES + dy, ny) * CORES + lax.rem(yc + dc, CORES)

    def back_from(k):
        dy, dc = offsets[k]
        return lax.rem(yc // CORES + ny - dy, ny) * CORES + lax.rem(yc + dc, CORES)

    def at_yc(k):
        return (z * nyc + there(k), x)

    def at_z(k):
        return (lax.rem(z + k + nz, nz) * nyc + yc, x)

    barrier = pltpu.get_barrier_semaphore()
    peers = [at_x(k) for k in range(1, nx)] + [at_yc(k) for k in range(n_off)] + [at_z(k) for k in range(1, nz)]
    for device in peers:
        pl.semaphore_signal(barrier, inc=1, device_id=device, device_id_type=MESH)

    tile_loads = [
        pltpu.make_async_copy(cite_tiles_hbm, cite_tiles, local_sem.at[6]),
        pltpu.make_async_copy(write_tiles_hbm, write_tiles, local_sem.at[7]),
    ]
    columns = pl.ds(pl.multiple_of(x * quarter, quarter), quarter)
    loads = []
    for i, w in enumerate((w_cite, w_write, w_self)):
        loads.append(pltpu.make_async_copy(w.at[:, columns], win.at[i], local_sem.at[i]))
        loads.append(pltpu.make_async_copy(w.at[columns, :], rows.at[i], local_sem.at[3 + i]))
    for load in tile_loads + loads:
        load.start()

    n_slots = nyc * nz
    lanes = lax.broadcasted_iota(jnp.int32, (n_slots, 128), 1)
    table_f = jnp.zeros((n_slots, 128), F32)
    table_i = jnp.zeros((n_slots, 128), jnp.int32)
    lists = (
        (cite_owner, cite_source, cite_target, cite_edges),
        (write_owner, write_author, write_paper, write_edges),
    )
    for m, (owner, sources, targets, edges) in enumerate(lists):
        n = owner.shape[1]
        number = lax.broadcasted_iota(jnp.int32, (n_slots, n), 1)
        slot = lax.broadcasted_iota(jnp.int32, (n_slots, n), 0)
        named = owner[...] == (slot % nz) * nyc + slot // nz
        scale = 1.0 / edges[...].astype(F32)
        source = jnp.max(jnp.where(named, sources[...], 0), axis=1, keepdims=True)
        target = jnp.max(jnp.where(named, targets[...], 0), axis=1, keepdims=True)
        place = jnp.max(jnp.where(named, number, 0), axis=1, keepdims=True)
        live = named & (number < cite_count[0]) if m == 0 else named
        scale = jnp.sum(jnp.where(live, scale, 0.0), axis=1, keepdims=True)
        for kind, value in enumerate((source, target, place)):
            table_i = jnp.where(lanes == 4 * m + kind, value, table_i)
        for kind, (end, b) in enumerate(((target, 0), (target, 1), (source, 0), (source, 1))):
            table_f = jnp.where(lanes == 4 * m + kind, jnp.where(end == b, scale, 0.0), table_f)
    meta_f[...] = table_f.reshape(nyc, nz, 128)
    meta_i[...] = table_i.reshape(nyc, nz, 128)
    tab = pltpu.make_async_copy(meta_i, slot_tab, local_sem.at[8])
    tab.start()
    meta_fv[yc] = meta_f[yc]
    meta_iv[yc] = meta_i[yc]

    pl.semaphore_wait(barrier, len(peers))

    feats_in = {}
    for m, own in enumerate((paper, author)):
        for k in range(1, nx):
            feats_in[m, k] = send(own, feats.at[m, x], feats_sem, (m, k), at_x(k))
    meta_in = []
    for k in range(n_off):
        to = there(k)
        meta_in.append(send(meta_f.at[to], meta_fv.at[yc], meta_sem, (0, k), at_yc(k)))
        meta_in.append(send(meta_i.at[to], meta_iv.at[yc], meta_sem, (1, k), at_yc(k)))

    tab.wait()
    for load in tile_loads:
        load.wait()
    tiles_in = {}
    for k in range(n_off):
        to = there(k)
        for m, source in enumerate((cite_tiles, write_tiles)):
            for j in range(nz):
                slots[m, to, j // 2, j % 2] = source[slot_tab[to, j, 4 * m + 2]]
            for half in range(nx if k == 0 else 2):
                q = lax.rem(x + half, nx)
                tiles_in[m, k, half] = send(
                    slots.at[m, to, q], tiles.at[m, yc, q], tile_sem, (m, half, k), at_yc(k)
                )
    for m, source in enumerate((cite_tiles, write_tiles)):
        for j in range(nz):
            tiles[m, yc, j // 2, j % 2] = source[slot_tab[yc, j, 4 * m + 2]]

    shared_in = {}

    def share_on(k):
        for m in range(2):
            for half in range(2):
                tiles_in[m, k, half].wait_recv()
                place_at = tiles.at[m, back_from(k), lax.rem(x + half, nx)]
                shared_in[m, k, half] = send(
                    place_at, place_at, share_sem, (m, half, k), at_x(1 if half == 0 else -1)
                )

    turns = ((nz // 2, nz - 1 - nz // 2), (nz - 1 - nz // 2, nz // 2))
    ring = {}

    def pass_on(m, way, k):
        sign = 1 if way == 0 else -1
        origin = lax.rem(z - sign * (k - 1) + nz, nz)
        ring[m, way, k] = send(
            proj.at[m, origin], proj.at[m, origin], proj_sem, (m, way, k), at_z(sign)
        )

    def ring_step(k):
        for m in range(2):
            for way in range(2):
                if k <= turns[m][way]:
                    ring[m, way, k - 1].wait_recv()
                    pass_on(m, way, k)

    def project(m, window):
        total = dot(feats[m, 0], win[window, 0:quarter, :])
        for i in range(1, nx):
            total += dot(feats[m, i], win[window, i * quarter : (i + 1) * quarter, :])
        return total

    for load in loads:
        load.wait()
    for m, own in enumerate((paper, author)):
        feats[m, x] = own[...]
        for k in range(1, nx):
            feats_in[m, k].wait_recv()
        total = project(m, m).astype(BF16)
        proj[m, z, 0] = total[0:block]
        proj[m, z, 1] = total[block:]
        for way in range(2):
            pass_on(m, way, 1)
        share_on(2 * m + 1)
        share_on(2 * m + 2)
    ring_step(2)
    pre[...] = project(0, 2)
    ring_step(3)
    share_on(5)
    share_on(6)
    ring_step(4)
    for copy in meta_in:
        copy.wait_recv()
    small = [
        pltpu.make_async_copy(meta_fv, meta_fs, local_sem.at[6]),
        pltpu.make_async_copy(meta_iv, meta_is, local_sem.at[7]),
    ]
    for copy in small:
        copy.start()
    for copy in small:
        copy.wait()
    for m in range(2):
        for way in range(2):
            ring[m, way, turns[m][way]].wait_recv()

    def share_of(target):
        acc[...] = jnp.zeros_like(acc)

        def step(i, carry):
            m = i // nz
            s = i % nz
            source = meta_is[target, s, 4 * m]
            product = dot(
                tiles[m, target, s // 2, s % 2],
                proj[m, s, source],
            )
            acc[0:block, :] += meta_fs[target, s, 4 * m] * product
            acc[block:, :] += meta_fs[target, s, 4 * m + 1] * product
            return carry

        lax.fori_loop(0, 2 * nz, step, 0)

    share_of(yc)
    pre[...] += acc[...]
    part_in = {}
    for k in range(n_off):
        opposite = (0, 2, 1, 4, 3, 5, 6)[k]
        if k == 0:
            for m in range(2):
                for half in range(nx):
                    tiles_in[m, k, half].wait_recv()
        else:
            for m in range(2):
                for half in range(2):
                    shared_in[m, k, half].wait_recv()
        share_of(there(opposite))
        part_send[opposite] = acc[...].astype(BF16)
        part_in[opposite] = send(
            part_send.at[opposite], part_recv.at[opposite], part_sem, (opposite,), at_yc(opposite)
        )
    for k in range(n_off):
        part_in[k].wait_recv()
        pre[...] += part_recv[k].astype(F32)

    preact = pre[...]
    sigma = jax.nn.sigmoid(preact)
    paper_out[...] = (paper[...].astype(F32) + preact * sigma).astype(BF16)
    slope = sigma * (1.0 + preact * (1.0 - sigma))
    own = (cot[...].astype(F32) * slope).astype(BF16)
    grads[yc, 0] = own[0:block]
    grads[yc, 1] = own[block:]
    grads_x[x] = own
    grads_in = [send(grads.at[yc], grads.at[yc], grads_sem, (k,), at_yc(k)) for k in range(n_off)]
    grads_x_in = [send(grads_x.at[x], grads_x.at[x], grads_x_sem, (k,), at_x(k)) for k in range(1, nx)]

    def back_of(m, place_z):
        acc[...] = jnp.zeros_like(acc)

        def step(i, carry):
            target = meta_is[i, place_z, 4 * m + 1]
            product = dot_left_flipped(
                tiles[m, i, place_z // 2, place_z % 2],
                grads[i, target],
            )
            acc[0:block, :] += meta_fs[i, place_z, 4 * m + 2] * product
            acc[block:, :] += meta_fs[i, place_z, 4 * m + 3] * product
            return carry

        lax.fori_loop(0, nyc, step, 0)

    for copy in grads_in:
        copy.wait_recv()
    back = {}
    for k in range(1, nz // 2 + 1):
        for m in range(2):
            for way in range(2):
                if k <= turns[m][way]:
                    sign = 1 if way == 0 else -1
                    distance = turns[m][way] - k + 1
                    back_of(m, lax.rem(z + sign * distance + nz, nz))
                    total = acc[...]
                    if k > 1:
                        back[m, way, k - 1].wait_recv()
                        total += back_recv[m, way, k - 1].astype(F32)
                    back_send[m, way, k] = total.astype(BF16)
                    back[m, way, k] = send(
                        back_send.at[m, way, k],
                        back_recv.at[m, way, k],
                        back_sem,
                        (m, way, k),
                        at_z(sign),
                    )

    for copy in grads_x_in:
        copy.wait_recv()
    total = cot[...].astype(F32)
    for i in range(nx):
        total += dot_right_flipped(grads_x[i], rows[2, :, i * quarter : (i + 1) * quarter])
    pre[...] = total
    sums_in = {}
    for m in range(2):
        back_of(m, z)
        total = acc[...]
        for way in range(2):
            back[m, way, turns[m][way]].wait_recv()
            total += back_recv[m, way, turns[m][way]].astype(F32)
        sums[m, x] = total.astype(BF16)
        for k in range(1, nx):
            sums_in[m, k] = send(sums.at[m, x], sums.at[m, x], sums_sem, (m, k), at_x(k))
    for m, out in enumerate((paper_grad, author_grad)):
        for k in range(1, nx):
            sums_in[m, k].wait_recv()
        total = dot_right_flipped(sums[m, 0], rows[m, :, 0:quarter])
        for i in range(1, nx):
            total += dot_right_flipped(sums[m, i], rows[m, :, i * quarter : (i + 1) * quarter])
        if m == 0:
            total += pre[...]
        out[...] = total.astype(BF16)
    for copy in sent:
        copy.wait_send()


def body(
    nx,
    paper_feat,
    author_feat,
    cite_owner,
    cite_source,
    cite_target,
    cite_edges,
    cite_count,
    citation_weight_tiles,
    write_owner,
    write_paper,
    write_author,
    write_edges,
    authorship_weight_tiles,
    w_self,
    w_cite,
    w_write,
    cotangent,
):
    nyc = 4 * CORES
    nz = lax.axis_size("paper") // nyc
    n_rows, quarter = paper_feat.shape
    block = citation_weight_tiles.shape[1]
    width = w_self.shape[0]

    lists = (
        cite_owner, cite_source, cite_target, cite_edges, write_owner, write_author, write_paper, write_edges
    )
    steps = nz // 2 + 1
    vmem = pl.BlockSpec(memory_space=pltpu.VMEM)
    hbm = pl.BlockSpec(memory_space=pl.ANY)
    unit = jax.ShapeDtypeStruct((n_rows, quarter), BF16)

    def sems(*shape):
        return pltpu.SemaphoreType.DMA((2,) + shape)

    return pl.pallas_call(
        functools.partial(kernel, nx, nyc, nz),
        out_shape=(unit, unit, unit),
        in_specs=[pl.BlockSpec(memory_space=pltpu.SMEM)] + [vmem] * 11 + [hbm] * 5,
        out_specs=(vmem, vmem, vmem),
        scratch_shapes=[
            pltpu.VMEM(citation_weight_tiles.shape, BF16),
            pltpu.VMEM(authorship_weight_tiles.shape, BF16),
            pltpu.VMEM((3, width, quarter), BF16),
            pltpu.VMEM((3, quarter, width), BF16),
            pltpu.VMEM((2, nx, n_rows, quarter), BF16),
            pltpu.VMEM((2, nz, 2, block, quarter), BF16),
            pltpu.VMEM((nyc, nz, 128), F32),
            pltpu.VMEM((nyc, nz, 128), jnp.int32),
            pltpu.SMEM((nyc, nz, 128), jnp.int32),
            pltpu.VMEM((2, nyc, nz // 2, 2, block, block), BF16),
            pltpu.VMEM((2, nyc, nz // 2, 2, block, block), BF16),
            pltpu.VMEM((nyc, nz, 128), F32),
            pltpu.VMEM((nyc, nz, 128), jnp.int32),
            pltpu.SMEM((nyc, nz, 128), F32),
            pltpu.SMEM((nyc, nz, 128), jnp.int32),
            pltpu.VMEM((n_rows, quarter), F32),
            pltpu.VMEM((nyc, n_rows, quarter), BF16),
            pltpu.VMEM((nyc, n_rows, quarter), BF16),
            pltpu.VMEM((n_rows, quarter), F32),
            pltpu.VMEM((nyc, 2, block, quarter), BF16),
            pltpu.VMEM((nx, n_rows, quarter), BF16),
            pltpu.VMEM((2, 2, steps, n_rows, quarter), BF16),
            pltpu.VMEM((2, 2, steps, n_rows, quarter), BF16),
            pltpu.VMEM((2, nx, n_rows, quarter), BF16),
            pltpu.SemaphoreType.DMA((9,)),
            sems(2, nx),
            sems(2, nyc),
            sems(2, nx, nyc),
            sems(2, 2, nyc),
            sems(2, 2, steps),
            sems(nyc),
            sems(nyc),
            sems(nx),
            sems(2, 2, steps),
            sems(2, nx),
        ],
        compiler_params=pltpu.CompilerParams(
            collective_id=0, has_side_effects=True, vmem_limit_bytes=56 * 1024 * 1024
        ),
    )(
        cite_count,
        *[a.reshape(1, -1) for a in lists],
        paper_feat,
        author_feat,
        cotangent,
        citation_weight_tiles,
        authorship_weight_tiles,
        w_self,
        w_cite,
        w_write,
    )


def solution(mesh):
    in_specs = (
        P("paper", "author"),
        P("paper", "author"),
        P("paper", None),
        P("paper"),
        P("paper"),
        P("paper"),
        P("paper"),
        P("paper", None, None),
        P("paper", None),
        P("paper"),
        P("paper"),
        P("paper"),
        P("paper", None, None),
        P(),
        P(),
        P(),
        P("paper", "author"),
    )
    out_specs = (P("paper", "author"), P("paper", "author"), P("paper", "author"))
    return jax.shard_map(
        functools.partial(body, mesh.shape["author"]),
        mesh=mesh,
        in_specs=in_specs,
        out_specs=out_specs,
        check_vma=False,
    )
```

```python
import functools

import jax
import jax.numpy as jnp
from jax import lax
from jax.experimental import pallas as pl
from jax.experimental.pallas import tpu as pltpu
from jax.sharding import PartitionSpec as P

MESH = pl.DeviceIdType.MESH
F32 = jnp.float32
BF16 = jnp.bfloat16
CORES = 2
UNROLL = 8


def dot(left, right):
    return jnp.dot(left, right, preferred_element_type=F32)


def dot_left_flipped(left, right):
    return lax.dot_general(left, right, (((0,), (0,)), ((), ())), preferred_element_type=F32)


def dot_right_flipped(left, right):
    return lax.dot_general(left, right, (((1,), (1,)), ((), ())), preferred_element_type=F32)


def kernel(
    nx,
    nyc,
    nz,
    cite_count,
    cite_owner,
    cite_source,
    cite_target,
    cite_edges,
    write_owner,
    write_author,
    write_paper,
    write_edges,
    paper,
    author,
    cot,
    cite_tiles_hbm,
    write_tiles_hbm,
    w_self,
    w_cite,
    w_write,
    paper_out,
    paper_grad,
    author_grad,
    cite_tiles,
    write_tiles,
    win,
    rows,
    feats,
    proj,
    meta_f,
    meta_i,
    slot_tab,
    slots,
    tiles,
    meta_fv,
    meta_iv,
    meta_fs,
    meta_is,
    acc,
    part_send,
    part_recv,
    pre,
    grads,
    grads_x,
    back_send,
    back_recv,
    sums,
    local_sem,
    feats_sem,
    meta_sem,
    tile_sem,
    share_sem,
    proj_sem,
    part_sem,
    grads_sem,
    grads_x_sem,
    back_sem,
    sums_sem,
):
    p = lax.axis_index("paper")
    x = lax.axis_index("author")
    z = p // nyc
    yc = p % nyc
    block = cite_tiles.shape[1]
    quarter = paper.shape[1]
    sent = []

    def send(src, dst, sems, index, device):
        copy = pltpu.make_async_remote_copy(
            src_ref=src,
            dst_ref=dst,
            send_sem=sems.at[(0,) + index],
            recv_sem=sems.at[(1,) + index],
            device_id=device,
            device_id_type=MESH,
        )
        copy.start()
        sent.append(copy)
        return copy

    def at_x(k):
        return (p, lax.rem(x + k + nx, nx))

    ny = nyc // CORES
    offsets = [(0, 1), (1, 1), (ny - 1, 1), (2, 1), (1, 0), (ny - 1, 0), (2, 0)]
    opposite = (0, 2, 1, 3, 5, 4, 6)
    n_off = len(offsets)

    def there(k):
        dy, dc = offsets[k]
        return lax.rem(yc // CORES + dy, ny) * CORES + lax.rem(yc + dc, CORES)

    def back_from(k):
        dy, dc = offsets[k]
        return lax.rem(yc // CORES + ny - dy, ny) * CORES + lax.rem(yc + dc, CORES)

    def at_yc(k):
        return (z * nyc + there(k), x)

    def at_z(k):
        return (lax.rem(z + k + nz, nz) * nyc + yc, x)

    def gather_x(buffer, sems, m, own):
        return {(m, k): send(own, buffer.at[m, x], sems, (m, k % nx), at_x(k)) for k in (1, -1)}

    def chain_x(copies, buffer, sems, m):
        onward = 1 if m == 0 else -1
        copies[m, onward].wait_recv()
        piece = buffer.at[m, lax.rem(x - onward + nx, nx)]
        copies[m, 2] = send(piece, piece, sems, (m, 2), at_x(onward))

    barrier = pltpu.get_barrier_semaphore()
    peers = [at_x(k) for k in range(1, nx)] + [at_yc(k) for k in range(n_off)] + [at_z(k) for k in range(1, nz)]
    for device in peers:
        pl.semaphore_signal(barrier, inc=1, device_id=device, device_id_type=MESH)

    tile_loads = [
        pltpu.make_async_copy(cite_tiles_hbm, cite_tiles, local_sem.at[6]),
        pltpu.make_async_copy(write_tiles_hbm, write_tiles, local_sem.at[7]),
    ]
    columns = pl.ds(pl.multiple_of(x * quarter, quarter), quarter)
    loads = []
    for i, w in enumerate((w_cite, w_write, w_self)):
        loads.append(pltpu.make_async_copy(w.at[:, columns], win.at[i], local_sem.at[i]))
        loads.append(pltpu.make_async_copy(w.at[columns, :], rows.at[i], local_sem.at[3 + i]))
    for load in tile_loads + loads:
        load.start()

    n_slots = nyc * nz
    lanes = lax.broadcasted_iota(jnp.int32, (n_slots, 128), 1)
    table_f = jnp.zeros((n_slots, 128), F32)
    table_i = jnp.zeros((n_slots, 128), jnp.int32)
    lists = (
        (cite_owner, cite_source, cite_target, cite_edges),
        (write_owner, write_author, write_paper, write_edges),
    )
    for m, (owner, sources, targets, edges) in enumerate(lists):
        n = owner.shape[1]
        number = lax.broadcasted_iota(jnp.int32, (n_slots, n), 1)
        slot = lax.broadcasted_iota(jnp.int32, (n_slots, n), 0)
        named = owner[...] == (slot % nz) * nyc + slot // nz
        scale = 1.0 / edges[...].astype(F32)
        source = jnp.max(jnp.where(named, sources[...], 0), axis=1, keepdims=True)
        target = jnp.max(jnp.where(named, targets[...], 0), axis=1, keepdims=True)
        place = jnp.max(jnp.where(named, number, 0), axis=1, keepdims=True)
        live = named & (number < cite_count[0]) if m == 0 else named
        scale = jnp.sum(jnp.where(live, scale, 0.0), axis=1, keepdims=True)
        for kind, value in enumerate((source, target, place)):
            table_i = jnp.where(lanes == 4 * m + kind, value, table_i)
        for kind, (end, b) in enumerate(((target, 0), (target, 1), (source, 0), (source, 1))):
            table_f = jnp.where(lanes == 4 * m + kind, jnp.where(end == b, scale, 0.0), table_f)
    meta_f[...] = table_f.reshape(nyc, nz, 128)
    meta_i[...] = table_i.reshape(nyc, nz, 128)
    tab = pltpu.make_async_copy(meta_i, slot_tab, local_sem.at[8])
    tab.start()
    meta_fv[yc] = meta_f[yc]
    meta_iv[yc] = meta_i[yc]

    pl.semaphore_wait(barrier, len(peers))

    feats_in = gather_x(feats, feats_sem, 0, paper)
    feats_in.update(gather_x(feats, feats_sem, 1, author))
    meta_in = []
    for k in range(n_off):
        to = there(k)
        meta_in.append(send(meta_f.at[to], meta_fv.at[yc], meta_sem, (0, k), at_yc(k)))
        meta_in.append(send(meta_i.at[to], meta_iv.at[yc], meta_sem, (1, k), at_yc(k)))

    tab.wait()
    for load in tile_loads:
        load.wait()
    tiles_in = {}
    for k in range(n_off):
        to = there(k)
        for m, source in enumerate((cite_tiles, write_tiles)):
            for j in range(nz):
                slots[m, to, j // 2, j % 2] = source[slot_tab[to, j, 4 * m + 2]]
            for half in range(nx if k == 0 else 2):
                q = lax.rem(x + half, nx)
                tiles_in[m, k, half] = send(
                    slots.at[m, to, q], tiles.at[m, yc, q], tile_sem, (m, half, k), at_yc(k)
                )
    for m, source in enumerate((cite_tiles, write_tiles)):
        for j in range(nz):
            tiles[m, yc, j // 2, j % 2] = source[slot_tab[yc, j, 4 * m + 2]]

    shared_in = {}

    def share_on(k):
        for m in range(2):
            for half in range(2):
                tiles_in[m, k, half].wait_recv()
                place_at = tiles.at[m, back_from(k), lax.rem(x + half, nx)]
                shared_in[m, k, half] = send(
                    place_at, place_at, share_sem, (m, half, k), at_x(1 if half == 0 else -1)
                )

    turns = ((nz // 2, nz - 1 - nz // 2), (nz - 1 - nz // 2, nz // 2))
    ring = {}

    def pass_on(m, way, k):
        sign = 1 if way == 0 else -1
        origin = lax.rem(z - sign * (k - 1) + nz, nz)
        ring[m, way, k] = send(
            proj.at[m, origin], proj.at[m, origin], proj_sem, (m, way, k), at_z(sign)
        )

    def ring_step(k):
        for m in range(2):
            for way in range(2):
                if k <= turns[m][way]:
                    ring[m, way, k - 1].wait_recv()
                    pass_on(m, way, k)

    def project(m, window):
        total = dot(feats[m, 0], win[window, 0:quarter, :])
        for i in range(1, nx):
            total += dot(feats[m, i], win[window, i * quarter : (i + 1) * quarter, :])
        return total

    for load in loads:
        load.wait()
    for m, own in enumerate((paper, author)):
        feats[m, x] = own[...]
        if m == 0:
            for i in range(2):
                chain_x(feats_in, feats, feats_sem, i)
        for k in (-1 if m == 0 else 1, 2):
            feats_in[m, k].wait_recv()
        total = project(m, m).astype(BF16)
        proj[m, z, 0] = total[0:block]
        proj[m, z, 1] = total[block:]
        for way in range(2):
            pass_on(m, way, 1)
        share_on(2 * m + 1)
        share_on(2 * m + 2)
    ring_step(2)
    pre[...] = project(0, 2)
    ring_step(3)
    share_on(5)
    share_on(6)
    ring_step(4)
    for copy in meta_in:
        copy.wait_recv()
    small = [
        pltpu.make_async_copy(meta_fv, meta_fs, local_sem.at[6]),
        pltpu.make_async_copy(meta_iv, meta_is, local_sem.at[7]),
    ]
    for copy in small:
        copy.start()
    for copy in small:
        copy.wait()
    for m in range(2):
        for way in range(2):
            ring[m, way, turns[m][way]].wait_recv()

    def share_of(target):
        acc[...] = jnp.zeros_like(acc)

        def step(i, carry):
            m = i // nz
            s = i % nz
            source = meta_is[target, s, 4 * m]
            product = dot(
                tiles[m, target, s // 2, s % 2],
                proj[m, s, source],
            )
            acc[0:block, :] += meta_fs[target, s, 4 * m] * product
            acc[block:, :] += meta_fs[target, s, 4 * m + 1] * product
            return carry

        lax.fori_loop(0, 2 * nz, step, 0, unroll=UNROLL)

    part_in = {}

    def share_from(k):
        for m in range(2):
            for half in range(nx if k == 0 else 2):
                (tiles_in if k == 0 else shared_in)[m, k, half].wait_recv()
        share_of(there(opposite[k]))

    def pass_part(slot, device):
        part_send[slot] = acc[...].astype(BF16)
        part_in[slot] = send(part_send.at[slot], part_recv.at[slot], part_sem, (slot,), device)

    for k in range(ny):
        share_from(k)
        pass_part(opposite[k], at_yc(0))
    for k in range(ny, n_off):
        share_from(k)
        part_in[opposite[k] - ny + 1].wait_recv()
        acc[...] += part_recv[opposite[k] - ny + 1].astype(F32)
        pass_part(opposite[k], at_yc(opposite[k]))
    share_of(yc)
    pre[...] += acc[...]
    for k in (0,) + tuple(range(ny, n_off)):
        part_in[k].wait_recv()
        pre[...] += part_recv[k].astype(F32)

    preact = pre[...]
    sigma = jax.nn.sigmoid(preact)
    paper_out[...] = (paper[...].astype(F32) + preact * sigma).astype(BF16)
    slope = sigma * (1.0 + preact * (1.0 - sigma))
    own = (cot[...].astype(F32) * slope).astype(BF16)
    grads[yc, 0] = own[0:block]
    grads[yc, 1] = own[block:]
    grads_x[x] = own
    grads_in = {k: send(grads.at[yc], grads.at[yc], grads_sem, (k,), at_yc(k)) for k in range(ny, n_off)}
    grads_in[0] = send(grads.at[yc], grads.at[yc], grads_sem, (0,), at_yc(0))
    grads_x_in = [send(grads_x.at[x], grads_x.at[x], grads_x_sem, (k,), at_x(k)) for k in range(1, nx)]
    for k in range(ny, n_off):
        grads_in[k].wait_recv()
        piece = grads.at[back_from(k)]
        grads_in[k - ny + 1] = send(piece, piece, grads_sem, (k - ny + 1,), at_yc(0))

    def back_of(m, place_z):
        acc[...] = jnp.zeros_like(acc)

        def step(i, carry):
            target = meta_is[i, place_z, 4 * m + 1]
            product = dot_left_flipped(
                tiles[m, i, place_z // 2, place_z % 2],
                grads[i, target],
            )
            acc[0:block, :] += meta_fs[i, place_z, 4 * m + 2] * product
            acc[block:, :] += meta_fs[i, place_z, 4 * m + 3] * product
            return carry

        lax.fori_loop(0, nyc, step, 0, unroll=UNROLL)

    for k in range(ny):
        grads_in[k].wait_recv()
    back = {}
    for k in range(1, nz // 2 + 1):
        for m in range(2):
            for way in range(2):
                if k <= turns[m][way]:
                    sign = 1 if way == 0 else -1
                    distance = turns[m][way] - k + 1
                    back_of(m, lax.rem(z + sign * distance + nz, nz))
                    total = acc[...]
                    if k > 1:
                        back[m, way, k - 1].wait_recv()
                        total += back_recv[m, way, k - 1].astype(F32)
                    back_send[m, way, k] = total.astype(BF16)
                    back[m, way, k] = send(
                        back_send.at[m, way, k],
                        back_recv.at[m, way, k],
                        back_sem,
                        (m, way, k),
                        at_z(sign),
                    )

    for copy in grads_x_in:
        copy.wait_recv()
    total = cot[...].astype(F32)
    for i in range(nx):
        total += dot_right_flipped(grads_x[i], rows[2, :, i * quarter : (i + 1) * quarter])
    pre[...] = total
    sums_in = {}
    for m in range(2):
        back_of(m, z)
        total = acc[...]
        for way in range(2):
            back[m, way, turns[m][way]].wait_recv()
            total += back_recv[m, way, turns[m][way]].astype(F32)
        sums[m, x] = total.astype(BF16)
        sums_in.update(gather_x(sums, sums_sem, m, sums.at[m, x]))
    for m in range(2):
        chain_x(sums_in, sums, sums_sem, m)
    for m, out in enumerate((paper_grad, author_grad)):
        for k in (-1 if m == 0 else 1, 2):
            sums_in[m, k].wait_recv()
        total = dot_right_flipped(sums[m, 0], rows[m, :, 0:quarter])
        for i in range(1, nx):
            total += dot_right_flipped(sums[m, i], rows[m, :, i * quarter : (i + 1) * quarter])
        if m == 0:
            total += pre[...]
        out[...] = total.astype(BF16)
    for copy in sent:
        copy.wait_send()


def body(
    nx,
    paper_feat,
    author_feat,
    cite_owner,
    cite_source,
    cite_target,
    cite_edges,
    cite_count,
    citation_weight_tiles,
    write_owner,
    write_paper,
    write_author,
    write_edges,
    authorship_weight_tiles,
    w_self,
    w_cite,
    w_write,
    cotangent,
):
    nyc = 4 * CORES
    nz = lax.axis_size("paper") // nyc
    n_rows, quarter = paper_feat.shape
    block = citation_weight_tiles.shape[1]
    width = w_self.shape[0]

    lists = (
        cite_owner, cite_source, cite_target, cite_edges, write_owner, write_author, write_paper, write_edges
    )
    steps = nz // 2 + 1
    vmem = pl.BlockSpec(memory_space=pltpu.VMEM)
    hbm = pl.BlockSpec(memory_space=pl.ANY)
    unit = jax.ShapeDtypeStruct((n_rows, quarter), BF16)

    def sems(*shape):
        return pltpu.SemaphoreType.DMA((2,) + shape)

    return pl.pallas_call(
        functools.partial(kernel, nx, nyc, nz),
        out_shape=(unit, unit, unit),
        in_specs=[pl.BlockSpec(memory_space=pltpu.SMEM)] + [vmem] * 11 + [hbm] * 5,
        out_specs=(vmem, vmem, vmem),
        scratch_shapes=[
            pltpu.VMEM(citation_weight_tiles.shape, BF16),
            pltpu.VMEM(authorship_weight_tiles.shape, BF16),
            pltpu.VMEM((3, width, quarter), BF16),
            pltpu.VMEM((3, quarter, width), BF16),
            pltpu.VMEM((2, nx, n_rows, quarter), BF16),
            pltpu.VMEM((2, nz, 2, block, quarter), BF16),
            pltpu.VMEM((nyc, nz, 128), F32),
            pltpu.VMEM((nyc, nz, 128), jnp.int32),
            pltpu.SMEM((nyc, nz, 128), jnp.int32),
            pltpu.VMEM((2, nyc, nz // 2, 2, block, block), BF16),
            pltpu.VMEM((2, nyc, nz // 2, 2, block, block), BF16),
            pltpu.VMEM((nyc, nz, 128), F32),
            pltpu.VMEM((nyc, nz, 128), jnp.int32),
            pltpu.SMEM((nyc, nz, 128), F32),
            pltpu.SMEM((nyc, nz, 128), jnp.int32),
            pltpu.VMEM((n_rows, quarter), F32),
            pltpu.VMEM((nyc, n_rows, quarter), BF16),
            pltpu.VMEM((nyc, n_rows, quarter), BF16),
            pltpu.VMEM((n_rows, quarter), F32),
            pltpu.VMEM((nyc, 2, block, quarter), BF16),
            pltpu.VMEM((nx, n_rows, quarter), BF16),
            pltpu.VMEM((2, 2, steps, n_rows, quarter), BF16),
            pltpu.VMEM((2, 2, steps, n_rows, quarter), BF16),
            pltpu.VMEM((2, nx, n_rows, quarter), BF16),
            pltpu.SemaphoreType.DMA((9,)),
            sems(2, nx),
            sems(2, nyc),
            sems(2, nx, nyc),
            sems(2, 2, nyc),
            sems(2, 2, steps),
            sems(nyc),
            sems(nyc),
            sems(nx),
            sems(2, 2, steps),
            sems(2, nx),
        ],
        compiler_params=pltpu.CompilerParams(
            collective_id=0, has_side_effects=True, vmem_limit_bytes=56 * 1024 * 1024
        ),
    )(
        cite_count,
        *[a.reshape(1, -1) for a in lists],
        paper_feat,
        author_feat,
        cotangent,
        citation_weight_tiles,
        authorship_weight_tiles,
        w_self,
        w_cite,
        w_write,
    )


def solution(mesh):
    in_specs = (
        P("paper", "author"),
        P("paper", "author"),
        P("paper", None),
        P("paper"),
        P("paper"),
        P("paper"),
        P("paper"),
        P("paper", None, None),
        P("paper", None),
        P("paper"),
        P("paper"),
        P("paper"),
        P("paper", None, None),
        P(),
        P(),
        P(),
        P("paper", "author"),
    )
    out_specs = (P("paper", "author"), P("paper", "author"), P("paper", "author"))
    return jax.shard_map(
        functools.partial(body, mesh.shape["author"]),
        mesh=mesh,
        in_specs=in_specs,
        out_specs=out_specs,
        check_vma=False,
    )
```

```python
import functools

import jax
import jax.numpy as jnp
from jax import lax
from jax.experimental import pallas as pl
from jax.experimental.pallas import tpu as pltpu
from jax.sharding import PartitionSpec as P

MESH = pl.DeviceIdType.MESH
F32 = jnp.float32
BF16 = jnp.bfloat16
CORES = 2
UNROLL = 8


def dot(left, right):
    return jnp.dot(left, right, preferred_element_type=F32)


def dot_left_flipped(left, right):
    return lax.dot_general(left, right, (((0,), (0,)), ((), ())), preferred_element_type=F32)


def dot_right_flipped(left, right):
    return lax.dot_general(left, right, (((1,), (1,)), ((), ())), preferred_element_type=F32)


def kernel(
    nx,
    nyc,
    nz,
    cite_count,
    cite_owner,
    cite_source,
    cite_target,
    cite_edges,
    write_owner,
    write_author,
    write_paper,
    write_edges,
    paper,
    author,
    cot,
    cite_tiles_hbm,
    write_tiles_hbm,
    w_self,
    w_cite,
    w_write,
    paper_out,
    paper_grad,
    author_grad,
    cite_tiles,
    write_tiles,
    win,
    rows,
    feats,
    proj,
    meta_f,
    meta_i,
    slot_tab,
    slots,
    tiles,
    meta_fv,
    meta_iv,
    meta_fs,
    meta_is,
    acc,
    part_send,
    part_recv,
    pre,
    grads,
    grads_x,
    back_send,
    back_recv,
    sums,
    local_sem,
    feats_sem,
    meta_sem,
    tile_sem,
    share_sem,
    proj_sem,
    part_sem,
    grads_sem,
    grads_x_sem,
    back_sem,
    sums_sem,
):
    p = lax.axis_index("paper")
    x = lax.axis_index("author")
    z = p // nyc
    yc = p % nyc
    block = cite_tiles.shape[1]
    quarter = paper.shape[1]
    sent = []

    def send(src, dst, sems, index, device):
        copy = pltpu.make_async_remote_copy(
            src_ref=src,
            dst_ref=dst,
            send_sem=sems.at[(0,) + index],
            recv_sem=sems.at[(1,) + index],
            device_id=device,
            device_id_type=MESH,
        )
        copy.start()
        sent.append(copy)
        return copy

    def at_x(k):
        return (p, lax.rem(x + k + nx, nx))

    ny = nyc // CORES
    offsets = [(0, 1), (1, 1), (ny - 1, 1), (2, 1), (1, 0), (ny - 1, 0), (2, 0)]
    opposite = (0, 2, 1, 3, 5, 4, 6)
    n_off = len(offsets)

    def there(k):
        dy, dc = offsets[k]
        return lax.rem(yc // CORES + dy, ny) * CORES + lax.rem(yc + dc, CORES)

    def back_from(k):
        dy, dc = offsets[k]
        return lax.rem(yc // CORES + ny - dy, ny) * CORES + lax.rem(yc + dc, CORES)

    def at_yc(k):
        return (z * nyc + there(k), x)

    def at_z(k):
        return (lax.rem(z + k + nz, nz) * nyc + yc, x)

    def gather_x(buffer, sems, m, own):
        piece = buffer.at[m, x]
        copies = {}
        for k in (1, -1):
            if own is None:
                copies[k] = send(piece, piece, sems, (m, k % nx), at_x(k))
            else:
                copies[k] = send(own, piece, sems, (m, k % nx), at_x(k))
        return copies

    def chain_x(copies, buffer, sems, m):
        for b, onward in ((0, 1), (1, -1)):
            copies[onward].wait_recv()
            piece = buffer.at[m, lax.rem(x - onward + nx, nx), pl.ds(b * block, block)]
            copies[2 + b] = send(piece, piece, sems, (m, 2 * b), at_x(onward))

    def end_x(copies):
        for b in range(2):
            copies[2 + b].wait_recv()

    barrier = pltpu.get_barrier_semaphore()
    peers = [at_x(k) for k in range(1, nx)] + [at_yc(k) for k in range(n_off)] + [at_z(1), at_z(-1)]
    for device in peers:
        pl.semaphore_signal(barrier, inc=1, device_id=device, device_id_type=MESH)

    tile_loads = [
        pltpu.make_async_copy(cite_tiles_hbm, cite_tiles, local_sem.at[6]),
        pltpu.make_async_copy(write_tiles_hbm, write_tiles, local_sem.at[7]),
    ]
    columns = pl.ds(pl.multiple_of(x * quarter, quarter), quarter)
    loads = []
    for i, w in enumerate((w_cite, w_write, w_self)):
        loads.append(pltpu.make_async_copy(w.at[:, columns], win.at[i], local_sem.at[i]))
        loads.append(pltpu.make_async_copy(w.at[columns, :], rows.at[i], local_sem.at[3 + i]))
    for load in tile_loads + loads:
        load.start()

    n_slots = nyc * nz
    lanes = lax.broadcasted_iota(jnp.int32, (n_slots, 128), 1)
    table_f = jnp.zeros((n_slots, 128), F32)
    table_i = jnp.zeros((n_slots, 128), jnp.int32)
    lists = (
        (cite_owner, cite_source, cite_target, cite_edges),
        (write_owner, write_author, write_paper, write_edges),
    )
    for m, (owner, sources, targets, edges) in enumerate(lists):
        n = owner.shape[1]
        number = lax.broadcasted_iota(jnp.int32, (n_slots, n), 1)
        slot = lax.broadcasted_iota(jnp.int32, (n_slots, n), 0)
        named = owner[...] == (slot % nz) * nyc + slot // nz
        scale = 1.0 / edges[...].astype(F32)
        source = jnp.max(jnp.where(named, sources[...], 0), axis=1, keepdims=True)
        target = jnp.max(jnp.where(named, targets[...], 0), axis=1, keepdims=True)
        place = jnp.max(jnp.where(named, number, 0), axis=1, keepdims=True)
        live = named & (number < cite_count[0]) if m == 0 else named
        scale = jnp.sum(jnp.where(live, scale, 0.0), axis=1, keepdims=True)
        for kind, value in enumerate((source, target, place)):
            table_i = jnp.where(lanes == 4 * m + kind, value, table_i)
        for kind, (end, b) in enumerate(((target, 0), (target, 1), (source, 0), (source, 1))):
            table_f = jnp.where(lanes == 4 * m + kind, jnp.where(end == b, scale, 0.0), table_f)
    meta_f[...] = table_f.reshape(nyc, nz, 128)
    meta_i[...] = table_i.reshape(nyc, nz, 128)
    tab = pltpu.make_async_copy(meta_i, slot_tab, local_sem.at[8])
    tab.start()
    meta_fv[yc] = meta_f[yc]
    meta_iv[yc] = meta_i[yc]

    pl.semaphore_wait(barrier, len(peers))

    feats_x = gather_x(feats, feats_sem, 0, paper)
    meta_in = []
    for k in range(n_off):
        to = there(k)
        meta_in.append(send(meta_f.at[to], meta_fv.at[yc], meta_sem, (0, k), at_yc(k)))
        meta_in.append(send(meta_i.at[to], meta_iv.at[yc], meta_sem, (1, k), at_yc(k)))

    tab.wait()
    for load in tile_loads:
        load.wait()
    tiles_in = {}
    shared_in = {}

    def tiles_out(k):
        to = there(k)
        for m, source in enumerate((cite_tiles, write_tiles)):
            for j in range(nz):
                slots[m, to, j // 2, j % 2] = source[slot_tab[to, j, 4 * m + 2]]
            for half in range(nx if k == 0 else 2):
                q = lax.rem(x + half, nx)
                tiles_in[m, k, half] = send(
                    slots.at[m, to, q], tiles.at[m, yc, q], tile_sem, (m, half, k), at_yc(k)
                )

    def share_on(k):
        for m in range(2):
            for half in range(2):
                tiles_in[m, k, half].wait_recv()
                place_at = tiles.at[m, back_from(k), lax.rem(x + half, nx)]
                shared_in[m, k, half] = send(
                    place_at, place_at, share_sem, (m, half, k), at_x(1 if half == 0 else -1)
                )

    far = nz // 2
    turns = ((far, nz - 1 - far), (nz - 1 - far, far))
    ring = {}

    def pass_on(m, b, way, k):
        sign = 1 if way == 0 else -1
        piece = proj.at[m, lax.rem(z - sign * (k - 1) + nz, nz), b]
        ring[m, b, way, k] = send(piece, piece, proj_sem, (m, b, way, k), at_z(sign))

    def ring_step(m, k):
        for way in range(2):
            for b in range(2):
                if k <= turns[b][way]:
                    if k > 1:
                        ring[m, b, way, k - 1].wait_recv()
                    pass_on(m, b, way, k)

    def project(m, window):
        total = dot(feats[m, 0], win[window, 0:quarter, :])
        for i in range(1, nx):
            total += dot(feats[m, i], win[window, i * quarter : (i + 1) * quarter, :])
        return total

    def project_own(m):
        total = project(m, m).astype(BF16)
        proj[m, z, 0] = total[0:block]
        proj[m, z, 1] = total[block:]
        ring_step(m, 1)

    for k in range(3):
        tiles_out(k)
    chain_x(feats_x, feats, feats_sem, 0)
    feats_y = gather_x(feats, feats_sem, 1, author)
    tiles_out(3)
    feats[0, x] = paper[...]
    feats[1, x] = author[...]
    for load in loads:
        load.wait()
    end_x(feats_x)
    project_own(0)
    share_on(1)
    share_on(2)
    tiles_out(4)
    tiles_out(5)
    chain_x(feats_y, feats, feats_sem, 1)
    ring_step(0, 2)
    end_x(feats_y)
    project_own(1)
    share_on(3)
    tiles_out(6)
    ring_step(0, 3)
    pre[...] = project(0, 2)
    for m, source in enumerate((cite_tiles, write_tiles)):
        for j in range(nz):
            tiles[m, yc, j // 2, j % 2] = source[slot_tab[yc, j, 4 * m + 2]]
    ring_step(1, 2)
    share_on(4)
    share_on(5)
    ring_step(0, 4)
    ring_step(1, 3)
    share_on(6)
    ring_step(1, 4)
    for copy in meta_in:
        copy.wait_recv()
    small = [
        pltpu.make_async_copy(meta_fv, meta_fs, local_sem.at[6]),
        pltpu.make_async_copy(meta_iv, meta_is, local_sem.at[7]),
    ]
    for copy in small:
        copy.start()
    for copy in small:
        copy.wait()
    for m in range(2):
        for b in range(2):
            for way in range(2):
                ring[m, b, way, turns[b][way]].wait_recv()

    def share_of(target):
        acc[...] = jnp.zeros_like(acc)

        def step(i, carry):
            m = i // nz
            s = i % nz
            source = meta_is[target, s, 4 * m]
            product = dot(
                tiles[m, target, s // 2, s % 2],
                proj[m, s, source],
            )
            acc[0:block, :] += meta_fs[target, s, 4 * m] * product
            acc[block:, :] += meta_fs[target, s, 4 * m + 1] * product
            return carry

        lax.fori_loop(0, 2 * nz, step, 0, unroll=UNROLL)

    part_in = {}

    def share_from(k):
        for m in range(2):
            for half in range(nx if k == 0 else 2):
                (tiles_in if k == 0 else shared_in)[m, k, half].wait_recv()
        share_of(there(opposite[k]))

    def pass_part(slot, device):
        part_send[slot] = acc[...].astype(BF16)
        part_in[slot] = send(part_send.at[slot], part_recv.at[slot], part_sem, (slot,), device)

    for k in range(ny):
        share_from(k)
        pass_part(opposite[k], at_yc(0))
    for k in range(ny, n_off):
        share_from(k)
        part_in[opposite[k] - ny + 1].wait_recv()
        acc[...] += part_recv[opposite[k] - ny + 1].astype(F32)
        pass_part(opposite[k], at_yc(opposite[k]))
    share_of(yc)
    pre[...] += acc[...]
    for k in (0,) + tuple(range(ny, n_off)):
        part_in[k].wait_recv()
        pre[...] += part_recv[k].astype(F32)

    preact = pre[...]
    sigma = jax.nn.sigmoid(preact)
    paper_out[...] = (paper[...].astype(F32) + preact * sigma).astype(BF16)
    slope = sigma * (1.0 + preact * (1.0 - sigma))
    own = (cot[...].astype(F32) * slope).astype(BF16)
    grads[yc, 0] = own[0:block]
    grads[yc, 1] = own[block:]
    grads_x[x] = own
    grads_in = {k: send(grads.at[yc], grads.at[yc], grads_sem, (k,), at_yc(k)) for k in range(ny, n_off)}
    grads_in[0] = send(grads.at[yc], grads.at[yc], grads_sem, (0,), at_yc(0))
    grads_x_in = [send(grads_x.at[x], grads_x.at[x], grads_x_sem, (k,), at_x(k)) for k in range(1, nx)]
    for k in range(ny, n_off):
        grads_in[k].wait_recv()
        piece = grads.at[back_from(k)]
        grads_in[k - ny + 1] = send(piece, piece, grads_sem, (k - ny + 1,), at_yc(0))

    def back_of(m, place_z):
        acc[...] = jnp.zeros_like(acc)

        def step(i, carry):
            target = meta_is[i, place_z, 4 * m + 1]
            product = dot_left_flipped(
                tiles[m, i, place_z // 2, place_z % 2],
                grads[i, target],
            )
            acc[0:block, :] += meta_fs[i, place_z, 4 * m + 2] * product
            acc[block:, :] += meta_fs[i, place_z, 4 * m + 3] * product
            return carry

        lax.fori_loop(0, nyc, step, 0, unroll=UNROLL)

    for k in range(ny):
        grads_in[k].wait_recv()
    back = {}

    def back_on(m, b, way, distance):
        k = turns[b][way] - distance + 1
        total = acc[b * block : (b + 1) * block, :]
        if k > 1:
            back[m, b, way, k - 1].wait_recv()
            total += back_recv[m, b, way, k - 1].astype(F32)
        back_send[m, b, way, k] = total.astype(BF16)
        back[m, b, way, k] = send(
            back_send.at[m, b, way, k],
            back_recv.at[m, b, way, k],
            back_sem,
            (m, b, way, k),
            at_z(1 if way == 0 else -1),
        )

    for distance in range(far, 0, -1):
        for way in range(2):
            for m in range(2):
                if distance < far:
                    back_of(m, lax.rem(z + (distance if way == 0 else nz - distance), nz))
                    for b in (way, 1 - way):
                        back_on(m, b, way, distance)
                elif way == 0:
                    back_of(m, lax.rem(z + far, nz))
                    back_on(m, 0, 0, far)
                    back_on(m, 1, 1, far)

    for copy in grads_x_in:
        copy.wait_recv()
    total = cot[...].astype(F32)
    for i in range(nx):
        total += dot_right_flipped(grads_x[i], rows[2, :, i * quarter : (i + 1) * quarter])
    pre[...] = total
    sums_in = {}
    for m in range(2):
        back_of(m, z)
        for b in range(2):
            total = acc[b * block : (b + 1) * block, :]
            for way in range(2):
                back[m, b, way, turns[b][way]].wait_recv()
                total += back_recv[m, b, way, turns[b][way]].astype(F32)
            sums[m, x, pl.ds(b * block, block)] = total.astype(BF16)
        sums_in[m] = gather_x(sums, sums_sem, m, None)
    for m in range(2):
        chain_x(sums_in[m], sums, sums_sem, m)
    for m, out in enumerate((paper_grad, author_grad)):
        end_x(sums_in[m])
        total = dot_right_flipped(sums[m, 0], rows[m, :, 0:quarter])
        for i in range(1, nx):
            total += dot_right_flipped(sums[m, i], rows[m, :, i * quarter : (i + 1) * quarter])
        if m == 0:
            total += pre[...]
        out[...] = total.astype(BF16)
    for copy in sent:
        copy.wait_send()


def body(
    nx,
    paper_feat,
    author_feat,
    cite_owner,
    cite_source,
    cite_target,
    cite_edges,
    cite_count,
    citation_weight_tiles,
    write_owner,
    write_paper,
    write_author,
    write_edges,
    authorship_weight_tiles,
    w_self,
    w_cite,
    w_write,
    cotangent,
):
    nyc = 4 * CORES
    nz = lax.axis_size("paper") // nyc
    n_rows, quarter = paper_feat.shape
    block = citation_weight_tiles.shape[1]
    width = w_self.shape[0]

    lists = (
        cite_owner, cite_source, cite_target, cite_edges, write_owner, write_author, write_paper, write_edges
    )
    steps = nz // 2 + 1
    vmem = pl.BlockSpec(memory_space=pltpu.VMEM)
    hbm = pl.BlockSpec(memory_space=pl.ANY)
    unit = jax.ShapeDtypeStruct((n_rows, quarter), BF16)

    def sems(*shape):
        return pltpu.SemaphoreType.DMA((2,) + shape)

    results = pl.pallas_call(
        functools.partial(kernel, nx, nyc, nz),
        out_shape=(unit, unit, unit),
        in_specs=[pl.BlockSpec(memory_space=pltpu.SMEM)] + [vmem] * 11 + [hbm] * 5,
        out_specs=(vmem, vmem, vmem),
        scratch_shapes=[
            pltpu.VMEM(citation_weight_tiles.shape, BF16),
            pltpu.VMEM(authorship_weight_tiles.shape, BF16),
            pltpu.VMEM((3, width, quarter), BF16),
            pltpu.VMEM((3, quarter, width), BF16),
            pltpu.VMEM((2, nx, n_rows, quarter), BF16),
            pltpu.VMEM((2, nz, 2, block, quarter), BF16),
            pltpu.VMEM((nyc, nz, 128), F32),
            pltpu.VMEM((nyc, nz, 128), jnp.int32),
            pltpu.SMEM((nyc, nz, 128), jnp.int32),
            pltpu.VMEM((2, nyc, nz // 2, 2, block, block), BF16),
            pltpu.VMEM((2, nyc, nz // 2, 2, block, block), BF16),
            pltpu.VMEM((nyc, nz, 128), F32),
            pltpu.VMEM((nyc, nz, 128), jnp.int32),
            pltpu.SMEM((nyc, nz, 128), F32),
            pltpu.SMEM((nyc, nz, 128), jnp.int32),
            pltpu.VMEM((n_rows, quarter), F32),
            pltpu.VMEM((nyc, n_rows, quarter), BF16),
            pltpu.VMEM((nyc, n_rows, quarter), BF16),
            pltpu.VMEM((n_rows, quarter), F32),
            pltpu.VMEM((nyc, 2, block, quarter), BF16),
            pltpu.VMEM((nx, n_rows, quarter), BF16),
            pltpu.VMEM((2, 2, 2, steps, block, quarter), BF16),
            pltpu.VMEM((2, 2, 2, steps, block, quarter), BF16),
            pltpu.VMEM((2, nx, n_rows, quarter), BF16),
            pltpu.SemaphoreType.DMA((9,)),
            sems(2, nx),
            sems(2, nyc),
            sems(2, nx, nyc),
            sems(2, 2, nyc),
            sems(2, 2, 2, steps),
            sems(nyc),
            sems(nyc),
            sems(nx),
            sems(2, 2, 2, steps),
            sems(2, nx),
        ],
        compiler_params=pltpu.CompilerParams(
            collective_id=0, has_side_effects=True, vmem_limit_bytes=56 * 1024 * 1024
        ),
    )(
        cite_count,
        *[a.reshape(1, -1) for a in lists],
        paper_feat,
        author_feat,
        cotangent,
        citation_weight_tiles,
        authorship_weight_tiles,
        w_self,
        w_cite,
        w_write,
    )
    return pl.pallas_call(
        hand_over,
        out_shape=(unit, unit, unit),
        in_specs=[hbm] * 3,
        out_specs=(hbm, hbm, hbm),
        scratch_shapes=[pltpu.SemaphoreType.DMA((3,))],
    )(*results)


def hand_over(*refs):
    copies = [pltpu.make_async_copy(refs[i], refs[3 + i], refs[6].at[i]) for i in range(3)]
    for copy in copies:
        copy.start()
    for copy in copies:
        copy.wait()


def solution(mesh):
    in_specs = (
        P("paper", "author"),
        P("paper", "author"),
        P("paper", None),
        P("paper"),
        P("paper"),
        P("paper"),
        P("paper"),
        P("paper", None, None),
        P("paper", None),
        P("paper"),
        P("paper"),
        P("paper"),
        P("paper", None, None),
        P(),
        P(),
        P(),
        P("paper", "author"),
    )
    out_specs = (P("paper", "author"), P("paper", "author"), P("paper", "author"))
    return jax.shard_map(
        functools.partial(body, mesh.shape["author"]),
        mesh=mesh,
        in_specs=in_specs,
        out_specs=out_specs,
        check_vma=False,
    )
```

```python
import functools

import jax
import jax.numpy as jnp
from jax import lax
from jax.experimental import pallas as pl
from jax.experimental.pallas import tpu as pltpu
from jax.sharding import PartitionSpec as P

MESH = pl.DeviceIdType.MESH
F32 = jnp.float32
BF16 = jnp.bfloat16
CORES = 2
UNROLL = 8


def dot(left, right):
    return jnp.dot(left, right, preferred_element_type=F32)


def dot_left_flipped(left, right):
    return lax.dot_general(left, right, (((0,), (0,)), ((), ())), preferred_element_type=F32)


def dot_right_flipped(left, right):
    return lax.dot_general(left, right, (((1,), (1,)), ((), ())), preferred_element_type=F32)


def kernel(
    nx,
    nyc,
    nz,
    cite_count,
    cite_owner_hbm,
    cite_source_hbm,
    cite_target_hbm,
    cite_edges_hbm,
    write_owner_hbm,
    write_author_hbm,
    write_paper_hbm,
    write_edges_hbm,
    paper_hbm,
    author_hbm,
    cot_hbm,
    cite_tiles_hbm,
    write_tiles_hbm,
    w_self,
    w_cite,
    w_write,
    paper_out_hbm,
    paper_grad_hbm,
    author_grad_hbm,
    cite_lists,
    write_lists,
    cot,
    outs,
    cite_tiles,
    write_tiles,
    win,
    rows,
    feats,
    proj,
    meta_f,
    meta_i,
    slot_tab,
    slots,
    tiles,
    meta_fv,
    meta_iv,
    meta_fs,
    meta_is,
    acc,
    part_send,
    part_recv,
    pre,
    grads,
    grads_x,
    back_send,
    back_recv,
    sums,
    local_sem,
    feats_sem,
    meta_sem,
    tile_sem,
    share_sem,
    proj_sem,
    part_sem,
    grads_sem,
    grads_x_sem,
    back_sem,
    sums_sem,
):
    p = lax.axis_index("paper")
    x = lax.axis_index("author")
    z = p // nyc
    yc = p % nyc
    block = cite_tiles_hbm.shape[1]
    quarter = paper_hbm.shape[1]
    sent = []

    def send(src, dst, sems, index, device):
        copy = pltpu.make_async_remote_copy(
            src_ref=src,
            dst_ref=dst,
            send_sem=sems.at[(0,) + index],
            recv_sem=sems.at[(1,) + index],
            device_id=device,
            device_id_type=MESH,
        )
        copy.start()
        sent.append(copy)
        return copy

    def at_x(k):
        return (p, lax.rem(x + k + nx, nx))

    ny = nyc // CORES
    offsets = [(0, 1), (1, 1), (ny - 1, 1), (2, 1), (1, 0), (ny - 1, 0), (2, 0)]
    opposite = (0, 2, 1, 3, 5, 4, 6)
    n_off = len(offsets)

    def there(k):
        dy, dc = offsets[k]
        return lax.rem(yc // CORES + dy, ny) * CORES + lax.rem(yc + dc, CORES)

    def back_from(k):
        dy, dc = offsets[k]
        return lax.rem(yc // CORES + ny - dy, ny) * CORES + lax.rem(yc + dc, CORES)

    def at_yc(k):
        return (z * nyc + there(k), x)

    def at_z(k):
        return (lax.rem(z + k + nz, nz) * nyc + yc, x)

    def gather_x(buffer, sems, m):
        piece = buffer.at[m, x]
        return {k: send(piece, piece, sems, (m, k % nx), at_x(k)) for k in (1, -1)}

    def chain_x(copies, buffer, sems, m):
        for b, onward in ((0, 1), (1, -1)):
            copies[onward].wait_recv()
            piece = buffer.at[m, lax.rem(x - onward + nx, nx), pl.ds(b * block, block)]
            copies[2 + b] = send(piece, piece, sems, (m, 2 * b), at_x(onward))

    def end_x(copies):
        for b in range(2):
            copies[2 + b].wait_recv()

    barrier = pltpu.get_barrier_semaphore()
    peers = [at_x(k) for k in range(1, nx)] + [at_yc(k) for k in range(n_off)] + [at_z(1), at_z(-1)]
    for device in peers:
        pl.semaphore_signal(barrier, inc=1, device_id=device, device_id_type=MESH)

    paper, author = feats.at[0, x], feats.at[1, x]
    own_loads = [
        pltpu.make_async_copy(paper_hbm, paper, local_sem.at[9]),
        pltpu.make_async_copy(author_hbm, author, local_sem.at[10]),
        pltpu.make_async_copy(cot_hbm, cot, local_sem.at[11]),
    ]
    list_loads = [
        pltpu.make_async_copy(source, into.at[i], local_sem.at[12 + 4 * m + i])
        for m, into, sources in (
            (0, cite_lists, (cite_owner_hbm, cite_source_hbm, cite_target_hbm, cite_edges_hbm)),
            (1, write_lists, (write_owner_hbm, write_author_hbm, write_paper_hbm, write_edges_hbm)),
        )
        for i, source in enumerate(sources)
    ]
    tile_loads = [
        pltpu.make_async_copy(cite_tiles_hbm, cite_tiles, local_sem.at[6]),
        pltpu.make_async_copy(write_tiles_hbm, write_tiles, local_sem.at[7]),
    ]
    columns = pl.ds(pl.multiple_of(x * quarter, quarter), quarter)
    loads = []
    for i, w in enumerate((w_cite, w_write, w_self)):
        loads.append(pltpu.make_async_copy(w.at[:, columns], win.at[i], local_sem.at[i]))
        loads.append(pltpu.make_async_copy(w.at[columns, :], rows.at[i], local_sem.at[3 + i]))
    for load in list_loads + own_loads + tile_loads + loads:
        load.start()
    for load in list_loads:
        load.wait()

    n_slots = nyc * nz
    lanes = lax.broadcasted_iota(jnp.int32, (n_slots, 128), 1)
    table_f = jnp.zeros((n_slots, 128), F32)
    table_i = jnp.zeros((n_slots, 128), jnp.int32)
    for m, lists in enumerate((cite_lists, write_lists)):
        owner, sources, targets, edges = lists[0], lists[1], lists[2], lists[3]
        n = lists.shape[2]
        number = lax.broadcasted_iota(jnp.int32, (n_slots, n), 1)
        slot = lax.broadcasted_iota(jnp.int32, (n_slots, n), 0)
        named = owner == (slot % nz) * nyc + slot // nz
        scale = 1.0 / edges.astype(F32)
        source = jnp.max(jnp.where(named, sources, 0), axis=1, keepdims=True)
        target = jnp.max(jnp.where(named, targets, 0), axis=1, keepdims=True)
        place = jnp.max(jnp.where(named, number, 0), axis=1, keepdims=True)
        live = named & (number < cite_count[0]) if m == 0 else named
        scale = jnp.sum(jnp.where(live, scale, 0.0), axis=1, keepdims=True)
        for kind, value in enumerate((source, target, place)):
            table_i = jnp.where(lanes == 4 * m + kind, value, table_i)
        for kind, (end, b) in enumerate(((target, 0), (target, 1), (source, 0), (source, 1))):
            table_f = jnp.where(lanes == 4 * m + kind, jnp.where(end == b, scale, 0.0), table_f)
    meta_f[...] = table_f.reshape(nyc, nz, 128)
    meta_i[...] = table_i.reshape(nyc, nz, 128)
    tab = pltpu.make_async_copy(meta_i, slot_tab, local_sem.at[8])
    tab.start()
    meta_fv[yc] = meta_f[yc]
    meta_iv[yc] = meta_i[yc]

    pl.semaphore_wait(barrier, len(peers))

    for load in own_loads:
        load.wait()
    feats_x = gather_x(feats, feats_sem, 0)
    feats_y = gather_x(feats, feats_sem, 1)
    meta_in = []
    for k in range(n_off):
        to = there(k)
        meta_in.append(send(meta_f.at[to], meta_fv.at[yc], meta_sem, (0, k), at_yc(k)))
        meta_in.append(send(meta_i.at[to], meta_iv.at[yc], meta_sem, (1, k), at_yc(k)))

    tab.wait()
    for load in tile_loads:
        load.wait()
    tiles_in = {}
    shared_in = {}

    def tiles_out(k):
        to = there(k)
        for m, source in enumerate((cite_tiles, write_tiles)):
            for j in range(nz):
                slots[m, to, j // 2, j % 2] = source[slot_tab[to, j, 4 * m + 2]]
            for half in range(nx if k == 0 else 2):
                q = lax.rem(x + half, nx)
                tiles_in[m, k, half] = send(
                    slots.at[m, to, q], tiles.at[m, yc, q], tile_sem, (m, half, k), at_yc(k)
                )

    def share_on(k):
        for m in range(2):
            for half in range(2):
                tiles_in[m, k, half].wait_recv()
                place_at = tiles.at[m, back_from(k), lax.rem(x + half, nx)]
                shared_in[m, k, half] = send(
                    place_at, place_at, share_sem, (m, half, k), at_x(1 if half == 0 else -1)
                )

    far = nz // 2
    turns = ((far, nz - 1 - far), (nz - 1 - far, far))
    ring = {}

    def pass_on(m, b, way, k):
        sign = 1 if way == 0 else -1
        piece = proj.at[m, lax.rem(z - sign * (k - 1) + nz, nz), b]
        ring[m, b, way, k] = send(piece, piece, proj_sem, (m, b, way, k), at_z(sign))

    def ring_step(m, k):
        for way in range(2):
            for b in range(2):
                if k <= turns[b][way]:
                    if k > 1:
                        ring[m, b, way, k - 1].wait_recv()
                    pass_on(m, b, way, k)

    def project(m, window):
        total = dot(feats[m, 0], win[window, 0:quarter, :])
        for i in range(1, nx):
            total += dot(feats[m, i], win[window, i * quarter : (i + 1) * quarter, :])
        return total

    def project_own(m):
        total = project(m, m).astype(BF16)
        proj[m, z, 0] = total[0:block]
        proj[m, z, 1] = total[block:]
        ring_step(m, 1)

    for k in range(3):
        tiles_out(k)
    chain_x(feats_x, feats, feats_sem, 0)
    tiles_out(3)
    chain_x(feats_y, feats, feats_sem, 1)
    tiles_out(4)
    for load in loads:
        load.wait()
    end_x(feats_x)
    project_own(0)
    tiles_out(5)
    end_x(feats_y)
    project_own(1)
    tiles_out(6)
    share_on(1)
    share_on(2)
    ring_step(0, 2)
    ring_step(1, 2)
    share_on(3)
    pre[...] = project(0, 2)
    for m, source in enumerate((cite_tiles, write_tiles)):
        for j in range(nz):
            tiles[m, yc, j // 2, j % 2] = source[slot_tab[yc, j, 4 * m + 2]]
    ring_step(0, 3)
    ring_step(1, 3)
    share_on(4)
    share_on(5)
    ring_step(0, 4)
    ring_step(1, 4)
    share_on(6)
    for copy in meta_in:
        copy.wait_recv()
    small = [
        pltpu.make_async_copy(meta_fv, meta_fs, local_sem.at[6]),
        pltpu.make_async_copy(meta_iv, meta_is, local_sem.at[7]),
    ]
    for copy in small:
        copy.start()
    for copy in small:
        copy.wait()
    for m in range(2):
        for b in range(2):
            for way in range(2):
                ring[m, b, way, turns[b][way]].wait_recv()

    def share_of(target):
        acc[...] = jnp.zeros_like(acc)

        def step(i, carry):
            m = i // nz
            s = i % nz
            source = meta_is[target, s, 4 * m]
            product = dot(
                tiles[m, target, s // 2, s % 2],
                proj[m, s, source],
            )
            acc[0:block, :] += meta_fs[target, s, 4 * m] * product
            acc[block:, :] += meta_fs[target, s, 4 * m + 1] * product
            return carry

        lax.fori_loop(0, 2 * nz, step, 0, unroll=UNROLL)

    part_in = {}

    def share_from(k):
        for m in range(2):
            for half in range(nx if k == 0 else 2):
                (tiles_in if k == 0 else shared_in)[m, k, half].wait_recv()
        share_of(there(opposite[k]))

    def pass_part(slot, device):
        part_send[slot] = acc[...].astype(BF16)
        part_in[slot] = send(part_send.at[slot], part_recv.at[slot], part_sem, (slot,), device)

    for k in range(ny):
        share_from(k)
        pass_part(opposite[k], at_yc(0))
    for k in range(ny, n_off):
        share_from(k)
        part_in[opposite[k] - ny + 1].wait_recv()
        acc[...] += part_recv[opposite[k] - ny + 1].astype(F32)
        pass_part(opposite[k], at_yc(opposite[k]))
    share_of(yc)
    pre[...] += acc[...]
    for k in (0,) + tuple(range(ny, n_off)):
        part_in[k].wait_recv()
        pre[...] += part_recv[k].astype(F32)

    preact = pre[...]
    sigma = jax.nn.sigmoid(preact)
    outs[0] = (paper[...].astype(F32) + preact * sigma).astype(BF16)
    slope = sigma * (1.0 + preact * (1.0 - sigma))
    own = (cot[...].astype(F32) * slope).astype(BF16)
    grads[yc, 0] = own[0:block]
    grads[yc, 1] = own[block:]
    grads_x[x] = own
    grads_in = {k: send(grads.at[yc], grads.at[yc], grads_sem, (k,), at_yc(k)) for k in range(ny, n_off)}
    grads_in[0] = send(grads.at[yc], grads.at[yc], grads_sem, (0,), at_yc(0))
    grads_x_in = [send(grads_x.at[x], grads_x.at[x], grads_x_sem, (k,), at_x(k)) for k in range(1, nx)]
    for k in range(ny, n_off):
        grads_in[k].wait_recv()
        piece = grads.at[back_from(k)]
        grads_in[k - ny + 1] = send(piece, piece, grads_sem, (k - ny + 1,), at_yc(0))

    def back_of(m, place_z):
        acc[...] = jnp.zeros_like(acc)

        def step(i, carry):
            target = meta_is[i, place_z, 4 * m + 1]
            product = dot_left_flipped(
                tiles[m, i, place_z // 2, place_z % 2],
                grads[i, target],
            )
            acc[0:block, :] += meta_fs[i, place_z, 4 * m + 2] * product
            acc[block:, :] += meta_fs[i, place_z, 4 * m + 3] * product
            return carry

        lax.fori_loop(0, nyc, step, 0, unroll=UNROLL)

    for k in range(ny):
        grads_in[k].wait_recv()
    back = {}

    def back_on(m, b, way, distance):
        k = turns[b][way] - distance + 1
        total = acc[b * block : (b + 1) * block, :]
        if k > 1:
            back[m, b, way, k - 1].wait_recv()
            total += back_recv[m, b, way, k - 1].astype(F32)
        back_send[m, b, way, k] = total.astype(BF16)
        back[m, b, way, k] = send(
            back_send.at[m, b, way, k],
            back_recv.at[m, b, way, k],
            back_sem,
            (m, b, way, k),
            at_z(1 if way == 0 else -1),
        )

    for distance in range(far, 0, -1):
        for way in range(2):
            for m in range(2):
                if distance < far:
                    back_of(m, lax.rem(z + (distance if way == 0 else nz - distance), nz))
                    for b in (way, 1 - way):
                        back_on(m, b, way, distance)
                elif way == 0:
                    back_of(m, lax.rem(z + far, nz))
                    back_on(m, 0, 0, far)
                    back_on(m, 1, 1, far)

    for copy in grads_x_in:
        copy.wait_recv()
    total = cot[...].astype(F32)
    for i in range(nx):
        total += dot_right_flipped(grads_x[i], rows[2, :, i * quarter : (i + 1) * quarter])
    pre[...] = total
    sums_in = {}
    for m in range(2):
        back_of(m, z)
        for b in range(2):
            total = acc[b * block : (b + 1) * block, :]
            for way in range(2):
                back[m, b, way, turns[b][way]].wait_recv()
                total += back_recv[m, b, way, turns[b][way]].astype(F32)
            sums[m, x, pl.ds(b * block, block)] = total.astype(BF16)
        sums_in[m] = gather_x(sums, sums_sem, m)
    for m in range(2):
        chain_x(sums_in[m], sums, sums_sem, m)
    stores = [
        pltpu.make_async_copy(outs.at[i], out, local_sem.at[i])
        for i, out in enumerate((paper_out_hbm, paper_grad_hbm, author_grad_hbm))
    ]
    stores[0].start()
    for m in range(2):
        end_x(sums_in[m])
        total = dot_right_flipped(sums[m, 0], rows[m, :, 0:quarter])
        for i in range(1, nx):
            total += dot_right_flipped(sums[m, i], rows[m, :, i * quarter : (i + 1) * quarter])
        if m == 0:
            total += pre[...]
        outs[1 + m] = total.astype(BF16)
        stores[1 + m].start()
    for copy in sent:
        copy.wait_send()
    for store in stores:
        store.wait()


def body(
    nx,
    paper_feat,
    author_feat,
    cite_owner,
    cite_source,
    cite_target,
    cite_edges,
    cite_count,
    citation_weight_tiles,
    write_owner,
    write_paper,
    write_author,
    write_edges,
    authorship_weight_tiles,
    w_self,
    w_cite,
    w_write,
    cotangent,
):
    nyc = 4 * CORES
    nz = lax.axis_size("paper") // nyc
    n_rows, quarter = paper_feat.shape
    block = citation_weight_tiles.shape[1]
    width = w_self.shape[0]

    lists = (
        cite_owner, cite_source, cite_target, cite_edges, write_owner, write_author, write_paper, write_edges
    )
    steps = nz // 2 + 1
    hbm = pl.BlockSpec(memory_space=pl.ANY)
    unit = jax.ShapeDtypeStruct((n_rows, quarter), BF16)

    def sems(*shape):
        return pltpu.SemaphoreType.DMA((2,) + shape)

    results = pl.pallas_call(
        functools.partial(kernel, nx, nyc, nz),
        out_shape=(unit, unit, unit),
        in_specs=[pl.BlockSpec(memory_space=pltpu.SMEM)] + [hbm] * 16,
        out_specs=(hbm, hbm, hbm),
        scratch_shapes=[
            pltpu.VMEM((4, 1, cite_edges.shape[0]), jnp.int32),
            pltpu.VMEM((4, 1, write_edges.shape[0]), jnp.int32),
            pltpu.VMEM((n_rows, quarter), BF16),
            pltpu.VMEM((3, n_rows, quarter), BF16),
            pltpu.VMEM(citation_weight_tiles.shape, BF16),
            pltpu.VMEM(authorship_weight_tiles.shape, BF16),
            pltpu.VMEM((3, width, quarter), BF16),
            pltpu.VMEM((3, quarter, width), BF16),
            pltpu.VMEM((2, nx, n_rows, quarter), BF16),
            pltpu.VMEM((2, nz, 2, block, quarter), BF16),
            pltpu.VMEM((nyc, nz, 128), F32),
            pltpu.VMEM((nyc, nz, 128), jnp.int32),
            pltpu.SMEM((nyc, nz, 128), jnp.int32),
            pltpu.VMEM((2, nyc, nz // 2, 2, block, block), BF16),
            pltpu.VMEM((2, nyc, nz // 2, 2, block, block), BF16),
            pltpu.VMEM((nyc, nz, 128), F32),
            pltpu.VMEM((nyc, nz, 128), jnp.int32),
            pltpu.SMEM((nyc, nz, 128), F32),
            pltpu.SMEM((nyc, nz, 128), jnp.int32),
            pltpu.VMEM((n_rows, quarter), F32),
            pltpu.VMEM((nyc, n_rows, quarter), BF16),
            pltpu.VMEM((nyc, n_rows, quarter), BF16),
            pltpu.VMEM((n_rows, quarter), F32),
            pltpu.VMEM((nyc, 2, block, quarter), BF16),
            pltpu.VMEM((nx, n_rows, quarter), BF16),
            pltpu.VMEM((2, 2, 2, steps, block, quarter), BF16),
            pltpu.VMEM((2, 2, 2, steps, block, quarter), BF16),
            pltpu.VMEM((2, nx, n_rows, quarter), BF16),
            pltpu.SemaphoreType.DMA((20,)),
            sems(2, nx),
            sems(2, nyc),
            sems(2, nx, nyc),
            sems(2, 2, nyc),
            sems(2, 2, 2, steps),
            sems(nyc),
            sems(nyc),
            sems(nx),
            sems(2, 2, 2, steps),
            sems(2, nx),
        ],
        compiler_params=pltpu.CompilerParams(
            collective_id=0, has_side_effects=True, vmem_limit_bytes=56 * 1024 * 1024
        ),
    )(
        cite_count,
        *[a.reshape(1, -1) for a in lists],
        paper_feat,
        author_feat,
        cotangent,
        citation_weight_tiles,
        authorship_weight_tiles,
        w_self,
        w_cite,
        w_write,
    )
    return pl.pallas_call(
        hand_over,
        out_shape=(unit, unit, unit),
        in_specs=[hbm] * 3,
        out_specs=(hbm, hbm, hbm),
        scratch_shapes=[
            pltpu.VMEM((3, n_rows, quarter), BF16),
            pltpu.SemaphoreType.DMA((2, 3)),
        ],
    )(*results)


def hand_over(*refs):
    sources, results, (held, sems) = refs[:3], refs[3:6], refs[6:]
    ins = [pltpu.make_async_copy(sources[i], held.at[i], sems.at[0, i]) for i in range(3)]
    ends = [pltpu.make_async_copy(held.at[i], results[i], sems.at[1, i]) for i in range(3)]
    for copy in ins:
        copy.start()
    for i in range(3):
        ins[i].wait()
        ends[i].start()
    for copy in ends:
        copy.wait()


def solution(mesh):
    in_specs = (
        P("paper", "author"),
        P("paper", "author"),
        P("paper", None),
        P("paper"),
        P("paper"),
        P("paper"),
        P("paper"),
        P("paper", None, None),
        P("paper", None),
        P("paper"),
        P("paper"),
        P("paper"),
        P("paper", None, None),
        P(),
        P(),
        P(),
        P("paper", "author"),
    )
    out_specs = (P("paper", "author"), P("paper", "author"), P("paper", "author"))
    return jax.shard_map(
        functools.partial(body, mesh.shape["author"]),
        mesh=mesh,
        in_specs=in_specs,
        out_specs=out_specs,
        check_vma=False,
    )
```

```python
import functools

import jax
import jax.numpy as jnp
from jax import lax
from jax.experimental import pallas as pl
from jax.experimental.pallas import tpu as pltpu
from jax.sharding import PartitionSpec as P

MESH = pl.DeviceIdType.MESH
F32 = jnp.float32
BF16 = jnp.bfloat16
CORES = 2
UNROLL = 8


def dot(left, right):
    return jnp.dot(left, right, preferred_element_type=F32)


def dot_left_flipped(left, right):
    return lax.dot_general(left, right, (((0,), (0,)), ((), ())), preferred_element_type=F32)


def dot_right_flipped(left, right):
    return lax.dot_general(left, right, (((1,), (1,)), ((), ())), preferred_element_type=F32)


def kernel(
    nx,
    nyc,
    nz,
    cite_count,
    cite_owner_hbm,
    cite_source_hbm,
    cite_target_hbm,
    cite_edges_hbm,
    write_owner_hbm,
    write_author_hbm,
    write_paper_hbm,
    write_edges_hbm,
    paper_hbm,
    author_hbm,
    cot_hbm,
    cite_tiles_hbm,
    write_tiles_hbm,
    w_self,
    w_cite,
    w_write,
    paper_out_hbm,
    paper_grad_hbm,
    author_grad_hbm,
    cite_lists,
    write_lists,
    cot,
    outs,
    cite_tiles,
    write_tiles,
    win,
    rows,
    feats,
    proj,
    meta_f,
    meta_i,
    slot_tab,
    slots,
    tiles,
    meta_fv,
    meta_iv,
    meta_fs,
    meta_is,
    acc,
    part_send,
    part_recv,
    pre,
    grads_left,
    grads_right,
    grads_x,
    back_send,
    back_recv,
    back_acc,
    sums,
    local_sem,
    feats_sem,
    meta_sem,
    tile_sem,
    share_sem,
    proj_sem,
    part_sem,
    grads_sem,
    grads_x_sem,
    back_sem,
    sums_sem,
):
    p = lax.axis_index("paper")
    x = lax.axis_index("author")
    z = p // nyc
    yc = p % nyc
    block = cite_tiles_hbm.shape[1]
    quarter = paper_hbm.shape[1]
    sent = []

    def send(src, dst, sems, index, device):
        copy = pltpu.make_async_remote_copy(
            src_ref=src,
            dst_ref=dst,
            send_sem=sems.at[(0,) + index],
            recv_sem=sems.at[(1,) + index],
            device_id=device,
            device_id_type=MESH,
        )
        copy.start()
        sent.append(copy)
        return copy

    def at_x(k):
        return (p, lax.rem(x + k + nx, nx))

    ny = nyc // CORES
    offsets = [(0, 1), (1, 1), (ny - 1, 1), (2, 1), (1, 0), (ny - 1, 0), (2, 0)]
    opposite = (0, 2, 1, 3, 5, 4, 6)
    n_off = len(offsets)

    def there(k):
        dy, dc = offsets[k]
        return lax.rem(yc // CORES + dy, ny) * CORES + lax.rem(yc + dc, CORES)

    def back_from(k):
        dy, dc = offsets[k]
        return lax.rem(yc // CORES + ny - dy, ny) * CORES + lax.rem(yc + dc, CORES)

    def at_yc(k):
        return (z * nyc + there(k), x)

    def at_z(k):
        return (lax.rem(z + k + nz, nz) * nyc + yc, x)

    def gather_x(buffer, sems, *at):
        piece = buffer.at[at + (x,)]
        return {k: send(piece, piece, sems, at + (k % nx,), at_x(k)) for k in (1, -1)}

    def chain_x(copies, buffer, sems, *at):
        for b, onward in ((0, 1), (1, -1)):
            copies[onward].wait_recv()
            piece = buffer.at[at + (lax.rem(x - onward + nx, nx), pl.ds(b * block, block))]
            copies[2 + b] = send(piece, piece, sems, at + (2 * b,), at_x(onward))

    def end_x(copies):
        for b in range(2):
            copies[2 + b].wait_recv()

    barrier = pltpu.get_barrier_semaphore()
    peers = [at_x(k) for k in range(1, nx)] + [at_yc(k) for k in range(n_off)] + [at_z(1), at_z(-1)]
    for device in peers:
        pl.semaphore_signal(barrier, inc=1, device_id=device, device_id_type=MESH)

    paper, author = feats.at[0, x], feats.at[1, x]
    own_loads = [
        pltpu.make_async_copy(paper_hbm, paper, local_sem.at[9]),
        pltpu.make_async_copy(author_hbm, author, local_sem.at[10]),
        pltpu.make_async_copy(cot_hbm, cot, local_sem.at[11]),
    ]
    list_loads = [
        pltpu.make_async_copy(source, into.at[i], local_sem.at[12 + 4 * m + i])
        for m, into, sources in (
            (0, cite_lists, (cite_owner_hbm, cite_source_hbm, cite_target_hbm, cite_edges_hbm)),
            (1, write_lists, (write_owner_hbm, write_author_hbm, write_paper_hbm, write_edges_hbm)),
        )
        for i, source in enumerate(sources)
    ]
    tile_loads = [
        pltpu.make_async_copy(cite_tiles_hbm, cite_tiles, local_sem.at[6]),
        pltpu.make_async_copy(write_tiles_hbm, write_tiles, local_sem.at[7]),
    ]
    columns = pl.ds(pl.multiple_of(x * quarter, quarter), quarter)
    loads = []
    for i, w in enumerate((w_cite, w_write, w_self)):
        loads.append(pltpu.make_async_copy(w.at[:, columns], win.at[i], local_sem.at[i]))
        loads.append(pltpu.make_async_copy(w.at[columns, :], rows.at[i], local_sem.at[3 + i]))
    for load in list_loads + own_loads + tile_loads + loads:
        load.start()
    for load in list_loads:
        load.wait()

    n_slots = nyc * nz
    lanes = lax.broadcasted_iota(jnp.int32, (n_slots, 128), 1)
    table_f = jnp.zeros((n_slots, 128), F32)
    table_i = jnp.zeros((n_slots, 128), jnp.int32)
    for m, lists in enumerate((cite_lists, write_lists)):
        owner, sources, targets, edges = lists[0], lists[1], lists[2], lists[3]
        n = lists.shape[2]
        number = lax.broadcasted_iota(jnp.int32, (n_slots, n), 1)
        slot = lax.broadcasted_iota(jnp.int32, (n_slots, n), 0)
        named = owner == (slot % nz) * nyc + slot // nz
        scale = 1.0 / edges.astype(F32)
        source = jnp.max(jnp.where(named, sources, 0), axis=1, keepdims=True)
        target = jnp.max(jnp.where(named, targets, 0), axis=1, keepdims=True)
        place = jnp.max(jnp.where(named, number, 0), axis=1, keepdims=True)
        live = named & (number < cite_count[0]) if m == 0 else named
        scale = jnp.sum(jnp.where(live, scale, 0.0), axis=1, keepdims=True)
        for kind, value in enumerate((source, target, place)):
            table_i = jnp.where(lanes == 4 * m + kind, value, table_i)
        for kind, (end, b) in enumerate(((target, 0), (target, 1), (source, 0), (source, 1))):
            table_f = jnp.where(lanes == 4 * m + kind, jnp.where(end == b, scale, 0.0), table_f)
    meta_f[...] = table_f.reshape(nyc, nz, 128)
    meta_i[...] = table_i.reshape(nyc, nz, 128)
    tab = pltpu.make_async_copy(meta_i, slot_tab, local_sem.at[8])
    tab.start()
    meta_fv[yc] = meta_f[yc]
    meta_iv[yc] = meta_i[yc]

    pl.semaphore_wait(barrier, len(peers))

    for load in own_loads:
        load.wait()
    feats_x = gather_x(feats, feats_sem, 0)
    feats_y = gather_x(feats, feats_sem, 1)
    meta_in = []
    for k in range(n_off):
        to = there(k)
        meta_in.append(send(meta_f.at[to], meta_fv.at[yc], meta_sem, (0, k), at_yc(k)))
        meta_in.append(send(meta_i.at[to], meta_iv.at[yc], meta_sem, (1, k), at_yc(k)))

    tab.wait()
    for load in tile_loads:
        load.wait()
    tiles_in = {}
    shared_in = {}

    def tiles_out(k):
        to = there(k)
        for m, source in enumerate((cite_tiles, write_tiles)):
            for j in range(nz):
                slots[m, to, j // 2, j % 2] = source[slot_tab[to, j, 4 * m + 2]]
            for half in range(nx if k == 0 else 2):
                q = lax.rem(x + half, nx)
                tiles_in[m, k, half] = send(
                    slots.at[m, to, q], tiles.at[m, yc, q], tile_sem, (m, half, k), at_yc(k)
                )

    def share_on(k):
        for m in range(2):
            for half in range(2):
                tiles_in[m, k, half].wait_recv()
                place_at = tiles.at[m, back_from(k), lax.rem(x + half, nx)]
                shared_in[m, k, half] = send(
                    place_at, place_at, share_sem, (m, half, k), at_x(1 if half == 0 else -1)
                )

    far = nz // 2
    turns = ((far, nz - 1 - far), (nz - 1 - far, far))
    ring = {}

    def pass_on(m, b, way, k):
        sign = 1 if way == 0 else -1
        piece = proj.at[m, lax.rem(z - sign * (k - 1) + nz, nz), b]
        ring[m, b, way, k] = send(piece, piece, proj_sem, (m, b, way, k), at_z(sign))

    def ring_step(m, k):
        for way in range(2):
            for b in range(2):
                if k <= turns[b][way]:
                    if k > 1:
                        ring[m, b, way, k - 1].wait_recv()
                    pass_on(m, b, way, k)

    def project(m, window):
        total = dot(feats[m, 0], win[window, 0:quarter, :])
        for i in range(1, nx):
            total += dot(feats[m, i], win[window, i * quarter : (i + 1) * quarter, :])
        return total

    def project_own(m):
        total = project(m, m).astype(BF16)
        proj[m, z, 0] = total[0:block]
        proj[m, z, 1] = total[block:]
        ring_step(m, 1)

    for k in range(3):
        tiles_out(k)
    chain_x(feats_x, feats, feats_sem, 0)
    tiles_out(3)
    chain_x(feats_y, feats, feats_sem, 1)
    tiles_out(4)
    for load in loads:
        load.wait()
    end_x(feats_x)
    project_own(0)
    tiles_out(5)
    end_x(feats_y)
    project_own(1)
    tiles_out(6)
    share_on(1)
    share_on(2)
    ring_step(0, 2)
    ring_step(1, 2)
    share_on(3)
    pre[...] = project(0, 2)
    for m, source in enumerate((cite_tiles, write_tiles)):
        for j in range(nz):
            tiles[m, yc, j // 2, j % 2] = source[slot_tab[yc, j, 4 * m + 2]]
    ring_step(0, 3)
    ring_step(1, 3)
    share_on(4)
    share_on(5)
    ring_step(0, 4)
    ring_step(1, 4)
    share_on(6)
    for copy in meta_in:
        copy.wait_recv()
    small = [
        pltpu.make_async_copy(meta_fv, meta_fs, local_sem.at[6]),
        pltpu.make_async_copy(meta_iv, meta_is, local_sem.at[7]),
    ]
    for copy in small:
        copy.start()
    for copy in small:
        copy.wait()
    for m in range(2):
        for b in range(2):
            for way in range(2):
                ring[m, b, way, turns[b][way]].wait_recv()

    def share_of(target):
        acc[...] = jnp.zeros_like(acc)

        def step(i, carry):
            m = i // nz
            s = i % nz
            source = meta_is[target, s, 4 * m]
            product = dot(
                tiles[m, target, s // 2, s % 2],
                proj[m, s, source],
            )
            acc[0:block, :] += meta_fs[target, s, 4 * m] * product
            acc[block:, :] += meta_fs[target, s, 4 * m + 1] * product
            return carry

        lax.fori_loop(0, 2 * nz, step, 0, unroll=UNROLL)

    part_in = {}

    def share_from(k):
        for m in range(2):
            for half in range(nx if k == 0 else 2):
                (tiles_in if k == 0 else shared_in)[m, k, half].wait_recv()
        share_of(there(opposite[k]))

    cut = quarter // 2
    halves = (slice(0, cut), slice(cut, quarter))

    def pass_part(slot, h, device):
        part_in[slot, h] = send(part_send.at[slot, h], part_recv.at[slot, h], part_sem, (slot, h), device)

    for k in range(ny):
        share_from(k)
        for h in range(2):
            part_send[opposite[k], h] = acc[:, halves[h]].astype(BF16)
            pass_part(opposite[k], h, at_yc(0))
    for k in range(ny, n_off):
        share_from(k)
        slot = opposite[k]
        for h in range(2):
            part_in[slot - ny + 1, h].wait_recv()
            total = acc[:, halves[h]] + part_recv[slot - ny + 1, h].astype(F32)
            part_send[slot, h] = total.astype(BF16)
            if h == 0:
                pass_part(slot, h, at_yc(slot))
    for k in range(ny, n_off):
        pass_part(opposite[k], 1, at_yc(opposite[k]))
    share_of(yc)
    pre[...] += acc[...]

    grads = (grads_left, grads_right)
    grads_in = {}
    for h in range(2):
        preact = pre[:, halves[h]]
        for k in (0,) + tuple(range(ny, n_off)):
            part_in[k, h].wait_recv()
            preact += part_recv[k, h].astype(F32)
        sigma = jax.nn.sigmoid(preact)
        slope = sigma * (1.0 + preact * (1.0 - sigma))
        own = (cot[:, halves[h]].astype(F32) * slope).astype(BF16)
        grads[h][yc, 0] = own[0:block]
        grads[h][yc, 1] = own[block:]
        for k in tuple(range(ny, n_off)) + (0,):
            grads_in[h, k] = send(grads[h].at[yc], grads[h].at[yc], grads_sem, (h, k), at_yc(k))
        grads_x[x, :, halves[h]] = own
        outs[0, :, halves[h]] = (feats[0, x, :, halves[h]].astype(F32) + preact * sigma).astype(BF16)
    grads_x_in = [send(grads_x.at[x], grads_x.at[x], grads_x_sem, (k,), at_x(k)) for k in range(1, nx)]

    def grads_on(h):
        for k in range(ny, n_off):
            grads_in[h, k].wait_recv()
            piece = grads[h].at[back_from(k)]
            grads_in[h, k - ny + 1] = send(piece, piece, grads_sem, (h, k - ny + 1), at_yc(0))

    def grads_end(h):
        for k in range(ny):
            grads_in[h, k].wait_recv()

    def back_of(m, place_z, h):
        back_acc[...] = jnp.zeros_like(back_acc)

        def step(i, carry):
            target = meta_is[i, place_z, 4 * m + 1]
            product = dot_left_flipped(tiles[m, i, place_z // 2, place_z % 2], grads[h][i, target])
            back_acc[0:block, :] += meta_fs[i, place_z, 4 * m + 2] * product
            back_acc[block:, :] += meta_fs[i, place_z, 4 * m + 3] * product
            return carry

        lax.fori_loop(0, nyc, step, 0, unroll=UNROLL)

    back = {}

    def back_step(h, distance):
        for way in range(2):
            if distance > turns[h][way]:
                continue
            sign = 1 if way == 0 else -1
            k = turns[h][way] - distance + 1
            for m in range(2):
                back_of(m, lax.rem(z + sign * distance + nz, nz), h)
                total = back_acc[...]
                if k > 1:
                    back[m, h, way, k - 1].wait_recv()
                    total += back_recv[m, h, way, k - 1].astype(F32)
                back_send[m, h, way, k] = total.astype(BF16)
                back[m, h, way, k] = send(
                    back_send.at[m, h, way, k],
                    back_recv.at[m, h, way, k],
                    back_sem,
                    (m, h, way, k),
                    at_z(sign),
                )

    sums_in = {}

    def back_end(h):
        for m in range(2):
            back_of(m, z, h)
            total = back_acc[...]
            for way in range(2):
                back[m, h, way, turns[h][way]].wait_recv()
                total += back_recv[m, h, way, turns[h][way]].astype(F32)
            sums[m, h, x] = total.astype(BF16)
            sums_in[m, h] = gather_x(sums, sums_sem, m, h)

    grads_on(0)
    grads_end(0)
    back_step(0, far)
    grads_on(1)
    back_step(0, far - 1)
    grads_end(1)
    back_step(1, far)
    for distance in range(far - 2, 0, -1):
        back_step(0, distance)
        back_step(1, distance + 1)

    for copy in grads_x_in:
        copy.wait_recv()
    total = cot[...].astype(F32)
    for i in range(nx):
        total += dot_right_flipped(grads_x[i], rows[2, :, i * quarter : (i + 1) * quarter])
    pre[...] = total
    back_end(0)
    back_step(1, 1)
    for m in range(2):
        chain_x(sums_in[m, 0], sums, sums_sem, m, 0)
    back_end(1)
    for m in range(2):
        chain_x(sums_in[m, 1], sums, sums_sem, m, 1)

    stores = [
        pltpu.make_async_copy(outs.at[i], out, local_sem.at[i])
        for i, out in enumerate((paper_out_hbm, paper_grad_hbm, author_grad_hbm))
    ]
    stores[0].start()

    def onto(m, h, total):
        end_x(sums_in[m, h])
        for i in range(nx):
            first = i * quarter + h * cut
            total += dot_right_flipped(sums[m, h, i], rows[m, :, first : first + cut])
        return total

    pre[...] = onto(0, 0, pre[...])
    acc[...] = onto(1, 0, jnp.zeros_like(acc))
    for m in range(2):
        total = onto(m, 1, pre[...] if m == 0 else acc[...])
        outs[1 + m] = total.astype(BF16)
        stores[1 + m].start()
    for copy in sent:
        copy.wait_send()
    for store in stores:
        store.wait()


def body(
    nx,
    paper_feat,
    author_feat,
    cite_owner,
    cite_source,
    cite_target,
    cite_edges,
    cite_count,
    citation_weight_tiles,
    write_owner,
    write_paper,
    write_author,
    write_edges,
    authorship_weight_tiles,
    w_self,
    w_cite,
    w_write,
    cotangent,
):
    nyc = 4 * CORES
    nz = lax.axis_size("paper") // nyc
    n_rows, quarter = paper_feat.shape
    block = citation_weight_tiles.shape[1]
    width = w_self.shape[0]

    lists = (
        cite_owner, cite_source, cite_target, cite_edges, write_owner, write_author, write_paper, write_edges
    )
    steps = nz // 2 + 1
    hbm = pl.BlockSpec(memory_space=pl.ANY)
    unit = jax.ShapeDtypeStruct((n_rows, quarter), BF16)

    def sems(*shape):
        return pltpu.SemaphoreType.DMA((2,) + shape)

    results = pl.pallas_call(
        functools.partial(kernel, nx, nyc, nz),
        out_shape=(unit, unit, unit),
        in_specs=[pl.BlockSpec(memory_space=pltpu.SMEM)] + [hbm] * 16,
        out_specs=(hbm, hbm, hbm),
        scratch_shapes=[
            pltpu.VMEM((4, 1, cite_edges.shape[0]), jnp.int32),
            pltpu.VMEM((4, 1, write_edges.shape[0]), jnp.int32),
            pltpu.VMEM((n_rows, quarter), BF16),
            pltpu.VMEM((3, n_rows, quarter), BF16),
            pltpu.VMEM(citation_weight_tiles.shape, BF16),
            pltpu.VMEM(authorship_weight_tiles.shape, BF16),
            pltpu.VMEM((3, width, quarter), BF16),
            pltpu.VMEM((3, quarter, width), BF16),
            pltpu.VMEM((2, nx, n_rows, quarter), BF16),
            pltpu.VMEM((2, nz, 2, block, quarter), BF16),
            pltpu.VMEM((nyc, nz, 128), F32),
            pltpu.VMEM((nyc, nz, 128), jnp.int32),
            pltpu.SMEM((nyc, nz, 128), jnp.int32),
            pltpu.VMEM((2, nyc, nz // 2, 2, block, block), BF16),
            pltpu.VMEM((2, nyc, nz // 2, 2, block, block), BF16),
            pltpu.VMEM((nyc, nz, 128), F32),
            pltpu.VMEM((nyc, nz, 128), jnp.int32),
            pltpu.SMEM((nyc, nz, 128), F32),
            pltpu.SMEM((nyc, nz, 128), jnp.int32),
            pltpu.VMEM((n_rows, quarter), F32),
            pltpu.VMEM((nyc, 2, n_rows, quarter // 2), BF16),
            pltpu.VMEM((nyc, 2, n_rows, quarter // 2), BF16),
            pltpu.VMEM((n_rows, quarter), F32),
            pltpu.VMEM((nyc, 2, block, quarter // 2), BF16),
            pltpu.VMEM((nyc, 2, block, quarter // 2), BF16),
            pltpu.VMEM((nx, n_rows, quarter), BF16),
            pltpu.VMEM((2, 2, 2, steps, n_rows, quarter // 2), BF16),
            pltpu.VMEM((2, 2, 2, steps, n_rows, quarter // 2), BF16),
            pltpu.VMEM((n_rows, quarter // 2), F32),
            pltpu.VMEM((2, 2, nx, n_rows, quarter // 2), BF16),
            pltpu.SemaphoreType.DMA((20,)),
            sems(2, nx),
            sems(2, nyc),
            sems(2, nx, nyc),
            sems(2, 2, nyc),
            sems(2, 2, 2, steps),
            sems(nyc, 2),
            sems(2, nyc),
            sems(nx),
            sems(2, 2, 2, steps),
            sems(2, 2, nx),
        ],
        compiler_params=pltpu.CompilerParams(
            collective_id=0, has_side_effects=True, vmem_limit_bytes=56 * 1024 * 1024
        ),
    )(
        cite_count,
        *[a.reshape(1, -1) for a in lists],
        paper_feat,
        author_feat,
        cotangent,
        citation_weight_tiles,
        authorship_weight_tiles,
        w_self,
        w_cite,
        w_write,
    )
    return pl.pallas_call(
        hand_over,
        out_shape=(unit, unit, unit),
        in_specs=[hbm] * 3,
        out_specs=(hbm, hbm, hbm),
        scratch_shapes=[
            pltpu.VMEM((3, n_rows, quarter), BF16),
            pltpu.SemaphoreType.DMA((2, 3)),
        ],
    )(*results)


def hand_over(*refs):
    sources, results, (held, sems) = refs[:3], refs[3:6], refs[6:]
    ins = [pltpu.make_async_copy(sources[i], held.at[i], sems.at[0, i]) for i in range(3)]
    ends = [pltpu.make_async_copy(held.at[i], results[i], sems.at[1, i]) for i in range(3)]
    for copy in ins:
        copy.start()
    for i in range(3):
        ins[i].wait()
        ends[i].start()
    for copy in ends:
        copy.wait()


def solution(mesh):
    in_specs = (
        P("paper", "author"),
        P("paper", "author"),
        P("paper", None),
        P("paper"),
        P("paper"),
        P("paper"),
        P("paper"),
        P("paper", None, None),
        P("paper", None),
        P("paper"),
        P("paper"),
        P("paper"),
        P("paper", None, None),
        P(),
        P(),
        P(),
        P("paper", "author"),
    )
    out_specs = (P("paper", "author"), P("paper", "author"), P("paper", "author"))
    return jax.shard_map(
        functools.partial(body, mesh.shape["author"]),
        mesh=mesh,
        in_specs=in_specs,
        out_specs=out_specs,
        check_vma=False,
    )
```

```python
import functools

import jax
import jax.numpy as jnp
from jax import lax
from jax.experimental import pallas as pl
from jax.experimental.pallas import tpu as pltpu
from jax.sharding import PartitionSpec as P

MESH = pl.DeviceIdType.MESH
F32 = jnp.float32
BF16 = jnp.bfloat16
CORES = 2
UNROLL = 8


def dot(left, right):
    return jnp.dot(left, right, preferred_element_type=F32)


def dot_left_flipped(left, right):
    return lax.dot_general(left, right, (((0,), (0,)), ((), ())), preferred_element_type=F32)


def dot_right_flipped(left, right):
    return lax.dot_general(left, right, (((1,), (1,)), ((), ())), preferred_element_type=F32)


def kernel(
    nx,
    nyc,
    nz,
    cite_count,
    cite_owner_hbm,
    cite_source_hbm,
    cite_target_hbm,
    cite_edges_hbm,
    write_owner_hbm,
    write_author_hbm,
    write_paper_hbm,
    write_edges_hbm,
    paper_hbm,
    author_hbm,
    cot_hbm,
    cite_tiles_hbm,
    write_tiles_hbm,
    w_self,
    w_cite,
    w_write,
    paper_out_hbm,
    paper_grad_hbm,
    author_grad_hbm,
    cite_lists,
    write_lists,
    cot,
    outs,
    cite_tiles,
    write_tiles,
    win,
    rows,
    feats,
    proj,
    meta_f,
    meta_i,
    slot_tab,
    slots,
    tiles,
    meta_fv,
    meta_iv,
    meta_fs,
    meta_is,
    acc,
    part_send,
    part_recv,
    pre,
    grads_left,
    grads_right,
    grads_x,
    back_send,
    back_recv,
    back_acc,
    sums,
    local_sem,
    feats_sem,
    meta_sem,
    tile_sem,
    share_sem,
    proj_sem,
    part_sem,
    grads_sem,
    grads_x_sem,
    back_sem,
    sums_sem,
):
    p = lax.axis_index("paper")
    x = lax.axis_index("author")
    z = p // nyc
    yc = p % nyc
    block = cite_tiles_hbm.shape[1]
    quarter = paper_hbm.shape[1]
    sent = []

    def send(src, dst, sems, index, device):
        copy = pltpu.make_async_remote_copy(
            src_ref=src,
            dst_ref=dst,
            send_sem=sems.at[(0,) + index],
            recv_sem=sems.at[(1,) + index],
            device_id=device,
            device_id_type=MESH,
        )
        copy.start()
        sent.append(copy)
        return copy

    def at_x(k):
        return (p, lax.rem(x + k + nx, nx))

    ny = nyc // CORES
    offsets = [(0, 1), (1, 1), (ny - 1, 1), (2, 1), (1, 0), (ny - 1, 0), (2, 0)]
    opposite = (0, 2, 1, 3, 5, 4, 6)
    n_off = len(offsets)

    def there(k):
        dy, dc = offsets[k]
        return lax.rem(yc // CORES + dy, ny) * CORES + lax.rem(yc + dc, CORES)

    def back_from(k):
        dy, dc = offsets[k]
        return lax.rem(yc // CORES + ny - dy, ny) * CORES + lax.rem(yc + dc, CORES)

    def at_yc(k):
        return (z * nyc + there(k), x)

    def at_z(k):
        return (lax.rem(z + k + nz, nz) * nyc + yc, x)

    def gather_x(buffer, sems, *at):
        piece = buffer.at[at + (x,)]
        return {k: send(piece, piece, sems, at + (k % nx,), at_x(k)) for k in (1, -1)}

    def chain_x(copies, buffer, sems, *at):
        for b, onward in ((0, 1), (1, -1)):
            copies[onward].wait_recv()
            piece = buffer.at[at + (lax.rem(x - onward + nx, nx), pl.ds(b * block, block))]
            copies[2 + b] = send(piece, piece, sems, at + (2 * b,), at_x(onward))

    def end_x(copies):
        for b in range(2):
            copies[2 + b].wait_recv()

    barrier = pltpu.get_barrier_semaphore()
    peers = [at_x(k) for k in range(1, nx)] + [at_yc(k) for k in range(n_off)] + [at_z(1), at_z(-1)]
    for device in peers:
        pl.semaphore_signal(barrier, inc=1, device_id=device, device_id_type=MESH)

    paper, author = feats.at[0, x], feats.at[1, x]
    own_loads = [
        pltpu.make_async_copy(paper_hbm, paper, local_sem.at[9]),
        pltpu.make_async_copy(author_hbm, author, local_sem.at[10]),
        pltpu.make_async_copy(cot_hbm, cot, local_sem.at[11]),
    ]
    list_loads = [
        pltpu.make_async_copy(source, into.at[i], local_sem.at[12 + 4 * m + i])
        for m, into, sources in (
            (0, cite_lists, (cite_owner_hbm, cite_source_hbm, cite_target_hbm, cite_edges_hbm)),
            (1, write_lists, (write_owner_hbm, write_author_hbm, write_paper_hbm, write_edges_hbm)),
        )
        for i, source in enumerate(sources)
    ]
    tile_loads = [
        pltpu.make_async_copy(cite_tiles_hbm, cite_tiles, local_sem.at[6]),
        pltpu.make_async_copy(write_tiles_hbm, write_tiles, local_sem.at[7]),
    ]
    columns = pl.ds(pl.multiple_of(x * quarter, quarter), quarter)
    loads = []
    for i, w in enumerate((w_cite, w_write, w_self)):
        loads.append(pltpu.make_async_copy(w.at[:, columns], win.at[i], local_sem.at[i]))
        loads.append(pltpu.make_async_copy(w.at[columns, :], rows.at[i], local_sem.at[3 + i]))
    for load in list_loads + own_loads + tile_loads + loads:
        load.start()
    for load in list_loads:
        load.wait()

    n_slots = nyc * nz
    lanes = lax.broadcasted_iota(jnp.int32, (n_slots, 128), 1)
    table_f = jnp.zeros((n_slots, 128), F32)
    table_i = jnp.zeros((n_slots, 128), jnp.int32)
    for m, lists in enumerate((cite_lists, write_lists)):
        owner, sources, targets, edges = lists[0], lists[1], lists[2], lists[3]
        n = lists.shape[2]
        number = lax.broadcasted_iota(jnp.int32, (n_slots, n), 1)
        slot = lax.broadcasted_iota(jnp.int32, (n_slots, n), 0)
        named = owner == (slot % nz) * nyc + slot // nz
        scale = 1.0 / edges.astype(F32)
        source = jnp.max(jnp.where(named, sources, 0), axis=1, keepdims=True)
        target = jnp.max(jnp.where(named, targets, 0), axis=1, keepdims=True)
        place = jnp.max(jnp.where(named, number, 0), axis=1, keepdims=True)
        live = named & (number < cite_count[0]) if m == 0 else named
        scale = jnp.sum(jnp.where(live, scale, 0.0), axis=1, keepdims=True)
        for kind, value in enumerate((source, target, place)):
            table_i = jnp.where(lanes == 4 * m + kind, value, table_i)
        for kind, (end, b) in enumerate(((target, 0), (target, 1), (source, 0), (source, 1))):
            table_f = jnp.where(lanes == 4 * m + kind, jnp.where(end == b, scale, 0.0), table_f)
    meta_f[...] = table_f.reshape(nyc, nz, 128)
    meta_i[...] = table_i.reshape(nyc, nz, 128)
    tab = pltpu.make_async_copy(meta_i, slot_tab, local_sem.at[8])
    tab.start()
    meta_fv[yc] = meta_f[yc]
    meta_iv[yc] = meta_i[yc]

    pl.semaphore_wait(barrier, len(peers))

    for load in own_loads:
        load.wait()
    feats_x = gather_x(feats, feats_sem, 0)
    feats_y = gather_x(feats, feats_sem, 1)
    meta_in = []
    for k in range(n_off):
        to = there(k)
        meta_in.append(send(meta_f.at[to], meta_fv.at[yc], meta_sem, (0, k), at_yc(k)))
        meta_in.append(send(meta_i.at[to], meta_iv.at[yc], meta_sem, (1, k), at_yc(k)))

    tab.wait()
    for load in tile_loads:
        load.wait()
    tiles_in = {}
    shared_in = {}

    def tiles_out(k):
        to = there(k)
        for m, source in enumerate((cite_tiles, write_tiles)):
            for j in range(nz):
                slots[m, to, j // 2, j % 2] = source[slot_tab[to, j, 4 * m + 2]]
            for half in range(nx if k == 0 else 2):
                q = lax.rem(x + half, nx)
                tiles_in[m, k, half] = send(
                    slots.at[m, to, q], tiles.at[m, yc, q], tile_sem, (m, half, k), at_yc(k)
                )

    def share_on(k):
        for m in range(2):
            for half in range(2):
                tiles_in[m, k, half].wait_recv()
                place_at = tiles.at[m, back_from(k), lax.rem(x + half, nx)]
                shared_in[m, k, half] = send(
                    place_at, place_at, share_sem, (m, half, k), at_x(1 if half == 0 else -1)
                )

    far = nz // 2
    turns = ((far, nz - 1 - far), (nz - 1 - far, far))
    ring = {}

    def pass_on(m, b, way, k):
        sign = 1 if way == 0 else -1
        piece = proj.at[m, lax.rem(z - sign * (k - 1) + nz, nz), b]
        ring[m, b, way, k] = send(piece, piece, proj_sem, (m, b, way, k), at_z(sign))

    def ring_step(m, k):
        for way in range(2):
            for b in range(2):
                if k <= turns[b][way]:
                    if k > 1:
                        ring[m, b, way, k - 1].wait_recv()
                    pass_on(m, b, way, k)

    def project(m, window):
        total = dot(feats[m, 0], win[window, 0:quarter, :])
        for i in range(1, nx):
            total += dot(feats[m, i], win[window, i * quarter : (i + 1) * quarter, :])
        return total

    def project_own(m):
        total = project(m, m).astype(BF16)
        proj[m, z, 0] = total[0:block]
        proj[m, z, 1] = total[block:]
        ring_step(m, 1)

    for k in range(3):
        tiles_out(k)
    chain_x(feats_x, feats, feats_sem, 0)
    tiles_out(3)
    chain_x(feats_y, feats, feats_sem, 1)
    tiles_out(4)
    for load in loads:
        load.wait()
    end_x(feats_x)
    project_own(0)
    tiles_out(5)
    end_x(feats_y)
    project_own(1)
    tiles_out(6)
    share_on(1)
    share_on(2)
    ring_step(0, 2)
    ring_step(1, 2)
    share_on(3)
    pre[...] = project(0, 2)
    for m, source in enumerate((cite_tiles, write_tiles)):
        for j in range(nz):
            tiles[m, yc, j // 2, j % 2] = source[slot_tab[yc, j, 4 * m + 2]]
    ring_step(0, 3)
    ring_step(1, 3)
    share_on(4)
    share_on(5)
    ring_step(0, 4)
    ring_step(1, 4)
    share_on(6)
    for copy in meta_in:
        copy.wait_recv()
    small = [
        pltpu.make_async_copy(meta_fv, meta_fs, local_sem.at[6]),
        pltpu.make_async_copy(meta_iv, meta_is, local_sem.at[7]),
    ]
    for copy in small:
        copy.start()
    for copy in small:
        copy.wait()
    for m in range(2):
        for b in range(2):
            for way in range(2):
                ring[m, b, way, turns[b][way]].wait_recv()

    def share_of(target):
        acc[...] = jnp.zeros_like(acc)

        def step(i, carry):
            m = i // nz
            s = i % nz
            source = meta_is[target, s, 4 * m]
            product = dot(
                tiles[m, target, s // 2, s % 2],
                proj[m, s, source],
            )
            acc[0:block, :] += meta_fs[target, s, 4 * m] * product
            acc[block:, :] += meta_fs[target, s, 4 * m + 1] * product
            return carry

        lax.fori_loop(0, 2 * nz, step, 0, unroll=UNROLL)

    part_in = {}

    def share_from(k):
        for m in range(2):
            for half in range(nx if k == 0 else 2):
                (tiles_in if k == 0 else shared_in)[m, k, half].wait_recv()
        share_of(there(opposite[k]))

    cut = quarter // 2
    halves = (slice(0, cut), slice(cut, quarter))

    def pass_part(slot, h, device):
        part_in[slot, h] = send(part_send.at[slot, h], part_recv.at[slot, h], part_sem, (slot, h), device)

    for k in range(ny):
        share_from(k)
        for h in range(2):
            part_send[opposite[k], h] = acc[:, halves[h]].astype(BF16)
            pass_part(opposite[k], h, at_yc(0))
    for k in range(ny, n_off):
        share_from(k)
        slot = opposite[k]
        for h in range(2):
            part_in[slot - ny + 1, h].wait_recv()
            total = acc[:, halves[h]] + part_recv[slot - ny + 1, h].astype(F32)
            part_send[slot, h] = total.astype(BF16)
            if h == 0:
                pass_part(slot, h, at_yc(slot))
    for k in range(ny, n_off):
        pass_part(opposite[k], 1, at_yc(opposite[k]))
    share_of(yc)
    pre[...] += acc[...]

    grads = (grads_left, grads_right)
    grads_in = {}
    for h in range(2):
        preact = pre[:, halves[h]]
        for k in (0,) + tuple(range(ny, n_off)):
            part_in[k, h].wait_recv()
            preact += part_recv[k, h].astype(F32)
        sigma = jax.nn.sigmoid(preact)
        slope = sigma * (1.0 + preact * (1.0 - sigma))
        own = (cot[:, halves[h]].astype(F32) * slope).astype(BF16)
        grads[h][yc, 0] = own[0:block]
        grads[h][yc, 1] = own[block:]
        for k in tuple(range(ny, n_off)) + (0,):
            grads_in[h, k] = send(grads[h].at[yc], grads[h].at[yc], grads_sem, (h, k), at_yc(k))
        grads_x[x, :, halves[h]] = own
        outs[0, :, halves[h]] = (feats[0, x, :, halves[h]].astype(F32) + preact * sigma).astype(BF16)
    grads_x_in = [send(grads_x.at[x], grads_x.at[x], grads_x_sem, (k,), at_x(k)) for k in range(1, nx)]

    def grads_on(h):
        for k in range(ny, n_off):
            grads_in[h, k].wait_recv()
            piece = grads[h].at[back_from(k)]
            grads_in[h, k - ny + 1] = send(piece, piece, grads_sem, (h, k - ny + 1), at_yc(0))

    def grads_end(h):
        for k in range(ny):
            grads_in[h, k].wait_recv()

    def back_of(m, place_z, h):
        back_acc[...] = jnp.zeros_like(back_acc)

        def step(i, carry):
            target = meta_is[i, place_z, 4 * m + 1]
            product = dot_left_flipped(tiles[m, i, place_z // 2, place_z % 2], grads[h][i, target])
            back_acc[0:block, :] += meta_fs[i, place_z, 4 * m + 2] * product
            back_acc[block:, :] += meta_fs[i, place_z, 4 * m + 3] * product
            return carry

        lax.fori_loop(0, nyc, step, 0, unroll=UNROLL)

    back = {}

    def back_step(h, k):
        for way in (h, 1 - h):
            if k > turns[h][way]:
                continue
            sign = 1 if way == 0 else -1
            distance = turns[h][way] - k + 1
            for m in range(2):
                back_of(m, lax.rem(z + sign * distance + nz, nz), h)
                total = back_acc[...]
                if k > 1:
                    back[m, h, way, k - 1].wait_recv()
                    total += back_recv[m, h, way, k - 1].astype(F32)
                back_send[m, h, way, k] = total.astype(BF16)
                back[m, h, way, k] = send(
                    back_send.at[m, h, way, k],
                    back_recv.at[m, h, way, k],
                    back_sem,
                    (m, h, way, k),
                    at_z(sign),
                )

    sums_in = {}

    def back_end(h):
        for m in range(2):
            back_of(m, z, h)
            total = back_acc[...]
            for way in range(2):
                back[m, h, way, turns[h][way]].wait_recv()
                total += back_recv[m, h, way, turns[h][way]].astype(F32)
            sums[m, h, x] = total.astype(BF16)
            sums_in[m, h] = gather_x(sums, sums_sem, m, h)

    grads_on(0)
    grads_end(0)
    back_step(0, 1)
    grads_on(1)
    grads_end(1)
    back_step(1, 1)
    for k in range(2, far):
        back_step(0, k)
        back_step(1, k)
    back_step(0, far)

    for copy in grads_x_in:
        copy.wait_recv()
    total = cot[...].astype(F32)
    for i in range(nx):
        total += dot_right_flipped(grads_x[i], rows[2, :, i * quarter : (i + 1) * quarter])
    pre[...] = total
    back_step(1, far)
    back_end(0)
    for m in range(2):
        chain_x(sums_in[m, 0], sums, sums_sem, m, 0)
    back_end(1)
    for m in range(2):
        chain_x(sums_in[m, 1], sums, sums_sem, m, 1)

    stores = [
        pltpu.make_async_copy(outs.at[i], out, local_sem.at[i])
        for i, out in enumerate((paper_out_hbm, paper_grad_hbm, author_grad_hbm))
    ]
    stores[0].start()

    def onto(m, h, total):
        end_x(sums_in[m, h])
        for i in range(nx):
            first = i * quarter + h * cut
            total += dot_right_flipped(sums[m, h, i], rows[m, :, first : first + cut])
        return total

    pre[...] = onto(0, 0, pre[...])
    acc[...] = onto(1, 0, jnp.zeros_like(acc))
    for m in range(2):
        total = onto(m, 1, pre[...] if m == 0 else acc[...])
        outs[1 + m] = total.astype(BF16)
        stores[1 + m].start()
    for copy in sent:
        copy.wait_send()
    for store in stores:
        store.wait()


def body(
    nx,
    paper_feat,
    author_feat,
    cite_owner,
    cite_source,
    cite_target,
    cite_edges,
    cite_count,
    citation_weight_tiles,
    write_owner,
    write_paper,
    write_author,
    write_edges,
    authorship_weight_tiles,
    w_self,
    w_cite,
    w_write,
    cotangent,
):
    nyc = 4 * CORES
    nz = lax.axis_size("paper") // nyc
    n_rows, quarter = paper_feat.shape
    block = citation_weight_tiles.shape[1]
    width = w_self.shape[0]

    lists = (
        cite_owner, cite_source, cite_target, cite_edges, write_owner, write_author, write_paper, write_edges
    )
    steps = nz // 2 + 1
    hbm = pl.BlockSpec(memory_space=pl.ANY)
    unit = jax.ShapeDtypeStruct((n_rows, quarter), BF16)

    def sems(*shape):
        return pltpu.SemaphoreType.DMA((2,) + shape)

    results = pl.pallas_call(
        functools.partial(kernel, nx, nyc, nz),
        out_shape=(unit, unit, unit),
        in_specs=[pl.BlockSpec(memory_space=pltpu.SMEM)] + [hbm] * 16,
        out_specs=(hbm, hbm, hbm),
        scratch_shapes=[
            pltpu.VMEM((4, 1, cite_edges.shape[0]), jnp.int32),
            pltpu.VMEM((4, 1, write_edges.shape[0]), jnp.int32),
            pltpu.VMEM((n_rows, quarter), BF16),
            pltpu.VMEM((3, n_rows, quarter), BF16),
            pltpu.VMEM(citation_weight_tiles.shape, BF16),
            pltpu.VMEM(authorship_weight_tiles.shape, BF16),
            pltpu.VMEM((3, width, quarter), BF16),
            pltpu.VMEM((3, quarter, width), BF16),
            pltpu.VMEM((2, nx, n_rows, quarter), BF16),
            pltpu.VMEM((2, nz, 2, block, quarter), BF16),
            pltpu.VMEM((nyc, nz, 128), F32),
            pltpu.VMEM((nyc, nz, 128), jnp.int32),
            pltpu.SMEM((nyc, nz, 128), jnp.int32),
            pltpu.VMEM((2, nyc, nz // 2, 2, block, block), BF16),
            pltpu.VMEM((2, nyc, nz // 2, 2, block, block), BF16),
            pltpu.VMEM((nyc, nz, 128), F32),
            pltpu.VMEM((nyc, nz, 128), jnp.int32),
            pltpu.SMEM((nyc, nz, 128), F32),
            pltpu.SMEM((nyc, nz, 128), jnp.int32),
            pltpu.VMEM((n_rows, quarter), F32),
            pltpu.VMEM((nyc, 2, n_rows, quarter // 2), BF16),
            pltpu.VMEM((nyc, 2, n_rows, quarter // 2), BF16),
            pltpu.VMEM((n_rows, quarter), F32),
            pltpu.VMEM((nyc, 2, block, quarter // 2), BF16),
            pltpu.VMEM((nyc, 2, block, quarter // 2), BF16),
            pltpu.VMEM((nx, n_rows, quarter), BF16),
            pltpu.VMEM((2, 2, 2, steps, n_rows, quarter // 2), BF16),
            pltpu.VMEM((2, 2, 2, steps, n_rows, quarter // 2), BF16),
            pltpu.VMEM((n_rows, quarter // 2), F32),
            pltpu.VMEM((2, 2, nx, n_rows, quarter // 2), BF16),
            pltpu.SemaphoreType.DMA((20,)),
            sems(2, nx),
            sems(2, nyc),
            sems(2, nx, nyc),
            sems(2, 2, nyc),
            sems(2, 2, 2, steps),
            sems(nyc, 2),
            sems(2, nyc),
            sems(nx),
            sems(2, 2, 2, steps),
            sems(2, 2, nx),
        ],
        compiler_params=pltpu.CompilerParams(
            collective_id=0, has_side_effects=True, vmem_limit_bytes=56 * 1024 * 1024
        ),
    )(
        cite_count,
        *[a.reshape(1, -1) for a in lists],
        paper_feat,
        author_feat,
        cotangent,
        citation_weight_tiles,
        authorship_weight_tiles,
        w_self,
        w_cite,
        w_write,
    )
    return pl.pallas_call(
        hand_over,
        out_shape=(unit, unit, unit),
        in_specs=[hbm] * 3,
        out_specs=(hbm, hbm, hbm),
        scratch_shapes=[
            pltpu.VMEM((3, n_rows, quarter), BF16),
            pltpu.SemaphoreType.DMA((2, 3)),
        ],
    )(*results)


def hand_over(*refs):
    sources, results, (held, sems) = refs[:3], refs[3:6], refs[6:]
    ins = [pltpu.make_async_copy(sources[i], held.at[i], sems.at[0, i]) for i in range(3)]
    ends = [pltpu.make_async_copy(held.at[i], results[i], sems.at[1, i]) for i in range(3)]
    for copy in ins:
        copy.start()
    for i in range(3):
        ins[i].wait()
        ends[i].start()
    for copy in ends:
        copy.wait()


def solution(mesh):
    in_specs = (
        P("paper", "author"),
        P("paper", "author"),
        P("paper", None),
        P("paper"),
        P("paper"),
        P("paper"),
        P("paper"),
        P("paper", None, None),
        P("paper", None),
        P("paper"),
        P("paper"),
        P("paper"),
        P("paper", None, None),
        P(),
        P(),
        P(),
        P("paper", "author"),
    )
    out_specs = (P("paper", "author"), P("paper", "author"), P("paper", "author"))
    return jax.shard_map(
        functools.partial(body, mesh.shape["author"]),
        mesh=mesh,
        in_specs=in_specs,
        out_specs=out_specs,
        check_vma=False,
    )
```

```python
import functools

import jax
import jax.numpy as jnp
from jax import lax
from jax.experimental import pallas as pl
from jax.experimental.pallas import tpu as pltpu
from jax.sharding import PartitionSpec as P

MESH = pl.DeviceIdType.MESH
F32 = jnp.float32
BF16 = jnp.bfloat16
CORES = 2
UNROLL = 8


def dot(left, right):
    return jnp.dot(left, right, preferred_element_type=F32)


def dot_left_flipped(left, right):
    return lax.dot_general(left, right, (((0,), (0,)), ((), ())), preferred_element_type=F32)


def dot_right_flipped(left, right):
    return lax.dot_general(left, right, (((1,), (1,)), ((), ())), preferred_element_type=F32)


def kernel(
    nx,
    nyc,
    nz,
    cite_count,
    cite_owner_hbm,
    cite_source_hbm,
    cite_target_hbm,
    cite_edges_hbm,
    write_owner_hbm,
    write_author_hbm,
    write_paper_hbm,
    write_edges_hbm,
    paper_hbm,
    author_hbm,
    cot_hbm,
    cite_tiles_hbm,
    write_tiles_hbm,
    w_self,
    w_cite,
    w_write,
    paper_out_hbm,
    paper_grad_hbm,
    author_grad_hbm,
    cite_lists,
    write_lists,
    cot,
    outs,
    cite_tiles,
    write_tiles,
    win,
    rows,
    feats,
    proj_cite,
    proj_write,
    shares,
    meta_f,
    meta_i,
    slot_tab,
    slots,
    tiles,
    meta_fv,
    meta_iv,
    meta_fs,
    meta_is,
    acc,
    part_send,
    part_recv,
    pre,
    grads_left,
    grads_right,
    grads_x,
    back_send,
    back_recv,
    back_acc,
    sums,
    local_sem,
    feats_sem,
    meta_sem,
    tile_sem,
    share_sem,
    proj_sem,
    part_sem,
    grads_sem,
    grads_x_sem,
    back_sem,
    sums_sem,
):
    p = lax.axis_index("paper")
    x = lax.axis_index("author")
    z = p // nyc
    yc = p % nyc
    block = cite_tiles_hbm.shape[1]
    quarter = paper_hbm.shape[1]
    sent = []

    def send(src, dst, sems, index, device):
        copy = pltpu.make_async_remote_copy(
            src_ref=src,
            dst_ref=dst,
            send_sem=sems.at[(0,) + index],
            recv_sem=sems.at[(1,) + index],
            device_id=device,
            device_id_type=MESH,
        )
        copy.start()
        sent.append(copy)
        return copy

    def at_x(k):
        return (p, lax.rem(x + k + nx, nx))

    ny = nyc // CORES
    offsets = [(0, 1), (1, 1), (ny - 1, 1), (2, 1), (1, 0), (ny - 1, 0), (2, 0)]
    opposite = (0, 2, 1, 3, 5, 4, 6)
    n_off = len(offsets)

    def there(k):
        dy, dc = offsets[k]
        return lax.rem(yc // CORES + dy, ny) * CORES + lax.rem(yc + dc, CORES)

    def back_from(k):
        dy, dc = offsets[k]
        return lax.rem(yc // CORES + ny - dy, ny) * CORES + lax.rem(yc + dc, CORES)

    def at_yc(k):
        return (z * nyc + there(k), x)

    def at_z(k):
        return (lax.rem(z + k + nz, nz) * nyc + yc, x)

    def gather_x(buffer, sems, *at):
        piece = buffer.at[at + (x,)]
        return {k: send(piece, piece, sems, at + (k % nx,), at_x(k)) for k in (1, -1)}

    def chain_x(copies, buffer, sems, *at):
        for b, onward in ((0, 1), (1, -1)):
            copies[onward].wait_recv()
            piece = buffer.at[at + (lax.rem(x - onward + nx, nx), pl.ds(b * block, block))]
            copies[2 + b] = send(piece, piece, sems, at + (2 * b,), at_x(onward))

    def end_x(copies):
        for b in range(2):
            copies[2 + b].wait_recv()

    barrier = pltpu.get_barrier_semaphore()
    peers = [at_x(k) for k in range(1, nx)] + [at_yc(k) for k in range(n_off)] + [at_z(1), at_z(-1)]
    for device in peers:
        pl.semaphore_signal(barrier, inc=1, device_id=device, device_id_type=MESH)

    paper, author = feats.at[0, x], feats.at[1, x]
    own_loads = [
        pltpu.make_async_copy(paper_hbm, paper, local_sem.at[9]),
        pltpu.make_async_copy(author_hbm, author, local_sem.at[10]),
        pltpu.make_async_copy(cot_hbm, cot, local_sem.at[11]),
    ]
    list_loads = [
        pltpu.make_async_copy(source, into.at[i], local_sem.at[12 + 4 * m + i])
        for m, into, sources in (
            (0, cite_lists, (cite_owner_hbm, cite_source_hbm, cite_target_hbm, cite_edges_hbm)),
            (1, write_lists, (write_owner_hbm, write_author_hbm, write_paper_hbm, write_edges_hbm)),
        )
        for i, source in enumerate(sources)
    ]
    tile_loads = [
        pltpu.make_async_copy(cite_tiles_hbm, cite_tiles, local_sem.at[6]),
        pltpu.make_async_copy(write_tiles_hbm, write_tiles, local_sem.at[7]),
    ]
    columns = pl.ds(pl.multiple_of(x * quarter, quarter), quarter)
    loads = []
    for i, w in enumerate((w_cite, w_write, w_self)):
        loads.append(pltpu.make_async_copy(w.at[:, columns], win.at[i], local_sem.at[i]))
        loads.append(pltpu.make_async_copy(w.at[columns, :], rows.at[i], local_sem.at[3 + i]))
    for load in list_loads + own_loads + tile_loads + loads:
        load.start()
    for load in list_loads:
        load.wait()

    n_slots = nyc * nz
    lanes = lax.broadcasted_iota(jnp.int32, (n_slots, 128), 1)
    table_f = jnp.zeros((n_slots, 128), F32)
    table_i = jnp.zeros((n_slots, 128), jnp.int32)
    for m, lists in enumerate((cite_lists, write_lists)):
        owner, sources, targets, edges = lists[0], lists[1], lists[2], lists[3]
        n = lists.shape[2]
        number = lax.broadcasted_iota(jnp.int32, (n_slots, n), 1)
        slot = lax.broadcasted_iota(jnp.int32, (n_slots, n), 0)
        named = owner == (slot % nz) * nyc + slot // nz
        scale = 1.0 / edges.astype(F32)
        source = jnp.max(jnp.where(named, sources, 0), axis=1, keepdims=True)
        target = jnp.max(jnp.where(named, targets, 0), axis=1, keepdims=True)
        place = jnp.max(jnp.where(named, number, 0), axis=1, keepdims=True)
        live = named & (number < cite_count[0]) if m == 0 else named
        scale = jnp.sum(jnp.where(live, scale, 0.0), axis=1, keepdims=True)
        for kind, value in enumerate((source, target, place)):
            table_i = jnp.where(lanes == 4 * m + kind, value, table_i)
        for kind, (end, b) in enumerate(((target, 0), (target, 1), (source, 0), (source, 1))):
            table_f = jnp.where(lanes == 4 * m + kind, jnp.where(end == b, scale, 0.0), table_f)
    meta_f[...] = table_f.reshape(nyc, nz, 128)
    meta_i[...] = table_i.reshape(nyc, nz, 128)
    tab = pltpu.make_async_copy(meta_i, slot_tab, local_sem.at[8])
    tab.start()
    meta_fv[yc] = meta_f[yc]
    meta_iv[yc] = meta_i[yc]

    pl.semaphore_wait(barrier, len(peers))

    for load in own_loads:
        load.wait()
    feats_x = gather_x(feats, feats_sem, 0)
    feats_y = gather_x(feats, feats_sem, 1)
    meta_in = []
    for k in range(n_off):
        to = there(k)
        meta_in.append(send(meta_f.at[to], meta_fv.at[yc], meta_sem, (0, k), at_yc(k)))
        meta_in.append(send(meta_i.at[to], meta_iv.at[yc], meta_sem, (1, k), at_yc(k)))

    tab.wait()
    for load in tile_loads:
        load.wait()
    tiles_in = {}
    shared_in = {}

    def tiles_out(k):
        to = there(k)
        for m, source in enumerate((cite_tiles, write_tiles)):
            for j in range(nz):
                slots[m, to, j // 2, j % 2] = source[slot_tab[to, j, 4 * m + 2]]
            for half in range(nx if k == 0 else 2):
                q = lax.rem(x + half, nx)
                tiles_in[m, k, half] = send(
                    slots.at[m, to, q], tiles.at[m, yc, q], tile_sem, (m, half, k), at_yc(k)
                )

    def share_on(k):
        for m in range(2):
            for half in range(2):
                tiles_in[m, k, half].wait_recv()
                place_at = tiles.at[m, back_from(k), lax.rem(x + half, nx)]
                shared_in[m, k, half] = send(
                    place_at, place_at, share_sem, (m, half, k), at_x(1 if half == 0 else -1)
                )

    far = nz // 2
    turns = ((far, nz - 1 - far), (nz - 1 - far, far))
    ring = {}
    proj = (proj_cite, proj_write)

    def pass_on(m, b, way, k):
        sign = 1 if way == 0 else -1
        piece = proj[m].at[lax.rem(z - sign * (k - 1) + nz, nz), b]
        ring[m, b, way, k] = send(piece, piece, proj_sem, (m, b, way, k), at_z(sign))

    def ring_step(m, k):
        for way in range(2):
            for b in range(2):
                if k <= turns[b][way]:
                    if k > 1:
                        ring[m, b, way, k - 1].wait_recv()
                    pass_on(m, b, way, k)

    def project(m, window):
        total = dot(feats[m, 0], win[window, 0:quarter, :])
        for i in range(1, nx):
            total += dot(feats[m, i], win[window, i * quarter : (i + 1) * quarter, :])
        return total

    def project_own(m):
        total = project(m, m).astype(BF16)
        proj[m][z, 0] = total[0:block]
        proj[m][z, 1] = total[block:]
        ring_step(m, 1)

    for k in range(3):
        tiles_out(k)
    chain_x(feats_x, feats, feats_sem, 0)
    tiles_out(3)
    chain_x(feats_y, feats, feats_sem, 1)
    tiles_out(4)
    for load in loads:
        load.wait()
    end_x(feats_x)
    project_own(0)
    tiles_out(5)
    end_x(feats_y)
    project_own(1)
    tiles_out(6)
    share_on(1)
    share_on(2)
    ring_step(0, 2)
    ring_step(1, 2)
    share_on(3)
    pre[...] = project(0, 2)
    for m, source in enumerate((cite_tiles, write_tiles)):
        for j in range(nz):
            tiles[m, yc, j // 2, j % 2] = source[slot_tab[yc, j, 4 * m + 2]]
    ring_step(0, 3)
    ring_step(1, 3)
    share_on(4)
    share_on(5)
    ring_step(0, 4)
    ring_step(1, 4)
    share_on(6)
    for copy in meta_in:
        copy.wait_recv()
    small = [
        pltpu.make_async_copy(meta_fv, meta_fs, local_sem.at[6]),
        pltpu.make_async_copy(meta_iv, meta_is, local_sem.at[7]),
    ]
    for copy in small:
        copy.start()
    for copy in small:
        copy.wait()
    def ring_end(m):
        for b in range(2):
            for way in range(2):
                ring[m, b, way, turns[b][way]].wait_recv()

    def add_share(m, target):
        def step(source_z, carry):
            source = meta_is[target, source_z, 4 * m]
            product = dot(tiles[m, target, source_z // 2, source_z % 2], proj[m][source_z, source])
            acc[0:block, :] += meta_fs[target, source_z, 4 * m] * product
            acc[block:, :] += meta_fs[target, source_z, 4 * m + 1] * product
            return carry

        lax.fori_loop(0, nz, step, 0, unroll=UNROLL)

    part_in = {}

    def share_wait(m, k):
        for half in range(nx if k == 0 else 2):
            (tiles_in if k == 0 else shared_in)[m, k, half].wait_recv()

    def cite_share(k):
        acc[...] = jnp.zeros_like(acc)
        share_wait(0, k)
        add_share(0, there(opposite[k]))

    ring_end(0)
    acc[...] = jnp.zeros_like(acc)
    add_share(0, yc)
    pre[...] += acc[...]
    early = n_off - 1
    for k in range(early):
        cite_share(k)
        shares[k] = acc[...]
    ring_end(1)

    def share_from(k):
        if k < early:
            acc[...] = shares[k]
        else:
            cite_share(k)
        share_wait(1, k)
        add_share(1, there(opposite[k]))

    cut = quarter // 2
    halves = (slice(0, cut), slice(cut, quarter))

    def pass_part(slot, h, device):
        part_in[slot, h] = send(part_send.at[slot, h], part_recv.at[slot, h], part_sem, (slot, h), device)

    for k in range(ny):
        share_from(k)
        for h in range(2):
            part_send[opposite[k], h] = acc[:, halves[h]].astype(BF16)
            pass_part(opposite[k], h, at_yc(0))
    for k in range(ny, n_off):
        share_from(k)
        slot = opposite[k]
        for h in range(2):
            part_in[slot - ny + 1, h].wait_recv()
            total = acc[:, halves[h]] + part_recv[slot - ny + 1, h].astype(F32)
            part_send[slot, h] = total.astype(BF16)
            if h == 0:
                pass_part(slot, h, at_yc(slot))
    for k in range(ny, n_off):
        pass_part(opposite[k], 1, at_yc(opposite[k]))
    acc[...] = pre[...]
    add_share(1, yc)
    pre[...] = acc[...]

    grads = (grads_left, grads_right)
    grads_in = {}
    for h in range(2):
        preact = pre[:, halves[h]]
        for k in (0,) + tuple(range(ny, n_off)):
            part_in[k, h].wait_recv()
            preact += part_recv[k, h].astype(F32)
        sigma = jax.nn.sigmoid(preact)
        slope = sigma * (1.0 + preact * (1.0 - sigma))
        own = (cot[:, halves[h]].astype(F32) * slope).astype(BF16)
        grads[h][yc, 0] = own[0:block]
        grads[h][yc, 1] = own[block:]
        for k in tuple(range(ny, n_off)) + (0,):
            grads_in[h, k] = send(grads[h].at[yc], grads[h].at[yc], grads_sem, (h, k), at_yc(k))
        grads_x[x, :, halves[h]] = own
        outs[0, :, halves[h]] = (feats[0, x, :, halves[h]].astype(F32) + preact * sigma).astype(BF16)
    grads_x_in = [send(grads_x.at[x], grads_x.at[x], grads_x_sem, (k,), at_x(k)) for k in range(1, nx)]

    def grads_on(h):
        for k in range(ny, n_off):
            grads_in[h, k].wait_recv()
            piece = grads[h].at[back_from(k)]
            grads_in[h, k - ny + 1] = send(piece, piece, grads_sem, (h, k - ny + 1), at_yc(0))

    def grads_end(h):
        for k in range(ny):
            grads_in[h, k].wait_recv()

    def back_of(m, place_z, h):
        back_acc[...] = jnp.zeros_like(back_acc)

        def step(i, carry):
            target = meta_is[i, place_z, 4 * m + 1]
            product = dot_left_flipped(tiles[m, i, place_z // 2, place_z % 2], grads[h][i, target])
            back_acc[0:block, :] += meta_fs[i, place_z, 4 * m + 2] * product
            back_acc[block:, :] += meta_fs[i, place_z, 4 * m + 3] * product
            return carry

        lax.fori_loop(0, nyc, step, 0, unroll=UNROLL)

    back = {}

    def back_step(h, k):
        for way in (h, 1 - h):
            if k > turns[h][way]:
                continue
            sign = 1 if way == 0 else -1
            distance = turns[h][way] - k + 1
            for m in range(2):
                back_of(m, lax.rem(z + sign * distance + nz, nz), h)
                total = back_acc[...]
                if k > 1:
                    back[m, h, way, k - 1].wait_recv()
                    total += back_recv[m, h, way, k - 1].astype(F32)
                back_send[m, h, way, k] = total.astype(BF16)
                back[m, h, way, k] = send(
                    back_send.at[m, h, way, k],
                    back_recv.at[m, h, way, k],
                    back_sem,
                    (m, h, way, k),
                    at_z(sign),
                )

    sums_in = {}

    def back_end(h):
        for m in range(2):
            back_of(m, z, h)
            total = back_acc[...]
            for way in range(2):
                back[m, h, way, turns[h][way]].wait_recv()
                total += back_recv[m, h, way, turns[h][way]].astype(F32)
            sums[m, h, x] = total.astype(BF16)
            sums_in[m, h] = gather_x(sums, sums_sem, m, h)

    grads_on(0)
    grads_end(0)
    back_step(0, 1)
    grads_on(1)
    grads_end(1)
    back_step(1, 1)
    for k in range(2, far):
        back_step(0, k)
        back_step(1, k)
    back_step(0, far)

    for copy in grads_x_in:
        copy.wait_recv()
    total = cot[...].astype(F32)
    for i in range(nx):
        total += dot_right_flipped(grads_x[i], rows[2, :, i * quarter : (i + 1) * quarter])
    pre[...] = total
    back_step(1, far)
    back_end(0)
    for m in range(2):
        chain_x(sums_in[m, 0], sums, sums_sem, m, 0)
    back_end(1)
    for m in range(2):
        chain_x(sums_in[m, 1], sums, sums_sem, m, 1)

    stores = [
        pltpu.make_async_copy(outs.at[i], out, local_sem.at[i])
        for i, out in enumerate((paper_out_hbm, paper_grad_hbm, author_grad_hbm))
    ]
    stores[0].start()

    def onto(m, h, total):
        end_x(sums_in[m, h])
        for i in range(nx):
            first = i * quarter + h * cut
            total += dot_right_flipped(sums[m, h, i], rows[m, :, first : first + cut])
        return total

    pre[...] = onto(0, 0, pre[...])
    acc[...] = onto(1, 0, jnp.zeros_like(acc))
    for m in range(2):
        total = onto(m, 1, pre[...] if m == 0 else acc[...])
        outs[1 + m] = total.astype(BF16)
        stores[1 + m].start()
    for copy in sent:
        copy.wait_send()
    for store in stores:
        store.wait()


def body(
    nx,
    paper_feat,
    author_feat,
    cite_owner,
    cite_source,
    cite_target,
    cite_edges,
    cite_count,
    citation_weight_tiles,
    write_owner,
    write_paper,
    write_author,
    write_edges,
    authorship_weight_tiles,
    w_self,
    w_cite,
    w_write,
    cotangent,
):
    nyc = 4 * CORES
    nz = lax.axis_size("paper") // nyc
    n_rows, quarter = paper_feat.shape
    block = citation_weight_tiles.shape[1]
    width = w_self.shape[0]

    lists = (
        cite_owner, cite_source, cite_target, cite_edges, write_owner, write_author, write_paper, write_edges
    )
    steps = nz // 2 + 1
    hbm = pl.BlockSpec(memory_space=pl.ANY)
    unit = jax.ShapeDtypeStruct((n_rows, quarter), BF16)

    def sems(*shape):
        return pltpu.SemaphoreType.DMA((2,) + shape)

    results = pl.pallas_call(
        functools.partial(kernel, nx, nyc, nz),
        out_shape=(unit, unit, unit),
        in_specs=[pl.BlockSpec(memory_space=pltpu.SMEM)] + [hbm] * 16,
        out_specs=(hbm, hbm, hbm),
        scratch_shapes=[
            pltpu.VMEM((4, 1, cite_edges.shape[0]), jnp.int32),
            pltpu.VMEM((4, 1, write_edges.shape[0]), jnp.int32),
            pltpu.VMEM((n_rows, quarter), BF16),
            pltpu.VMEM((3, n_rows, quarter), BF16),
            pltpu.VMEM(citation_weight_tiles.shape, BF16),
            pltpu.VMEM(authorship_weight_tiles.shape, BF16),
            pltpu.VMEM((3, width, quarter), BF16),
            pltpu.VMEM((3, quarter, width), BF16),
            pltpu.VMEM((2, nx, n_rows, quarter), BF16),
            pltpu.VMEM((nz, 2, block, quarter), BF16),
            pltpu.VMEM((nz, 2, block, quarter), BF16),
            pltpu.VMEM((nyc - 2, n_rows, quarter), F32),
            pltpu.VMEM((nyc, nz, 128), F32),
            pltpu.VMEM((nyc, nz, 128), jnp.int32),
            pltpu.SMEM((nyc, nz, 128), jnp.int32),
            pltpu.VMEM((2, nyc, nz // 2, 2, block, block), BF16),
            pltpu.VMEM((2, nyc, nz // 2, 2, block, block), BF16),
            pltpu.VMEM((nyc, nz, 128), F32),
            pltpu.VMEM((nyc, nz, 128), jnp.int32),
            pltpu.SMEM((nyc, nz, 128), F32),
            pltpu.SMEM((nyc, nz, 128), jnp.int32),
            pltpu.VMEM((n_rows, quarter), F32),
            pltpu.VMEM((nyc, 2, n_rows, quarter // 2), BF16),
            pltpu.VMEM((nyc, 2, n_rows, quarter // 2), BF16),
            pltpu.VMEM((n_rows, quarter), F32),
            pltpu.VMEM((nyc, 2, block, quarter // 2), BF16),
            pltpu.VMEM((nyc, 2, block, quarter // 2), BF16),
            pltpu.VMEM((nx, n_rows, quarter), BF16),
            pltpu.VMEM((2, 2, 2, steps, n_rows, quarter // 2), BF16),
            pltpu.VMEM((2, 2, 2, steps, n_rows, quarter // 2), BF16),
            pltpu.VMEM((n_rows, quarter // 2), F32),
            pltpu.VMEM((2, 2, nx, n_rows, quarter // 2), BF16),
            pltpu.SemaphoreType.DMA((20,)),
            sems(2, nx),
            sems(2, nyc),
            sems(2, nx, nyc),
            sems(2, 2, nyc),
            sems(2, 2, 2, steps),
            sems(nyc, 2),
            sems(2, nyc),
            sems(nx),
            sems(2, 2, 2, steps),
            sems(2, 2, nx),
        ],
        compiler_params=pltpu.CompilerParams(
            collective_id=0, has_side_effects=True, vmem_limit_bytes=56 * 1024 * 1024
        ),
    )(
        cite_count,
        *[a.reshape(1, -1) for a in lists],
        paper_feat,
        author_feat,
        cotangent,
        citation_weight_tiles,
        authorship_weight_tiles,
        w_self,
        w_cite,
        w_write,
    )
    return pl.pallas_call(
        hand_over,
        out_shape=(unit, unit, unit),
        in_specs=[hbm] * 3,
        out_specs=(hbm, hbm, hbm),
        scratch_shapes=[
            pltpu.VMEM((3, n_rows, quarter), BF16),
            pltpu.SemaphoreType.DMA((2, 3)),
        ],
    )(*results)


def hand_over(*refs):
    sources, results, (held, sems) = refs[:3], refs[3:6], refs[6:]
    ins = [pltpu.make_async_copy(sources[i], held.at[i], sems.at[0, i]) for i in range(3)]
    ends = [pltpu.make_async_copy(held.at[i], results[i], sems.at[1, i]) for i in range(3)]
    for copy in ins:
        copy.start()
    for i in range(3):
        ins[i].wait()
        ends[i].start()
    for copy in ends:
        copy.wait()


def solution(mesh):
    in_specs = (
        P("paper", "author"),
        P("paper", "author"),
        P("paper", None),
        P("paper"),
        P("paper"),
        P("paper"),
        P("paper"),
        P("paper", None, None),
        P("paper", None),
        P("paper"),
        P("paper"),
        P("paper"),
        P("paper", None, None),
        P(),
        P(),
        P(),
        P("paper", "author"),
    )
    out_specs = (P("paper", "author"), P("paper", "author"), P("paper", "author"))
    return jax.shard_map(
        functools.partial(body, mesh.shape["author"]),
        mesh=mesh,
        in_specs=in_specs,
        out_specs=out_specs,
        check_vma=False,
    )
```

```python
import functools

import jax
import jax.numpy as jnp
from jax import lax
from jax.experimental import pallas as pl
from jax.experimental.pallas import tpu as pltpu
from jax.sharding import PartitionSpec as P

MESH = pl.DeviceIdType.MESH
F32 = jnp.float32
BF16 = jnp.bfloat16
CORES = 2
UNROLL = 8


def dot(left, right):
    return jnp.dot(left, right, preferred_element_type=F32)


def dot_left_flipped(left, right):
    return lax.dot_general(left, right, (((0,), (0,)), ((), ())), preferred_element_type=F32)


def dot_right_flipped(left, right):
    return lax.dot_general(left, right, (((1,), (1,)), ((), ())), preferred_element_type=F32)


def kernel(
    nx,
    nyc,
    nz,
    cite_count,
    cite_owner_hbm,
    cite_source_hbm,
    cite_target_hbm,
    cite_edges_hbm,
    write_owner_hbm,
    write_author_hbm,
    write_paper_hbm,
    write_edges_hbm,
    paper_hbm,
    author_hbm,
    cot_hbm,
    cite_tiles_hbm,
    write_tiles_hbm,
    w_self,
    w_cite,
    w_write,
    paper_out_hbm,
    paper_grad_hbm,
    author_grad_hbm,
    cite_lists,
    write_lists,
    cot,
    outs,
    cite_tiles,
    write_tiles,
    win,
    rows,
    feats,
    proj_cite,
    proj_write,
    shares,
    meta_f,
    meta_i,
    slot_tab,
    slots,
    tiles,
    meta_fv,
    meta_iv,
    meta_fs,
    meta_is,
    acc,
    part_send,
    part_recv,
    pre,
    grads_left,
    grads_right,
    grads_x,
    back_send,
    back_recv,
    back_acc,
    sums,
    local_sem,
    feats_sem,
    meta_sem,
    tile_sem,
    share_sem,
    proj_sem,
    part_sem,
    grads_sem,
    grads_x_sem,
    back_sem,
    sums_sem,
):
    p = lax.axis_index("paper")
    x = lax.axis_index("author")
    z = p // nyc
    yc = p % nyc
    block = cite_tiles_hbm.shape[1]
    quarter = paper_hbm.shape[1]
    sent = []

    def send(src, dst, sems, index, device):
        copy = pltpu.make_async_remote_copy(
            src_ref=src,
            dst_ref=dst,
            send_sem=sems.at[(0,) + index],
            recv_sem=sems.at[(1,) + index],
            device_id=device,
            device_id_type=MESH,
        )
        copy.start()
        sent.append(copy)
        return copy

    def at_x(k):
        return (p, lax.rem(x + k + nx, nx))

    ny = nyc // CORES
    offsets = [(0, 1), (1, 1), (ny - 1, 1), (2, 1), (1, 0), (ny - 1, 0), (2, 0)]
    opposite = (0, 2, 1, 3, 5, 4, 6)
    n_off = len(offsets)

    def there(k):
        dy, dc = offsets[k]
        return lax.rem(yc // CORES + dy, ny) * CORES + lax.rem(yc + dc, CORES)

    def back_from(k):
        dy, dc = offsets[k]
        return lax.rem(yc // CORES + ny - dy, ny) * CORES + lax.rem(yc + dc, CORES)

    def at_yc(k):
        return (z * nyc + there(k), x)

    def at_z(k):
        return (lax.rem(z + k + nz, nz) * nyc + yc, x)

    def gather_x(buffer, sems, *at):
        piece = buffer.at[at + (x,)]
        return {k: send(piece, piece, sems, at + (k % nx,), at_x(k)) for k in (1, -1)}

    def chain_x(copies, buffer, sems, *at):
        for b, onward in ((0, 1), (1, -1)):
            copies[onward].wait_recv()
            piece = buffer.at[at + (lax.rem(x - onward + nx, nx), pl.ds(b * block, block))]
            copies[2 + b] = send(piece, piece, sems, at + (2 * b,), at_x(onward))

    def end_x(copies):
        for b in range(2):
            copies[2 + b].wait_recv()

    barrier = pltpu.get_barrier_semaphore()
    peers = [at_x(k) for k in range(1, nx)] + [at_yc(k) for k in range(n_off)] + [at_z(1), at_z(-1)]
    for device in peers:
        pl.semaphore_signal(barrier, inc=1, device_id=device, device_id_type=MESH)

    paper, author = feats.at[0, x], feats.at[1, x]
    own_loads = [
        pltpu.make_async_copy(paper_hbm, paper, local_sem.at[9]),
        pltpu.make_async_copy(author_hbm, author, local_sem.at[10]),
        pltpu.make_async_copy(cot_hbm, cot, local_sem.at[11]),
    ]
    list_loads = [
        pltpu.make_async_copy(source, into.at[i], local_sem.at[12 + 4 * m + i])
        for m, into, sources in (
            (0, cite_lists, (cite_owner_hbm, cite_source_hbm, cite_target_hbm, cite_edges_hbm)),
            (1, write_lists, (write_owner_hbm, write_author_hbm, write_paper_hbm, write_edges_hbm)),
        )
        for i, source in enumerate(sources)
    ]
    tile_loads = [
        pltpu.make_async_copy(cite_tiles_hbm, cite_tiles, local_sem.at[6]),
        pltpu.make_async_copy(write_tiles_hbm, write_tiles, local_sem.at[7]),
    ]
    columns = pl.ds(pl.multiple_of(x * quarter, quarter), quarter)
    loads = []
    for i, w in enumerate((w_cite, w_write, w_self)):
        loads.append(pltpu.make_async_copy(w.at[:, columns], win.at[i], local_sem.at[i]))
        loads.append(pltpu.make_async_copy(w.at[columns, :], rows.at[i], local_sem.at[3 + i]))
    for load in list_loads + own_loads + tile_loads + loads:
        load.start()
    for load in list_loads:
        load.wait()

    n_slots = nyc * nz
    lanes = lax.broadcasted_iota(jnp.int32, (n_slots, 128), 1)
    table_f = jnp.zeros((n_slots, 128), F32)
    table_i = jnp.zeros((n_slots, 128), jnp.int32)
    for m, lists in enumerate((cite_lists, write_lists)):
        owner, sources, targets, edges = lists[0], lists[1], lists[2], lists[3]
        n = lists.shape[2]
        number = lax.broadcasted_iota(jnp.int32, (n_slots, n), 1)
        slot = lax.broadcasted_iota(jnp.int32, (n_slots, n), 0)
        named = owner == (slot % nz) * nyc + slot // nz
        scale = 1.0 / edges.astype(F32)
        source = jnp.max(jnp.where(named, sources, 0), axis=1, keepdims=True)
        target = jnp.max(jnp.where(named, targets, 0), axis=1, keepdims=True)
        place = jnp.max(jnp.where(named, number, 0), axis=1, keepdims=True)
        live = named & (number < cite_count[0]) if m == 0 else named
        scale = jnp.sum(jnp.where(live, scale, 0.0), axis=1, keepdims=True)
        for kind, value in enumerate((source, target, place)):
            table_i = jnp.where(lanes == 4 * m + kind, value, table_i)
        for kind, (end, b) in enumerate(((target, 0), (target, 1), (source, 0), (source, 1))):
            table_f = jnp.where(lanes == 4 * m + kind, jnp.where(end == b, scale, 0.0), table_f)
    meta_f[...] = table_f.reshape(nyc, nz, 128)
    meta_i[...] = table_i.reshape(nyc, nz, 128)
    tab = pltpu.make_async_copy(meta_i, slot_tab, local_sem.at[8])
    tab.start()
    meta_fv[yc] = meta_f[yc]
    meta_iv[yc] = meta_i[yc]

    pl.semaphore_wait(barrier, len(peers))

    for load in own_loads:
        load.wait()
    feats_x = gather_x(feats, feats_sem, 0)
    feats_y = gather_x(feats, feats_sem, 1)
    meta_in = []
    for k in range(n_off):
        to = there(k)
        meta_in.append(send(meta_f.at[to], meta_fv.at[yc], meta_sem, (0, k), at_yc(k)))
        meta_in.append(send(meta_i.at[to], meta_iv.at[yc], meta_sem, (1, k), at_yc(k)))

    tab.wait()
    for load in tile_loads:
        load.wait()
    tiles_in = {}
    shared_in = {}

    def tiles_out(k):
        to = there(k)
        for m, source in enumerate((cite_tiles, write_tiles)):
            for j in range(nz):
                slots[m, to, j // 2, j % 2] = source[slot_tab[to, j, 4 * m + 2]]
            for half in range(nx if k == 0 else 2):
                q = lax.rem(x + half, nx)
                tiles_in[m, k, half] = send(
                    slots.at[m, to, q], tiles.at[m, yc, q], tile_sem, (m, half, k), at_yc(k)
                )

    def share_on(k):
        for m in range(2):
            for half in range(2):
                tiles_in[m, k, half].wait_recv()
                place_at = tiles.at[m, back_from(k), lax.rem(x + half, nx)]
                shared_in[m, k, half] = send(
                    place_at, place_at, share_sem, (m, half, k), at_x(1 if half == 0 else -1)
                )

    far = nz // 2
    turns = ((far, nz - 1 - far), (nz - 1 - far, far))
    ring = {}
    proj = (proj_cite, proj_write)

    def pass_on(m, b, way, k):
        sign = 1 if way == 0 else -1
        piece = proj[m].at[lax.rem(z - sign * (k - 1) + nz, nz), b]
        ring[m, b, way, k] = send(piece, piece, proj_sem, (m, b, way, k), at_z(sign))

    def ring_step(m, k):
        for way in range(2):
            for b in range(2):
                if k <= turns[b][way]:
                    if k > 1:
                        ring[m, b, way, k - 1].wait_recv()
                    pass_on(m, b, way, k)

    def project(m, window):
        total = dot(feats[m, 0], win[window, 0:quarter, :])
        for i in range(1, nx):
            total += dot(feats[m, i], win[window, i * quarter : (i + 1) * quarter, :])
        return total

    def project_own(m):
        total = project(m, m).astype(BF16)
        proj[m][z, 0] = total[0:block]
        proj[m][z, 1] = total[block:]
        ring_step(m, 1)

    for k in range(3):
        tiles_out(k)
    chain_x(feats_x, feats, feats_sem, 0)
    tiles_out(3)
    chain_x(feats_y, feats, feats_sem, 1)
    tiles_out(4)
    for load in loads:
        load.wait()
    end_x(feats_x)
    project_own(0)
    tiles_out(5)
    end_x(feats_y)
    project_own(1)
    tiles_out(6)
    pre[...] = project(0, 2)
    ring_step(0, 2)
    share_on(1)
    ring_step(1, 2)
    share_on(2)
    ring_step(0, 3)
    share_on(3)
    ring_step(1, 3)
    share_on(4)
    ring_step(0, 4)
    share_on(5)
    ring_step(1, 4)
    share_on(6)
    for m, source in enumerate((cite_tiles, write_tiles)):
        for j in range(nz):
            tiles[m, yc, j // 2, j % 2] = source[slot_tab[yc, j, 4 * m + 2]]
    for copy in meta_in:
        copy.wait_recv()
    small = [
        pltpu.make_async_copy(meta_fv, meta_fs, local_sem.at[6]),
        pltpu.make_async_copy(meta_iv, meta_is, local_sem.at[7]),
    ]
    for copy in small:
        copy.start()
    for copy in small:
        copy.wait()
    def ring_end(m):
        for b in range(2):
            for way in range(2):
                ring[m, b, way, turns[b][way]].wait_recv()

    def add_share(m, target):
        def step(source_z, carry):
            source = meta_is[target, source_z, 4 * m]
            product = dot(tiles[m, target, source_z // 2, source_z % 2], proj[m][source_z, source])
            acc[0:block, :] += meta_fs[target, source_z, 4 * m] * product
            acc[block:, :] += meta_fs[target, source_z, 4 * m + 1] * product
            return carry

        lax.fori_loop(0, nz, step, 0, unroll=UNROLL)

    part_in = {}

    def share_wait(m, k):
        for half in range(nx if k == 0 else 2):
            (tiles_in if k == 0 else shared_in)[m, k, half].wait_recv()

    def cite_share(k):
        acc[...] = jnp.zeros_like(acc)
        share_wait(0, k)
        add_share(0, there(opposite[k]))

    ring_end(0)
    acc[...] = jnp.zeros_like(acc)
    add_share(0, yc)
    pre[...] += acc[...]
    early = n_off - 1
    for k in range(early):
        cite_share(k)
        shares[k] = acc[...]
    ring_end(1)

    def share_from(k):
        if k < early:
            acc[...] = shares[k]
        else:
            cite_share(k)
        share_wait(1, k)
        add_share(1, there(opposite[k]))

    cut = quarter // 2
    halves = (slice(0, cut), slice(cut, quarter))

    def pass_part(slot, h, device):
        part_in[slot, h] = send(part_send.at[slot, h], part_recv.at[slot, h], part_sem, (slot, h), device)

    for k in range(ny):
        share_from(k)
        for h in range(2):
            part_send[opposite[k], h] = acc[:, halves[h]].astype(BF16)
            pass_part(opposite[k], h, at_yc(0))
    for k in range(ny, n_off):
        share_from(k)
        slot = opposite[k]
        for h in range(2):
            part_in[slot - ny + 1, h].wait_recv()
            total = acc[:, halves[h]] + part_recv[slot - ny + 1, h].astype(F32)
            part_send[slot, h] = total.astype(BF16)
            if h == 0:
                pass_part(slot, h, at_yc(slot))
    for k in range(ny, n_off):
        pass_part(opposite[k], 1, at_yc(opposite[k]))
    acc[...] = pre[...]
    add_share(1, yc)
    pre[...] = acc[...]

    grads = (grads_left, grads_right)
    grads_in = {}
    for h in range(2):
        preact = pre[:, halves[h]]
        for k in (0,) + tuple(range(ny, n_off)):
            part_in[k, h].wait_recv()
            preact += part_recv[k, h].astype(F32)
        sigma = jax.nn.sigmoid(preact)
        slope = sigma * (1.0 + preact * (1.0 - sigma))
        own = (cot[:, halves[h]].astype(F32) * slope).astype(BF16)
        grads[h][yc, 0] = own[0:block]
        grads[h][yc, 1] = own[block:]
        for k in tuple(range(ny, n_off)) + (0,):
            grads_in[h, k] = send(grads[h].at[yc], grads[h].at[yc], grads_sem, (h, k), at_yc(k))
        grads_x[x, :, halves[h]] = own
        outs[0, :, halves[h]] = (feats[0, x, :, halves[h]].astype(F32) + preact * sigma).astype(BF16)
    grads_x_in = [send(grads_x.at[x], grads_x.at[x], grads_x_sem, (k,), at_x(k)) for k in range(1, nx)]

    def grads_on(h):
        for k in range(ny, n_off):
            grads_in[h, k].wait_recv()
            piece = grads[h].at[back_from(k)]
            grads_in[h, k - ny + 1] = send(piece, piece, grads_sem, (h, k - ny + 1), at_yc(0))

    def grads_end(h):
        for k in range(ny):
            grads_in[h, k].wait_recv()

    def back_of(m, place_z, h):
        back_acc[...] = jnp.zeros_like(back_acc)

        def step(i, carry):
            target = meta_is[i, place_z, 4 * m + 1]
            product = dot_left_flipped(tiles[m, i, place_z // 2, place_z % 2], grads[h][i, target])
            back_acc[0:block, :] += meta_fs[i, place_z, 4 * m + 2] * product
            back_acc[block:, :] += meta_fs[i, place_z, 4 * m + 3] * product
            return carry

        lax.fori_loop(0, nyc, step, 0, unroll=UNROLL)

    back = {}

    def back_step(h, k):
        for way in (h, 1 - h):
            if k > turns[h][way]:
                continue
            sign = 1 if way == 0 else -1
            distance = turns[h][way] - k + 1
            for m in range(2):
                back_of(m, lax.rem(z + sign * distance + nz, nz), h)
                total = back_acc[...]
                if k > 1:
                    back[m, h, way, k - 1].wait_recv()
                    total += back_recv[m, h, way, k - 1].astype(F32)
                back_send[m, h, way, k] = total.astype(BF16)
                back[m, h, way, k] = send(
                    back_send.at[m, h, way, k],
                    back_recv.at[m, h, way, k],
                    back_sem,
                    (m, h, way, k),
                    at_z(sign),
                )

    sums_in = {}

    def back_end(h):
        for m in range(2):
            back_of(m, z, h)
            total = back_acc[...]
            for way in range(2):
                back[m, h, way, turns[h][way]].wait_recv()
                total += back_recv[m, h, way, turns[h][way]].astype(F32)
            sums[m, h, x] = total.astype(BF16)
            sums_in[m, h] = gather_x(sums, sums_sem, m, h)

    grads_on(0)
    grads_end(0)
    back_step(0, 1)
    grads_on(1)
    grads_end(1)
    back_step(1, 1)
    for k in range(2, far):
        back_step(0, k)
        back_step(1, k)
    back_step(0, far)

    for copy in grads_x_in:
        copy.wait_recv()
    total = cot[...].astype(F32)
    for i in range(nx):
        total += dot_right_flipped(grads_x[i], rows[2, :, i * quarter : (i + 1) * quarter])
    pre[...] = total
    back_step(1, far)
    back_end(0)
    for m in range(2):
        chain_x(sums_in[m, 0], sums, sums_sem, m, 0)
    back_end(1)
    for m in range(2):
        chain_x(sums_in[m, 1], sums, sums_sem, m, 1)

    stores = [
        pltpu.make_async_copy(outs.at[i], out, local_sem.at[i])
        for i, out in enumerate((paper_out_hbm, paper_grad_hbm, author_grad_hbm))
    ]
    stores[0].start()

    def onto(m, h, total):
        end_x(sums_in[m, h])
        for i in range(nx):
            first = i * quarter + h * cut
            total += dot_right_flipped(sums[m, h, i], rows[m, :, first : first + cut])
        return total

    pre[...] = onto(0, 0, pre[...])
    acc[...] = onto(1, 0, jnp.zeros_like(acc))
    for m in range(2):
        total = onto(m, 1, pre[...] if m == 0 else acc[...])
        outs[1 + m] = total.astype(BF16)
        stores[1 + m].start()
    for copy in sent:
        copy.wait_send()
    for store in stores:
        store.wait()


def body(
    nx,
    paper_feat,
    author_feat,
    cite_owner,
    cite_source,
    cite_target,
    cite_edges,
    cite_count,
    citation_weight_tiles,
    write_owner,
    write_paper,
    write_author,
    write_edges,
    authorship_weight_tiles,
    w_self,
    w_cite,
    w_write,
    cotangent,
):
    nyc = 4 * CORES
    nz = lax.axis_size("paper") // nyc
    n_rows, quarter = paper_feat.shape
    block = citation_weight_tiles.shape[1]
    width = w_self.shape[0]

    lists = (
        cite_owner, cite_source, cite_target, cite_edges, write_owner, write_author, write_paper, write_edges
    )
    steps = nz // 2 + 1
    hbm = pl.BlockSpec(memory_space=pl.ANY)
    unit = jax.ShapeDtypeStruct((n_rows, quarter), BF16)

    def sems(*shape):
        return pltpu.SemaphoreType.DMA((2,) + shape)

    results = pl.pallas_call(
        functools.partial(kernel, nx, nyc, nz),
        out_shape=(unit, unit, unit),
        in_specs=[pl.BlockSpec(memory_space=pltpu.SMEM)] + [hbm] * 16,
        out_specs=(hbm, hbm, hbm),
        scratch_shapes=[
            pltpu.VMEM((4, 1, cite_edges.shape[0]), jnp.int32),
            pltpu.VMEM((4, 1, write_edges.shape[0]), jnp.int32),
            pltpu.VMEM((n_rows, quarter), BF16),
            pltpu.VMEM((3, n_rows, quarter), BF16),
            pltpu.VMEM(citation_weight_tiles.shape, BF16),
            pltpu.VMEM(authorship_weight_tiles.shape, BF16),
            pltpu.VMEM((3, width, quarter), BF16),
            pltpu.VMEM((3, quarter, width), BF16),
            pltpu.VMEM((2, nx, n_rows, quarter), BF16),
            pltpu.VMEM((nz, 2, block, quarter), BF16),
            pltpu.VMEM((nz, 2, block, quarter), BF16),
            pltpu.VMEM((nyc - 2, n_rows, quarter), F32),
            pltpu.VMEM((nyc, nz, 128), F32),
            pltpu.VMEM((nyc, nz, 128), jnp.int32),
            pltpu.SMEM((nyc, nz, 128), jnp.int32),
            pltpu.VMEM((2, nyc, nz // 2, 2, block, block), BF16),
            pltpu.VMEM((2, nyc, nz // 2, 2, block, block), BF16),
            pltpu.VMEM((nyc, nz, 128), F32),
            pltpu.VMEM((nyc, nz, 128), jnp.int32),
            pltpu.SMEM((nyc, nz, 128), F32),
            pltpu.SMEM((nyc, nz, 128), jnp.int32),
            pltpu.VMEM((n_rows, quarter), F32),
            pltpu.VMEM((nyc, 2, n_rows, quarter // 2), BF16),
            pltpu.VMEM((nyc, 2, n_rows, quarter // 2), BF16),
            pltpu.VMEM((n_rows, quarter), F32),
            pltpu.VMEM((nyc, 2, block, quarter // 2), BF16),
            pltpu.VMEM((nyc, 2, block, quarter // 2), BF16),
            pltpu.VMEM((nx, n_rows, quarter), BF16),
            pltpu.VMEM((2, 2, 2, steps, n_rows, quarter // 2), BF16),
            pltpu.VMEM((2, 2, 2, steps, n_rows, quarter // 2), BF16),
            pltpu.VMEM((n_rows, quarter // 2), F32),
            pltpu.VMEM((2, 2, nx, n_rows, quarter // 2), BF16),
            pltpu.SemaphoreType.DMA((20,)),
            sems(2, nx),
            sems(2, nyc),
            sems(2, nx, nyc),
            sems(2, 2, nyc),
            sems(2, 2, 2, steps),
            sems(nyc, 2),
            sems(2, nyc),
            sems(nx),
            sems(2, 2, 2, steps),
            sems(2, 2, nx),
        ],
        compiler_params=pltpu.CompilerParams(
            collective_id=0, has_side_effects=True, vmem_limit_bytes=56 * 1024 * 1024
        ),
    )(
        cite_count,
        *[a.reshape(1, -1) for a in lists],
        paper_feat,
        author_feat,
        cotangent,
        citation_weight_tiles,
        authorship_weight_tiles,
        w_self,
        w_cite,
        w_write,
    )
    return pl.pallas_call(
        hand_over,
        out_shape=(unit, unit, unit),
        in_specs=[hbm] * 3,
        out_specs=(hbm, hbm, hbm),
        scratch_shapes=[
            pltpu.VMEM((3, n_rows, quarter), BF16),
            pltpu.SemaphoreType.DMA((2, 3)),
        ],
    )(*results)


def hand_over(*refs):
    sources, results, (held, sems) = refs[:3], refs[3:6], refs[6:]
    ins = [pltpu.make_async_copy(sources[i], held.at[i], sems.at[0, i]) for i in range(3)]
    ends = [pltpu.make_async_copy(held.at[i], results[i], sems.at[1, i]) for i in range(3)]
    for copy in ins:
        copy.start()
    for i in range(3):
        ins[i].wait()
        ends[i].start()
    for copy in ends:
        copy.wait()


def solution(mesh):
    in_specs = (
        P("paper", "author"),
        P("paper", "author"),
        P("paper", None),
        P("paper"),
        P("paper"),
        P("paper"),
        P("paper"),
        P("paper", None, None),
        P("paper", None),
        P("paper"),
        P("paper"),
        P("paper"),
        P("paper", None, None),
        P(),
        P(),
        P(),
        P("paper", "author"),
    )
    out_specs = (P("paper", "author"), P("paper", "author"), P("paper", "author"))
    return jax.shard_map(
        functools.partial(body, mesh.shape["author"]),
        mesh=mesh,
        in_specs=in_specs,
        out_specs=out_specs,
        check_vma=False,
    )
```
